32 devices in a mesh: shard: 4 (over z), seq: 8 (over y, x, core).
Axes of the slice: x: 2, y: 2, z: 4, core: 2. Of those that a mesh axis runs over, the one named last changes fastest.
Arguments:
- inputs: bfloat16 [4, 1536, 2048], P('shard', 'seq'), may hold values from -6 to 6
- positions: int32 [4, 1536], P('shard', 'seq'), may hold values from 0 to 1535, as said below
- attn_gain: bfloat16 [2048], P('shard'), may hold values from 0.5 to 1.5
- w_query: bfloat16 [2048, 2048], P('shard', 'seq'), may hold values from -0.125 to 0.125
- w_key: bfloat16 [2048, 2048], P('shard', 'seq'), may hold values from -0.125 to 0.125
- w_value: bfloat16 [2048, 2048], P('shard', 'seq'), may hold values from -0.125 to 0.125
- w_output: bfloat16 [2048, 2048], P('seq', 'shard'), may hold values from -0.75 to 0.75
- mlp_gain: bfloat16 [2048], P('shard'), may hold values from 0.5 to 1.5
- w_gate: bfloat16 [2048, 8192], P('shard', 'seq'), may hold values from -0.125 to 0.125
- w_up: bfloat16 [2048, 8192], P('shard', 'seq'), may hold values from -0.125 to 0.125
- w_down: bfloat16 [8192, 2048], P('seq', 'shard'), may hold values from -0.0625 to 0.0625
- cotangent: bfloat16 [4, 1536, 2048], P('shard', 'seq'), may hold values from -6 to 6
Outputs:
- output: bfloat16 [4, 1536, 2048], P('shard', 'seq')
- d_inputs: bfloat16 [4, 1536, 2048], P('shard', 'seq')
- d_attn_gain: float32 [2048], P('shard')
- d_w_query: float32 [2048, 2048], P('shard', 'seq')
- d_w_key: float32 [2048, 2048], P('shard', 'seq')
- d_w_value: float32 [2048, 2048], P('shard', 'seq')
- d_w_output: float32 [2048, 2048], P('seq', 'shard')
- d_mlp_gain: float32 [2048], P('shard')
- d_w_gate: float32 [2048, 8192], P('shard', 'seq')
- d_w_up: float32 [2048, 8192], P('shard', 'seq')
- d_w_down: float32 [8192, 2048], P('seq', 'shard')
The draws below stay inside these ranges and needn't reach their ends.
Inputs may be any that keep to these rules, and one draw needn't show every extreme that they name: `positions`: within each sequence documents begin at places drawn from the seed, the first at token 0; a token's id is its offset from the start of its document. One sequence, drawn from the seed, is a single document of all 1536 tokens.
All inputs are finite; a program needn't handle non-finite values.
Results may differ from the reference program's by a relative error of at most 0.02.
Values may be sent and summed in bfloat16 or wider, within the bound.
A program may use at most 256 MiB of HBM per device.

```python
import math
import jax
import jax.numpy as jnp
from jax import lax

D = 2048
HEADS = 32
HD = 64
FF = 8192
SEQS = 4
LEN = 1536


def draw_positions(key, part):
    key = jax.random.fold_in(key, 11)
    mark_key = jax.random.fold_in(key, 1)
    pick_key = jax.random.fold_in(key, 2)
    spacing = max(4, LEN // 8)
    marks = jax.random.randint(mark_key, (SEQS, LEN), 0, spacing) == 0
    chosen = jax.random.randint(pick_key, (), 0, SEQS).astype(jnp.int32)
    rows = jnp.arange(SEQS, dtype=jnp.int32)[:, None]
    marks = jnp.logical_and(marks, rows != chosen)
    index = jnp.broadcast_to(jnp.arange(LEN, dtype=jnp.int32)[None, :], (SEQS, LEN))
    starts = lax.cummax(jnp.where(marks, index, 0), axis=1)
    return (index - starts).astype(jnp.int32)


def block_levels(rng, extent, pieces, smallest, top_value):
    level = 1.0
    for position, parts in pieces:
        heights = jax.random.uniform(jax.random.fold_in(jax.random.fold_in(rng, 6), position), (parts,), jnp.float32, smallest / len(pieces), top_value / len(pieces))
        level = level * jnp.repeat(jnp.exp(heights), extent[position] // parts).reshape((-1,) + (1,) * (len(extent) - 1 - position))
    return level


def bell_draw(stream_key, extent, width, reach, split=(), held_as=jnp.bfloat16):
    array = width * jax.random.normal(stream_key, extent, jnp.float32)
    if split:
        array = array * block_levels(stream_key, extent, split, -0.22, 0.18)
    return jnp.clip(array, -reach, reach).astype(held_as)


def setup_inputs(seed: int = 0) -> dict:
    streams_of = jax.random.split(jax.random.key(seed), 13)
    return {
        "inputs": bell_draw(streams_of[0], (SEQS, LEN, D), 1.0, 6.0, ((0, 4), (1, 8))),
        "positions": draw_positions(jax.random.fold_in(streams_of[12], 71), 0),
        "attn_gain": jnp.clip(1.0 + 0.1 * jax.random.normal(streams_of[2], (D,), jnp.float32), 0.5, 1.5).astype(jnp.bfloat16),
        "w_query": bell_draw(streams_of[3], (D, D), D ** -0.5, 0.125, ((0, 4), (1, 8))),
        "w_key": bell_draw(streams_of[4], (D, D), D ** -0.5, 0.125, ((0, 4), (1, 8))),
        "w_value": bell_draw(streams_of[5], (D, D), D ** -0.5, 0.125, ((0, 4), (1, 8))),
        "w_output": bell_draw(streams_of[6], (D, D), (D // 32) ** -0.5, 0.75, ((0, 8), (1, 4))),
        "mlp_gain": jnp.clip(1.0 + 0.1 * jax.random.normal(streams_of[7], (D,), jnp.float32), 0.5, 1.5).astype(jnp.bfloat16),
        "w_gate": bell_draw(streams_of[8], (D, FF), D ** -0.5, 0.125, ((0, 4), (1, 8))),
        "w_up": bell_draw(streams_of[9], (D, FF), D ** -0.5, 0.125, ((0, 4), (1, 8))),
        "w_down": bell_draw(streams_of[10], (FF, D), FF ** -0.5, 0.0625, ((0, 8), (1, 4))),
        "cotangent": bell_draw(streams_of[11], (SEQS, LEN, D), 1.0, 6.0, ((0, 4), (1, 8))),
    }


epsilon = 1e-05
theta_base = 130000.0
highest = lax.Precision.HIGHEST

@jax.custom_vjp
def low(v):
    return lax.optimization_barrier(v.astype(jnp.bfloat16)).astype(jnp.float32)

@jax.custom_vjp
def low_back(v):
    return v

def low_keep(v):
    return (low(v), None)

def low_pass(kept, grad):
    return (grad,)

def back_keep(v):
    return (v, None)

def back_low(kept, grad):
    return (low(grad),)
low.defvjp(low_keep, low_pass)
low_back.defvjp(back_keep, back_low)

def rms_norm(values, gain):
    return values * lax.rsqrt(lax.optimization_barrier(jnp.mean(values * values, axis=-1, keepdims=True)) + epsilon) * gain

def rotate(values, position_ids):
    half = HD // 2
    freqs = theta_base ** (-(jnp.arange(half).astype(jnp.float32) * 2.0) / HD)
    angles = position_ids.astype(jnp.float32)[:, None] * freqs[None, :]
    cosine = jnp.cos(angles)[:, None, :]
    sine = jnp.sin(angles)[:, None, :]
    first_half = values[..., :half]
    second_half = values[..., half:]
    return jnp.concatenate([first_half * cosine - second_half * sine, second_half * cosine + first_half * sine], axis=-1)

def layer(layer_in, position_ids, gain_first, query_weight, key_weight, value_weight, output_weight, gain_second, gate_weight, up_weight, down_weight):
    length = layer_in.shape[0]
    score_scale = 1.0 / math.sqrt(HD)
    normed_one = low(rms_norm(layer_in, gain_first))

    def rotary(weight):
        projected = low_back(jnp.dot(normed_one, weight, precision=highest))
        return low(low_back(rotate(projected.reshape(length, HEADS, HD), position_ids)))
    queries = rotary(query_weight)
    keys = rotary(key_weight)
    values = low(low_back(jnp.dot(normed_one, value_weight, precision=highest))).reshape(length, HEADS, HD)
    block_rows = min(512, length)
    key_index = jnp.arange(length).astype(jnp.int32)

    def attend(start):
        query_block = lax.dynamic_slice_in_dim(queries, start, block_rows, 0)
        scores = low_back(jnp.einsum('qhd,khd->hqk', query_block, keys, precision=highest) * score_scale)
        row_index = start + jnp.arange(block_rows).astype(jnp.int32)
        allowed = row_index[:, None] >= key_index[None, :]
        probs = jax.nn.softmax(jnp.where(allowed[None], scores, -1e+30), axis=-1)
        return jnp.einsum('hqk,khd->qhd', low(probs), values, precision=highest)
    starts = (jnp.arange(length // block_rows) * block_rows).astype(jnp.int32)
    mixed = lax.map(jax.checkpoint(attend), starts).reshape(length, HEADS * HD)
    mixed = low(low_back(mixed))
    hidden_state = layer_in + low_back(jnp.dot(mixed, output_weight, precision=highest))
    normed_two = low(rms_norm(hidden_state, gain_second))
    gate_pre = low_back(jnp.dot(normed_two, gate_weight, precision=highest))
    up_pre = low_back(jnp.dot(normed_two, up_weight, precision=highest))
    activ = low(jax.nn.silu(gate_pre) * up_pre)
    return hidden_state + low_back(jnp.dot(activ, down_weight, precision=highest))

def reference(inputs, positions, attn_gain, w_query, w_key, w_value, w_output, mlp_gain, w_gate, w_up, w_down, cotangent):
    weights = tuple((item.astype(jnp.float32) for item in (attn_gain, w_query, w_key, w_value, w_output, mlp_gain, w_gate, w_up, w_down)))
    zero_grads = tuple((jnp.zeros(item.shape, jnp.float32) for item in weights))

    def one_sequence(totals, item):
        values_in, position_ids, grad_out = item

        def apply_layer(layer_in, *params):
            return layer(layer_in, position_ids, *params)
        result, pullback = jax.vjp(apply_layer, values_in.astype(jnp.float32), *weights)
        grads = pullback(grad_out.astype(jnp.float32))
        totals = tuple((total + grad for total, grad in zip(totals, grads[1:])))
        return (totals, (result.astype(jnp.bfloat16), grads[0].astype(jnp.bfloat16)))
    totals, (outputs, d_inputs) = lax.scan(one_sequence, zero_grads, (inputs, positions, cotangent))
    return (outputs, d_inputs, totals[0], totals[1], totals[2], totals[3], totals[4], totals[5], totals[6], totals[7], totals[8])
```

```python
import math

import jax
import jax.numpy as jnp
from jax import lax
from jax.sharding import PartitionSpec as P

HD = 64


epsilon = 1e-05
theta_base = 130000.0
masked_score = -1e30


def product(left, right):
    return jnp.dot(left, right, preferred_element_type=jnp.float32)


def product_left_t(left, right):
    return lax.dot_general(
        left, right, (((0,), (0,)), ((), ())), preferred_element_type=jnp.float32
    )


def product_right_t(left, right):
    return lax.dot_general(
        left, right, (((1,), (1,)), ((), ())), preferred_element_type=jnp.float32
    )


def inverse_rms(values):
    return lax.rsqrt(jnp.mean(values * values, axis=-1, keepdims=True) + epsilon)


def norm_backward(values, inverse, gain, d_normed):
    scaled = d_normed * gain
    cubed = inverse * inverse * inverse
    d_values = inverse * scaled - values * cubed * jnp.mean(scaled * values, axis=-1, keepdims=True)
    d_gain = jnp.sum(d_normed * values * inverse, axis=0)
    return (d_values, d_gain)


def rotation_tables(position_ids, head_size):
    half = head_size // 2
    freqs = theta_base ** (-(jnp.arange(half, dtype=jnp.float32) * 2.0) / head_size)
    angles = position_ids.astype(jnp.float32)[:, None] * freqs[None, :]
    return (jnp.cos(angles), jnp.sin(angles))


def rotate(values, cosine, sine, head_size):
    row_count = values.shape[0]
    shaped = values.reshape(row_count, -1, head_size)
    half = head_size // 2
    first_half = shaped[..., :half]
    second_half = shaped[..., half:]
    cos_rows = cosine[:, None, :]
    sin_rows = sine[:, None, :]
    turned = jnp.concatenate(
        [
            first_half * cos_rows - second_half * sin_rows,
            second_half * cos_rows + first_half * sin_rows,
        ],
        axis=-1,
    )
    return turned.reshape(row_count, -1)


def attention_forward(queries, keys, values, head_size):
    length, width = queries.shape
    heads = width // head_size
    block_rows = min(512, length)
    blocks = length // block_rows
    score_scale = 1.0 / math.sqrt(head_size)
    query_blocks = queries.reshape(blocks, block_rows, heads, head_size)
    key_heads = keys.reshape(length, heads, head_size)
    value_heads = values.reshape(length, heads, head_size)
    key_index = jnp.arange(length, dtype=jnp.int32)

    def one_block(inputs):
        index, query_block = inputs
        scores = (
            jnp.einsum("qhd,khd->hqk", query_block, key_heads, preferred_element_type=jnp.float32)
            * score_scale
        )
        row_index = index * block_rows + jnp.arange(block_rows, dtype=jnp.int32)
        allowed = row_index[:, None] >= key_index[None, :]
        scores = jnp.where(allowed[None], scores, masked_score)
        largest = jnp.max(scores, axis=-1, keepdims=True)
        expo = jnp.exp(scores - largest)
        totals = jnp.sum(expo, axis=-1, keepdims=True)
        probs_low = (expo / totals).astype(jnp.bfloat16)
        mixed = jnp.einsum(
            "hqk,khd->qhd", probs_low, value_heads, preferred_element_type=jnp.float32
        )
        return (mixed.astype(jnp.bfloat16), largest + jnp.log(totals))

    mixed, log_totals = lax.map(one_block, (jnp.arange(blocks, dtype=jnp.int32), query_blocks))
    return (mixed.reshape(length, width), log_totals)


def attention_backward(queries, keys, values, log_totals, d_mixed, head_size):
    length, width = queries.shape
    heads = width // head_size
    block_rows = min(512, length)
    blocks = length // block_rows
    score_scale = 1.0 / math.sqrt(head_size)
    query_blocks = queries.reshape(blocks, block_rows, heads, head_size)
    grad_blocks = d_mixed.reshape(blocks, block_rows, heads, head_size)
    key_heads = keys.reshape(length, heads, head_size)
    value_heads = values.reshape(length, heads, head_size)
    key_index = jnp.arange(length, dtype=jnp.int32)

    def one_block(carry, inputs):
        d_keys, d_values = carry
        index, query_block, grad_block, log_block = inputs
        scores = (
            jnp.einsum("qhd,khd->hqk", query_block, key_heads, preferred_element_type=jnp.float32)
            * score_scale
        )
        row_index = index * block_rows + jnp.arange(block_rows, dtype=jnp.int32)
        allowed = row_index[:, None] >= key_index[None, :]
        probs = jnp.where(allowed[None], jnp.exp(scores - log_block), 0.0)
        probs_low = probs.astype(jnp.bfloat16)
        d_values = d_values + jnp.einsum(
            "hqk,qhd->khd", probs_low, grad_block, preferred_element_type=jnp.float32
        )
        d_probs = jnp.einsum(
            "qhd,khd->hqk", grad_block, value_heads, preferred_element_type=jnp.float32
        )
        inner = jnp.sum(d_probs * probs, axis=-1, keepdims=True)
        d_scores = (probs * (d_probs - inner)).astype(jnp.bfloat16)
        d_query = (
            jnp.einsum("hqk,khd->qhd", d_scores, key_heads, preferred_element_type=jnp.float32)
            * score_scale
        )
        d_keys = (
            d_keys
            + jnp.einsum("hqk,qhd->khd", d_scores, query_block, preferred_element_type=jnp.float32)
            * score_scale
        )
        return ((d_keys, d_values), d_query)

    zeros = jnp.zeros((length, heads, head_size), jnp.float32)
    (d_keys, d_values), d_queries = lax.scan(
        one_block,
        (zeros, zeros),
        (jnp.arange(blocks, dtype=jnp.int32), query_blocks, grad_blocks, log_totals),
    )
    return (
        d_queries.reshape(length, width).astype(jnp.bfloat16),
        d_keys.reshape(length, width).astype(jnp.bfloat16),
        d_values.reshape(length, width).astype(jnp.bfloat16),
    )


def seq_partials(term, row_count):
    return lax.psum_scatter(
        term(jnp.int32(0), row_count * lax.axis_size("seq")).astype(jnp.bfloat16),
        "seq",
        scatter_dimension=0,
        tiled=True,
    ).astype(jnp.float32)


def body(
    inputs,
    positions,
    attn_gain,
    w_query,
    w_key,
    w_value,
    w_output,
    mlp_gain,
    w_gate,
    w_up,
    w_down,
    cotangent,
):
    tokens = inputs.shape[1]
    head_size = HD
    cols = w_query.shape[1]
    input_rows = inputs[0].astype(jnp.float32)
    grad_rows = cotangent[0]
    gains = lax.all_gather(jnp.stack([attn_gain, mlp_gain]), "shard", axis=1, tiled=True)
    gain_first = gains[0].astype(jnp.float32)
    gain_second = gains[1].astype(jnp.float32)
    position_all = lax.all_gather(positions[0], "seq", axis=0, tiled=True)
    inverse_one = inverse_rms(input_rows)
    normed_one = (input_rows * inverse_one * gain_first).astype(jnp.bfloat16)
    normed_all_one = lax.all_gather(normed_one, "seq", axis=0, tiled=True)
    attn_cols = lax.all_gather(
        jnp.concatenate([w_query, w_key, w_value], axis=1), "shard", axis=0, tiled=True
    )
    output_rows = lax.all_gather(w_output, "shard", axis=1, tiled=True)
    gate_cols = lax.all_gather(w_gate, "shard", axis=0, tiled=True)
    up_cols = lax.all_gather(w_up, "shard", axis=0, tiled=True)
    down_rows = lax.all_gather(w_down, "shard", axis=1, tiled=True)
    grad_all = lax.all_gather(grad_rows, "seq", axis=0, tiled=True)

    cosine, sine = rotation_tables(position_all, head_size)
    projected = product(normed_all_one, attn_cols)
    query_head = rotate(projected[:, :cols], cosine, sine, head_size).astype(jnp.bfloat16)
    key_head = rotate(projected[:, cols : 2 * cols], cosine, sine, head_size).astype(jnp.bfloat16)
    value_head = projected[:, 2 * cols :].astype(jnp.bfloat16)
    mixed_head, log_totals = attention_forward(query_head, key_head, value_head, head_size)
    attn_out = seq_partials(lambda start, count: product(mixed_head, output_rows), tokens)
    hidden_state = input_rows + attn_out
    inverse_two = inverse_rms(hidden_state)
    normed_two = (hidden_state * inverse_two * gain_second).astype(jnp.bfloat16)
    normed_all_two = lax.all_gather(normed_two, "seq", axis=0, tiled=True)
    gate_pre = product(normed_all_two, gate_cols)
    up_pre = product(normed_all_two, up_cols)
    gate_sigmoid = jax.nn.sigmoid(gate_pre)
    gate_silu = gate_pre * gate_sigmoid
    activ = (gate_silu * up_pre).astype(jnp.bfloat16)
    mlp_out = seq_partials(lambda start, count: product(activ, down_rows), tokens)
    output = (hidden_state + mlp_out).astype(jnp.bfloat16)
    d_activ = product_right_t(grad_all, down_rows)
    d_gate = (d_activ * up_pre * gate_sigmoid * (1.0 + gate_pre * (1.0 - gate_sigmoid))).astype(
        jnp.bfloat16
    )
    d_up = (d_activ * gate_silu).astype(jnp.bfloat16)
    d_normed_two = seq_partials(
        lambda start, count: product_right_t(d_gate, gate_cols) + product_right_t(d_up, up_cols),
        tokens,
    )
    grad_gate = product_left_t(normed_all_two, d_gate)
    grad_up = product_left_t(normed_all_two, d_up)
    grad_down = product_left_t(activ, grad_all)
    d_norm_two, gain_grad_two = norm_backward(hidden_state, inverse_two, gain_second, d_normed_two)
    d_hidden = grad_rows.astype(jnp.float32) + d_norm_two
    d_attn = lax.all_gather(d_hidden.astype(jnp.bfloat16), "seq", axis=0, tiled=True)
    d_mixed_head = product_right_t(d_attn, output_rows).astype(jnp.bfloat16)
    grad_output = product_left_t(mixed_head, d_attn)
    d_query_head, d_key_head, d_value_head = attention_backward(
        query_head, key_head, value_head, log_totals, d_mixed_head, head_size
    )
    d_query = rotate(d_query_head.astype(jnp.float32), cosine, -sine, head_size)
    d_key = rotate(d_key_head.astype(jnp.float32), cosine, -sine, head_size)
    d_qkv = jnp.concatenate(
        [d_query.astype(jnp.bfloat16), d_key.astype(jnp.bfloat16), d_value_head], axis=1
    )
    d_normed_one = seq_partials(lambda start, count: product_right_t(d_qkv, attn_cols), tokens)
    grad_attn = product_left_t(normed_all_one, d_qkv)
    d_norm_one, gain_grad_one = norm_backward(input_rows, inverse_one, gain_first, d_normed_one)
    d_inputs = (d_hidden + d_norm_one).astype(jnp.bfloat16)
    gain_sums = lax.psum(jnp.stack([gain_grad_one, gain_grad_two]), "seq")

    def shard_sum(grad, dimension):
        return lax.psum_scatter(
            grad.astype(jnp.bfloat16), "shard", scatter_dimension=dimension, tiled=True
        ).astype(jnp.float32)

    attn_sum = shard_sum(grad_attn, 0)
    gain_out = lax.psum_scatter(gain_sums, "shard", scatter_dimension=1, tiled=True)
    return (
        output[None],
        d_inputs[None],
        gain_out[0],
        attn_sum[:, :cols],
        attn_sum[:, cols : 2 * cols],
        attn_sum[:, 2 * cols :],
        shard_sum(grad_output, 1),
        gain_out[1],
        shard_sum(grad_gate, 0),
        shard_sum(grad_up, 0),
        shard_sum(grad_down, 1),
    )


def solution(mesh):
    in_specs = (
        P("shard", "seq", None),
        P("shard", "seq"),
        P("shard"),
        P("shard", "seq"),
        P("shard", "seq"),
        P("shard", "seq"),
        P("seq", "shard"),
        P("shard"),
        P("shard", "seq"),
        P("shard", "seq"),
        P("seq", "shard"),
        P("shard", "seq", None),
    )
    out_specs = (
        P("shard", "seq", None),
        P("shard", "seq", None),
        P("shard"),
        P("shard", "seq"),
        P("shard", "seq"),
        P("shard", "seq"),
        P("seq", "shard"),
        P("shard"),
        P("shard", "seq"),
        P("shard", "seq"),
        P("seq", "shard"),
    )
    return jax.shard_map(body, mesh=mesh, in_specs=in_specs, out_specs=out_specs, check_vma=False)
```

```python
import math

import jax
import jax.numpy as jnp
from jax import lax
from jax.experimental import pallas as pl
from jax.experimental.pallas import tpu as pltpu
from jax.sharding import PartitionSpec as P

HD = 64
epsilon = 1e-05
theta_base = 130000.0
bf16 = jnp.bfloat16
f32 = jnp.float32
VMEM = pltpu.VMEM
DMA = pltpu.SemaphoreType.DMA


def dot_nn(a, b):
    return jnp.dot(a, b, preferred_element_type=f32)


def dot_nt(a, b):
    return lax.dot_general(a, b, (((1,), (1,)), ((), ())), preferred_element_type=f32)


def in_vmem():
    return pl.BlockSpec(memory_space=VMEM)


def in_any():
    return pl.BlockSpec(memory_space=pl.ANY)


def kernel_params(collective_id=None, limit=60):
    if collective_id is None:
        return pltpu.CompilerParams(vmem_limit_bytes=limit << 20)
    return pltpu.CompilerParams(
        collective_id=collective_id, has_side_effects=True, vmem_limit_bytes=limit << 20
    )


def popcount(mask):
    return bin(mask).count("1")


def chip_masks(size):
    return sorted(range(0, size, 2), key=lambda m: (popcount(m), m))


def chip_bits(size):
    return [1 << b for b in range(1, size.bit_length() - 1)]


def last_hop(mask, core):
    set_bits = [1 << b for b in range(1, mask.bit_length()) if mask >> b & 1]
    return set_bits[-1] if core == 0 else set_bits[0]


def seq_neighbours(size):
    return [1] + chip_bits(size)


def entry_barrier(seq_size=0, shard_size=0):
    barrier = pltpu.get_barrier_semaphore()
    count = 0
    if seq_size:
        me = lax.axis_index("seq")
        for mask in seq_neighbours(seq_size):
            pl.semaphore_signal(
                barrier, inc=1, device_id={"seq": jnp.bitwise_xor(me, mask)},
                device_id_type=pl.DeviceIdType.MESH,
            )
            count += 1
    if shard_size:
        mine = lax.axis_index("shard")
        for step in range(1, shard_size):
            pl.semaphore_signal(
                barrier, inc=1, device_id={"shard": lax.rem(mine + step, shard_size)},
                device_id_type=pl.DeviceIdType.MESH,
            )
            count += 1
    pl.semaphore_wait(barrier, count)


class SeqGather:
    def __init__(self, size, all_ref, send_sem, recv_sem, own=None):
        self.size, self.all_ref = size, all_ref
        self.send_sem, self.recv_sem = send_sem, recv_sem
        self.me = lax.axis_index("seq")
        self.core = lax.rem(self.me, 2)
        self.own = own

    def copy(self, arrives, hop):
        block = jnp.bitwise_xor(self.me, arrives ^ hop)
        src = self.all_ref.at[block]
        if arrives == hop and self.own is not None:
            src = self.own
        return pltpu.make_async_remote_copy(
            src_ref=src,
            dst_ref=self.all_ref.at[block],
            send_sem=self.send_sem.at[arrives],
            recv_sem=self.recv_sem.at[arrives],
            device_id={"seq": jnp.bitwise_xor(self.me, hop)},
            device_id_type=pl.DeviceIdType.MESH,
        )

    def wait_recv(self, mask):
        block = self.all_ref.at[jnp.bitwise_xor(self.me, mask)]
        pltpu.make_async_remote_copy(
            src_ref=block,
            dst_ref=block,
            send_sem=self.send_sem.at[mask],
            recv_sem=self.recv_sem.at[mask],
            device_id={"seq": jnp.bitwise_xor(self.me, 1)},
            device_id_type=pl.DeviceIdType.MESH,
        ).wait_recv()

    def start(self):
        for hop in reversed(seq_neighbours(self.size)):
            self.copy(hop, hop).start()

    def forward(self, mask):
        self.wait_recv(mask)
        for core in (0, 1):
            for hop in chip_bits(self.size):
                if not mask & hop and last_hop(mask | hop, core) == hop:

                    @pl.when(self.core == core)
                    def _():
                        self.copy(mask | hop, hop).start()

        self.copy(mask | 1, 1).start()

    def finish(self):
        for mask in chip_masks(self.size):
            self.wait_recv(mask | 1)
        for mask in range(1, self.size):
            self.copy(mask, 1 if mask & 1 else mask & -mask).wait_send()

    def run(self):
        self.start()
        for mask in chip_masks(self.size)[1:]:
            self.forward(mask)
        self.finish()


class SeqScatter:
    def __init__(self, size, terms, arrived, send_sem, recv_sem):
        self.size, self.terms, self.arrived = size, terms, arrived
        self.send_sem, self.recv_sem = send_sem, recv_sem
        self.me = lax.axis_index("seq")
        self.core = lax.rem(self.me, 2)
        self.order = chip_masks(size)[::-1]

    def copy(self, mask, hop):
        if mask & 1:
            src = self.terms.at[mask // 2, 1 - self.core]
        else:
            src = self.terms.at[mask // 2, self.core]
        return pltpu.make_async_remote_copy(
            src_ref=src,
            dst_ref=self.arrived.at[mask],
            send_sem=self.send_sem.at[mask],
            recv_sem=self.recv_sem.at[mask],
            device_id={"seq": jnp.bitwise_xor(self.me, hop)},
            device_id_type=pl.DeviceIdType.MESH,
        )

    def chip(self, mask):
        return jnp.bitwise_xor(self.me, mask) // 2

    def send_sibling(self, mask):
        self.copy(mask | 1, 1).start()

    def add(self, mask, source, write):
        rows = self.terms.shape[2]
        step = 32 if rows % 32 == 0 else 16

        @pl.loop(0, rows // step)
        def _(i):
            part = pl.ds(pl.multiple_of(i * step, step), step)
            total = self.terms[mask // 2, self.core, part, :].astype(f32)
            for s in source:
                total = total + self.arrived[s, part, :].astype(f32)
            write(part, total)

    def merge(self, mask, result=None):
        def keep(part, total):
            if mask:
                self.terms[mask // 2, self.core, part, :] = total.astype(bf16)
            else:
                result[part, :] = total

        self.copy(mask | 1, 1).wait_recv()
        for core in (0, 1):
            further = [
                mask | hop
                for hop in chip_bits(self.size)
                if not mask & hop and last_hop(mask | hop, core) == hop
            ]

            @pl.when(self.core == core)
            def _():
                for m in further:
                    self.copy(m, 1).wait_recv()
                self.add(mask, [mask | 1] + further, keep)
                if mask:
                    self.copy(mask, last_hop(mask, core)).start()

    def finish(self):
        for mask in range(1, self.size):
            self.copy(mask, 1).wait_send()


class LineGather:
    def __init__(self, size, own, out, send_sem, recv_sem, copy_sem):
        self.size, self.own, self.out = size, own, out
        self.send_sem, self.recv_sem, self.copy_sem = send_sem, recv_sem, copy_sem
        self.k = lax.axis_index("shard")

    def sent(self, way, step):
        block = self.k - step if way == 0 else self.k + step
        valid = (
            jnp.logical_and(self.k < self.size - 1, block >= 0)
            if way == 0
            else jnp.logical_and(self.k > 0, block <= self.size - 1)
        )
        safe = jnp.clip(block, 0, self.size - 1)
        target = jnp.clip(self.k + 1 if way == 0 else self.k - 1, 0, self.size - 1)
        src = self.own if step == 0 else self.out.at[safe]
        return valid, pltpu.make_async_remote_copy(
            src_ref=src,
            dst_ref=self.out.at[safe],
            send_sem=self.send_sem.at[way, step],
            recv_sem=self.recv_sem.at[way, step],
            device_id={"shard": target},
            device_id_type=pl.DeviceIdType.MESH,
        )

    def received(self, way, step):
        block = self.k - 1 - step if way == 0 else self.k + 1 + step
        valid = block >= 0 if way == 0 else block <= self.size - 1
        safe = jnp.clip(block, 0, self.size - 1)
        return valid, pltpu.make_async_remote_copy(
            src_ref=self.own,
            dst_ref=self.out.at[safe],
            send_sem=self.send_sem.at[way, step],
            recv_sem=self.recv_sem.at[way, step],
            device_id={"shard": lax.rem(self.k + 1, self.size)},
            device_id_type=pl.DeviceIdType.MESH,
        )

    def local(self):
        return pltpu.make_async_copy(self.own, self.out.at[self.k], self.copy_sem)

    def step(self, step):
        if step == 0:
            self.local().start()
        for way in (0, 1):
            if step > 0:
                valid, copy = self.received(way, step - 1)

                @pl.when(valid)
                def _():
                    copy.wait_recv()

            if step < self.size - 1:
                valid, copy = self.sent(way, step)

                @pl.when(valid)
                def _():
                    copy.start()

    def finish(self):
        self.local().wait()
        for step in range(self.size - 1):
            for way in (0, 1):
                valid, copy = self.sent(way, step)

                @pl.when(valid)
                def _():
                    copy.wait_send()


def inverse_rms(values):
    return lax.rsqrt(jnp.mean(values * values, axis=-1, keepdims=True) + epsilon)


def group_a(seq_size, shard_size, x, gains, table, cot, wq, wk, wv):
    rows, width = x.shape
    part, cols = wq.shape

    def kernel(
        x_ref, gains_ref, table_ref, cot_ref, wq_ref, wk_ref, wv_ref,
        normed_ref, table_all, cot_all, gains_all, wq_all, wk_all, wv_all,
        ns, nr, ts, tr, cs, cr, gs, gr, ws, wr, wc, cc,
    ):
        me = lax.axis_index("seq")
        mine = lax.axis_index("shard")
        entry_barrier(seq_size, shard_size)

        def gain_copy(step):
            return pltpu.make_async_remote_copy(
                src_ref=gains_ref,
                dst_ref=gains_all.at[mine],
                send_sem=gs.at[step],
                recv_sem=gr.at[step],
                device_id={"shard": lax.rem(mine + step, shard_size)},
                device_id_type=pl.DeviceIdType.MESH,
            )

        def gain_arrival(step):
            return pltpu.make_async_remote_copy(
                src_ref=gains_ref,
                dst_ref=gains_all.at[lax.rem(mine + shard_size - step, shard_size)],
                send_sem=gs.at[step],
                recv_sem=gr.at[step],
                device_id={"shard": lax.rem(mine + step, shard_size)},
                device_id_type=pl.DeviceIdType.MESH,
            )

        for step in range(1, shard_size):
            gain_copy(step).start()
        lines = [
            LineGather(shard_size, own, out, ws.at[i], wr.at[i], wc.at[i])
            for i, (own, out) in enumerate(
                ((wq_ref, wq_all), (wk_ref, wk_all), (wv_ref, wv_all))
            )
        ]
        for line in lines:
            line.step(0)
        gains_all[mine] = gains_ref[...]
        table_all[me] = table_ref[...]
        own_cot = pltpu.make_async_copy(cot_ref, cot_all.at[me], cc)
        own_cot.start()
        tables = SeqGather(seq_size, table_all, ts, tr)
        normed = SeqGather(seq_size, normed_ref, ns, nr)
        cots = SeqGather(seq_size, cot_all, cs, cr, own=cot_ref)
        tables.start()
        for step in range(1, shard_size):
            gain_arrival(step).wait_recv()
        values = x_ref[...].astype(f32)
        scaled = values * inverse_rms(values)
        for z in range(shard_size):
            lanes = slice(z * part, (z + 1) * part)
            normed_ref[me, :, lanes] = (scaled[:, lanes] * gains_all[z, 0:1, :]).astype(bf16)
        normed.start()
        cots.start()
        masks = chip_masks(seq_size)[1:]
        for line in lines:
            line.step(1)
        for mask in masks:
            tables.forward(mask)
        for mask in masks:
            normed.forward(mask)
        for step in range(2, shard_size):
            for line in lines:
                line.step(step)
            if step == 2:
                for mask in masks:
                    cots.forward(mask)
        for step in range(1, shard_size):
            gain_copy(step).wait_send()
        tables.finish()
        normed.finish()
        own_cot.wait()
        cots.finish()
        for line in lines:
            line.finish()

    weight = jax.ShapeDtypeStruct((shard_size, part, cols), bf16)
    return pl.pallas_call(
        kernel,
        name="gather_tokens",
        out_shape=[
            jax.ShapeDtypeStruct((seq_size, rows, width), bf16),
            jax.ShapeDtypeStruct((seq_size, rows, table.shape[1]), f32),
            jax.ShapeDtypeStruct((seq_size, rows, width), bf16),
            jax.ShapeDtypeStruct((shard_size,) + gains.shape, f32),
            weight,
            weight,
            weight,
        ],
        in_specs=[in_vmem()] * 7,
        out_specs=[in_vmem(), in_vmem(), in_any(), in_vmem(), in_vmem(), in_vmem(), in_vmem()],
        scratch_shapes=[DMA((seq_size,))] * 6
        + [DMA((shard_size,))] * 2
        + [DMA((3, 2, shard_size - 1))] * 2
        + [DMA((3,)), DMA],
        compiler_params=kernel_params(1),
    )(x, gains, table, cot, wq, wk, wv)


def head_lanes(head, shape):
    lane = lax.broadcasted_iota(jnp.int32, shape, 1)
    return lane < HD if head == 0 else lane >= HD


def turn(values, table, back):
    count = values.shape[1] // HD
    cosine = jnp.concatenate([table[:, :HD]] * count, axis=1)
    sine = jnp.concatenate([table[:, HD:]] * count, axis=1)
    lane = lax.broadcasted_iota(jnp.int32, values.shape, 1)
    half = HD // 2
    width = values.shape[1]
    partner = jnp.where(
        lane % HD < half,
        pltpu.roll(values, width - half, 1),
        pltpu.roll(values, half, 1),
    )
    if back:
        return values * cosine - partner * sine
    return values * cosine + partner * sine


def attend(normed, table, wq, wk, wv):
    length, width = normed.shape
    cols = wq.shape[1]
    rows = 512 if length % 512 == 0 else length
    block = 256 if length % 256 == 0 else length
    scale = 1.0 / math.sqrt(HD)
    pair = 2 * HD

    def kernel(n_ref, t_ref, wq_ref, wk_ref, wv_ref, q_ref, k_ref, v_ref, o_ref, lse_ref):
        @pl.loop(0, length // rows)
        def _(i):
            part = pl.ds(pl.multiple_of(i * rows, rows), rows)
            tokens = n_ref[part, :]
            tab = t_ref[part, :]
            q = turn(dot_nn(tokens, wq_ref[...]), tab, False).astype(bf16)
            q_ref[part, :] = q * jnp.asarray(scale, bf16)
            k_ref[part, :] = turn(dot_nn(tokens, wk_ref[...]), tab, False).astype(bf16)
            v_ref[part, :] = dot_nn(tokens, wv_ref[...]).astype(bf16)

        @pl.loop(0, cols // pair)
        def _(hp):
            lanes = pl.ds(pl.multiple_of(hp * pair, pair), pair)
            for i in range(length // block):
                first, last = i * block, (i + 1) * block
                q2 = q_ref[first:last, lanes]
                out = None
                for head in (0, 1):
                    keep = head_lanes(head, q2.shape)
                    qm = jnp.where(keep, q2, jnp.zeros_like(q2))
                    s = dot_nt(qm, k_ref[:last, lanes])
                    r = lax.broadcasted_iota(jnp.int32, (block, block), 0)
                    c = lax.broadcasted_iota(jnp.int32, (block, block), 1)
                    tail = jnp.where(c <= r, s[:, first:], -1e30)
                    s = tail if i == 0 else jnp.concatenate([s[:, :first], tail], axis=1)
                    m = jnp.max(s, axis=1, keepdims=True)
                    p = jnp.exp(s - m)
                    total = jnp.sum(p, axis=1, keepdims=True)
                    low = (p * (1.0 / total)).astype(bf16)
                    o = dot_nn(low, v_ref[:last, lanes])
                    out = o if head == 0 else jnp.where(keep, o, out)
                    lse = jnp.transpose(jnp.broadcast_to(m + jnp.log(total), (block, 128)))
                    lse_ref[pl.ds(hp * 2 + head, 1), first:last] = lse[0:1, :]
                o_ref[first:last, lanes] = out.astype(bf16)

    head_array = jax.ShapeDtypeStruct((length, cols), bf16)
    return pl.pallas_call(
        kernel,
        name="attend",
        out_shape=[head_array] * 4
        + [jax.ShapeDtypeStruct((max(8, cols // HD), length), f32)],
        in_specs=[in_vmem()] * 5,
        out_specs=[in_vmem()] * 5,
        compiler_params=kernel_params(),
        cost_estimate=pl.CostEstimate(
            flops=6 * length * width * cols + 2 * length * length * cols,
            bytes_accessed=2 * length * width,
            transcendentals=length * length * cols // HD // 2,
        ),
    )(normed, table, wq, wk, wv)


def attend_back(d_attn, wo, mixed, q, k, v, lse, table, normed, wq, wk, wv):
    length, width = d_attn.shape
    cols = q.shape[1]
    shards, _, part = wo.shape
    rows = 512 if length % 512 == 0 else length
    block = 256 if length % 256 == 0 else length
    scale = 1.0 / math.sqrt(HD)
    pair = 2 * HD

    def kernel(
        da_ref, wo_ref, mixed_ref, q_ref, k_ref, v_ref, lse_ref, t_ref, n_ref,
        dq_ref, dk_ref, dv_ref, gq_ref, gk_ref, gv_ref, go_ref,
        do_ref, kt_ref, dk_acc, dv_acc, xt_ref,
    ):
        @pl.loop(0, length // rows)
        def _(i):
            r = pl.ds(pl.multiple_of(i * rows, rows), rows)
            total = dot_nt(da_ref[r, :part], wo_ref[0])
            for z in range(1, shards):
                total += dot_nt(da_ref[r, z * part : (z + 1) * part], wo_ref[z])
            do_ref[r, :] = total.astype(bf16)

        kt_ref[...] = jnp.transpose(k_ref[...])

        @pl.loop(0, cols // pair)
        def _(hp):
            lanes = pl.ds(pl.multiple_of(hp * pair, pair), pair)
            dk_acc[...] = jnp.zeros_like(dk_acc)
            dv_acc[...] = jnp.zeros_like(dv_acc)
            for i in range(length // block):
                first, last = i * block, (i + 1) * block
                q2 = q_ref[first:last, lanes]
                do2 = do_ref[first:last, lanes]
                keys = k_ref[:last, lanes]
                values = v_ref[:last, lanes]
                dqt = None
                dk_add, dv_add = None, None
                for head in (0, 1):
                    keep = head_lanes(head, q2.shape)
                    qm = jnp.where(keep, q2, jnp.zeros_like(q2))
                    dom = jnp.where(keep, do2, jnp.zeros_like(do2))
                    st = dot_nt(keys, qm)
                    row = lse_ref[pl.ds(hp * 2 + head, 1), first:last]
                    p = jnp.exp(st - row)
                    r = lax.broadcasted_iota(jnp.int32, (block, block), 0)
                    c = lax.broadcasted_iota(jnp.int32, (block, block), 1)
                    tail = jnp.where(r <= c, p[first:], 0.0)
                    p = tail if i == 0 else jnp.concatenate([p[:first], tail], axis=0)
                    dp = dot_nt(values, dom)
                    inner = jnp.sum(dp * p, axis=0, keepdims=True)
                    ds = (p * (dp - inner)).astype(bf16)
                    dv_one = dot_nn(p.astype(bf16), dom)
                    dk_one = dot_nn(ds, qm)
                    dv_add = dv_one if head == 0 else dv_add + dv_one
                    dk_add = dk_one if head == 0 else dk_add + dk_one
                    dqt_one = dot_nn(kt_ref[lanes, :last], ds)
                    if head == 0:
                        dqt = dqt_one
                    else:
                        sub = lax.broadcasted_iota(jnp.int32, dqt.shape, 0)
                        dqt = jnp.where(sub < HD, dqt, dqt_one)
                dk_acc[:last, :] += dk_add
                dv_acc[:last, :] += dv_add
                dq = (jnp.transpose(dqt) * scale).astype(bf16).astype(f32)
                dq_ref[first:last, lanes] = turn(dq, t_ref[first:last, :], True).astype(bf16)
            dv_ref[:, lanes] = dv_acc[...].astype(bf16)

            @pl.loop(0, length // rows)
            def _(i):
                r = pl.ds(pl.multiple_of(i * rows, rows), rows)
                dk = dk_acc[r, :].astype(bf16).astype(f32)
                dk_ref[r, lanes] = turn(dk, t_ref[r, :], True).astype(bf16)

        for source, out in ((dq_ref, gq_ref), (dk_ref, gk_ref), (dv_ref, gv_ref)):
            xt_ref[...] = jnp.transpose(source[...])
            for z in range(shards):
                out[z] = dot_nn(xt_ref[...], n_ref[:, z * part : (z + 1) * part]).astype(bf16)
        xt_ref[...] = jnp.transpose(mixed_ref[...])
        for z in range(shards):
            go_ref[z] = dot_nn(xt_ref[...], da_ref[:, z * part : (z + 1) * part]).astype(bf16)

    head_array = jax.ShapeDtypeStruct((length, cols), bf16)
    grad = jax.ShapeDtypeStruct((shards, cols, part), bf16)
    return pl.pallas_call(
        kernel,
        name="attend_back",
        out_shape=[head_array] * 3 + [grad] * 4,
        in_specs=[in_vmem()] * 9,
        out_specs=[in_vmem()] * 7,
        scratch_shapes=[
            VMEM((length, cols), bf16),
            VMEM((cols, length), bf16),
            VMEM((length, pair), f32),
            VMEM((length, pair), f32),
            VMEM((cols, length), bf16),
        ],
        compiler_params=kernel_params(),
        cost_estimate=pl.CostEstimate(
            flops=10 * length * width * cols + 5 * length * length * cols,
            bytes_accessed=4 * length * width,
            transcendentals=length * length * cols // HD // 2,
        ),
    )(d_attn, wo, mixed, q, k, v, lse, table, normed)


def merge_attention(seq_size, shard_size, mixed, wo, x, gains_all):
    rows, width = x.shape
    cols = mixed.shape[1]
    part = wo.shape[2]
    chips = seq_size // 2

    def kernel(
        mixed_ref, wo_ref, x_ref, gains_ref, hidden_ref, normed_all,
        terms, arrived, normed_ref, ss, sr, ns, nr, own_sem,
    ):
        me = lax.axis_index("seq")
        entry_barrier(seq_size)
        scatter = SeqScatter(seq_size, terms, arrived, ss, sr)

        def compute(mask):
            start = pl.multiple_of(scatter.chip(mask) * (2 * rows), 2 * rows)
            tokens = mixed_ref[pl.ds(start, 2 * rows), :]
            for z in range(shard_size):
                terms[mask // 2, :, :, z * part : (z + 1) * part] = (
                    dot_nn(tokens, wo_ref[z]).astype(bf16).reshape(2, rows, part)
                )

        for mask in scatter.order:
            compute(mask)
            scatter.send_sibling(mask)
        for mask in scatter.order:
            scatter.merge(mask, hidden_ref)
        hidden = hidden_ref[...] + x_ref[...].astype(f32)
        hidden_ref[...] = hidden
        scaled = hidden * inverse_rms(hidden)
        for z in range(shard_size):
            lanes = slice(z * part, (z + 1) * part)
            normed_ref[:, lanes] = (scaled[:, lanes] * gains_ref[z, 1:2, :]).astype(bf16)
        gather = SeqGather(seq_size, normed_all, ns, nr, own=normed_ref)
        gather.start()
        own = pltpu.make_async_copy(normed_ref, normed_all.at[me], own_sem)
        own.start()
        for mask in chip_masks(seq_size)[1:]:
            gather.forward(mask)
        own.wait()
        gather.finish()
        scatter.finish()

    return pl.pallas_call(
        kernel,
        name="merge_attention",
        out_shape=[
            jax.ShapeDtypeStruct((rows, width), f32),
            jax.ShapeDtypeStruct((seq_size, rows, width), bf16),
        ],
        in_specs=[in_vmem()] * 4,
        out_specs=[in_vmem(), in_any()],
        scratch_shapes=[
            VMEM((chips, 2, rows, width), bf16),
            VMEM((seq_size, rows, width), bf16),
            VMEM((rows, width), bf16),
        ]
        + [DMA((seq_size,))] * 4
        + [DMA],
        compiler_params=kernel_params(2),
    )(mixed, wo, x, gains_all)


def mlp_chunk(normed, cot, wg, wu, wd):
    length, width = normed.shape
    hidden = wg.shape[1]
    shards, _, part = wd.shape
    rows = 512 if length % 512 == 0 else length
    block = 256 if hidden % 256 == 0 else hidden

    def kernel(
        n_ref, c_ref, wg_ref, wu_ref, wd_ref,
        a_ref, dg_ref, du_ref, gg_ref, gu_ref, gd_ref, xt_ref,
    ):
        for f in range(hidden // block):
            lanes = slice(f * block, (f + 1) * block)

            @pl.loop(0, length // rows)
            def _(i):
                r = pl.ds(pl.multiple_of(i * rows, rows), rows)
                tokens = n_ref[r, :]
                gate = dot_nn(tokens, wg_ref[:, lanes])
                up = dot_nn(tokens, wu_ref[:, lanes])
                d_act = dot_nt(c_ref[r, :part], wd_ref[0, lanes, :])
                for z in range(1, shards):
                    d_act += dot_nt(c_ref[r, z * part : (z + 1) * part], wd_ref[z, lanes, :])
                sig = jax.nn.sigmoid(gate)
                silu = gate * sig
                a_ref[r, lanes] = (silu * up).astype(bf16)
                dg_ref[r, lanes] = (d_act * up * (sig * (1.0 + gate * (1.0 - sig)))).astype(bf16)
                du_ref[r, lanes] = (d_act * silu).astype(bf16)

            for left, right, out in (
                (dg_ref, n_ref, gg_ref),
                (du_ref, n_ref, gu_ref),
                (a_ref, c_ref, gd_ref),
            ):
                xt_ref[...] = jnp.transpose(left[:, lanes])
                for z in range(shards):
                    out[z, lanes, :] = dot_nn(
                        xt_ref[...], right[:, z * part : (z + 1) * part]
                    ).astype(bf16)

    act = jax.ShapeDtypeStruct((length, hidden), bf16)
    grad = jax.ShapeDtypeStruct((shards, hidden, part), bf16)
    return pl.pallas_call(
        kernel,
        name="mlp_chunk",
        out_shape=[act] * 3 + [grad] * 3,
        in_specs=[in_vmem()] * 5,
        out_specs=[in_vmem()] * 6,
        scratch_shapes=[VMEM((block, length), bf16)],
        compiler_params=kernel_params(),
        cost_estimate=pl.CostEstimate(
            flops=12 * length * width * hidden,
            bytes_accessed=4 * length * width,
            transcendentals=length * hidden,
        ),
    )(normed, cot, wg, wu, wd)


def norm_back(values, inverse, gain, d_normed):
    scaled = d_normed * gain
    d_values = inverse * scaled - values * (inverse * inverse * inverse) * jnp.mean(
        scaled * values, axis=-1, keepdims=True
    )
    return d_values, jnp.sum(d_normed * values * inverse, axis=0, keepdims=True)


def mlp_back(seq_size, shard_size, d_gate, d_up, wg, wu, hidden, cot, gains_all):
    rows, width = hidden.shape
    units = wg.shape[1]
    part = width // shard_size
    chips = seq_size // 2

    def kernel(
        dg_ref, du_ref, wg_ref, wu_ref, hidden_ref, cot_ref, gains_ref,
        d_hidden_ref, d_gain_ref, d_attn_all,
        terms, arrived, d_attn_ref, ss, sr, ns, nr, own_sem,
    ):
        me = lax.axis_index("seq")
        entry_barrier(seq_size)
        scatter = SeqScatter(seq_size, terms, arrived, ss, sr)

        def compute(mask):
            start = pl.multiple_of(scatter.chip(mask) * (2 * rows), 2 * rows)
            dg = dg_ref[pl.ds(start, 2 * rows), :]
            du = du_ref[pl.ds(start, 2 * rows), :]
            for z in range(shard_size):
                lanes = slice(z * part, (z + 1) * part)
                total = dot_nt(dg, wg_ref[lanes, :]) + dot_nt(du, wu_ref[lanes, :])
                terms[mask // 2, :, :, lanes] = total.astype(bf16).reshape(2, rows, part)

        previous = None
        for mask in scatter.order:
            compute(mask)
            scatter.send_sibling(mask)
            if previous is not None:
                scatter.merge(previous)
            previous = mask
        scatter.merge(previous, d_hidden_ref)
        values = hidden_ref[...]
        gain = jnp.concatenate([gains_ref[z, 1:2, :] for z in range(shard_size)], axis=1)
        d_values, d_gain = norm_back(values, inverse_rms(values), gain, d_hidden_ref[...])
        d_hidden = cot_ref[...].astype(f32) + d_values
        d_attn_ref[...] = d_hidden.astype(bf16)
        gather = SeqGather(seq_size, d_attn_all, ns, nr, own=d_attn_ref)
        gather.start()
        own = pltpu.make_async_copy(d_attn_ref, d_attn_all.at[me], own_sem)
        own.start()
        d_hidden_ref[...] = d_hidden
        d_gain_ref[...] = d_gain
        for mask in chip_masks(seq_size)[1:]:
            gather.forward(mask)
        own.wait()
        gather.finish()
        scatter.finish()

    return pl.pallas_call(
        kernel,
        name="mlp_back",
        out_shape=[
            jax.ShapeDtypeStruct((rows, width), f32),
            jax.ShapeDtypeStruct((1, width), f32),
            jax.ShapeDtypeStruct((seq_size, rows, width), bf16),
        ],
        in_specs=[in_vmem()] * 7,
        out_specs=[in_vmem(), in_vmem(), in_any()],
        scratch_shapes=[
            VMEM((chips, 2, rows, width), bf16),
            VMEM((seq_size, rows, width), bf16),
            VMEM((rows, width), bf16),
        ]
        + [DMA((seq_size,))] * 4
        + [DMA],
        compiler_params=kernel_params(3),
    )(d_gate, d_up, wg, wu, hidden, cot, gains_all)


def mlp_out(seq_size, shard_size, activ, wd, hidden):
    rows, width = hidden.shape
    part = width // shard_size
    chips = seq_size // 2

    def kernel(a_ref, wd_ref, hidden_ref, out_ref, terms, arrived, total_ref, ss, sr):
        entry_barrier(seq_size)
        scatter = SeqScatter(seq_size, terms, arrived, ss, sr)
        previous = None
        for mask in scatter.order:
            start = pl.multiple_of(scatter.chip(mask) * (2 * rows), 2 * rows)
            tokens = a_ref[pl.ds(start, 2 * rows), :]
            for z in range(shard_size):
                terms[mask // 2, :, :, z * part : (z + 1) * part] = (
                    dot_nn(tokens, wd_ref[z]).astype(bf16).reshape(2, rows, part)
                )
            scatter.send_sibling(mask)
            if previous is not None:
                scatter.merge(previous)
            previous = mask
        scatter.merge(previous, total_ref)
        out_ref[...] = (total_ref[...] + hidden_ref[...]).astype(bf16)
        scatter.finish()

    return pl.pallas_call(
        kernel,
        name="mlp_out",
        out_shape=jax.ShapeDtypeStruct((rows, width), bf16),
        in_specs=[in_vmem()] * 3,
        out_specs=in_vmem(),
        scratch_shapes=[
            VMEM((chips, 2, rows, width), bf16),
            VMEM((seq_size, rows, width), bf16),
            VMEM((rows, width), f32),
        ]
        + [DMA((seq_size,))] * 2,
        compiler_params=kernel_params(4),
    )(activ, wd, hidden)


def inputs_back(seq_size, shard_size, dq, dk, dv, wq, wk, wv, x, d_hidden, gains_all, d_gain_two):
    rows, width = x.shape
    part = width // shard_size
    chips = seq_size // 2

    def kernel(
        dq_ref, dk_ref, dv_ref, wq_ref, wk_ref, wv_ref, x_ref, d_hidden_ref, gains_ref, gain2_ref,
        out_ref, gain_ref,
        terms, arrived, total_ref, mine_ref, from_shard, line_ref, from_seq,
        ss, sr, gs, gr, hs, hr,
    ):
        me = lax.axis_index("seq")
        mine = lax.axis_index("shard")
        barrier = pltpu.get_barrier_semaphore()
        for step in range(1, seq_size):
            pl.semaphore_signal(
                barrier, inc=1, device_id={"seq": jnp.bitwise_xor(me, step)},
                device_id_type=pl.DeviceIdType.MESH,
            )
        for step in range(1, shard_size):
            pl.semaphore_signal(
                barrier, inc=1, device_id={"shard": lax.rem(mine + step, shard_size)},
                device_id_type=pl.DeviceIdType.MESH,
            )
        pl.semaphore_wait(barrier, seq_size + shard_size - 2)
        scatter = SeqScatter(seq_size, terms, arrived, ss, sr)

        previous = None
        for mask in scatter.order:
            start = pl.multiple_of(scatter.chip(mask) * (2 * rows), 2 * rows)
            pair = pl.ds(start, 2 * rows)
            for z in range(shard_size):
                lanes = slice(z * part, (z + 1) * part)
                total = (
                    dot_nt(dq_ref[pair, :], wq_ref[z])
                    + dot_nt(dk_ref[pair, :], wk_ref[z])
                    + dot_nt(dv_ref[pair, :], wv_ref[z])
                )
                terms[mask // 2, :, :, lanes] = total.astype(bf16).reshape(2, rows, part)
            scatter.send_sibling(mask)
            if previous is not None:
                scatter.merge(previous)
            previous = mask
        scatter.merge(previous, total_ref)
        values = x_ref[...].astype(f32)
        gain = jnp.concatenate([gains_ref[z, 0:1, :] for z in range(shard_size)], axis=1)
        d_values, d_gain = norm_back(values, inverse_rms(values), gain, total_ref[...])
        out_ref[...] = (d_hidden_ref[...] + d_values).astype(bf16)
        for z in range(shard_size):
            lanes = slice(z * part, (z + 1) * part)
            mine_ref[z, 0:1, :] = d_gain[:, lanes]
            mine_ref[z, 1:2, :] = gain2_ref[0:1, lanes]
            mine_ref[z, 2:, :] = jnp.zeros((6, part), f32)

        def to_shard(step):
            return pltpu.make_async_remote_copy(
                src_ref=mine_ref.at[lax.rem(mine + step, shard_size)],
                dst_ref=from_shard.at[step],
                send_sem=gs.at[step],
                recv_sem=gr.at[step],
                device_id={"shard": lax.rem(mine + step, shard_size)},
                device_id_type=pl.DeviceIdType.MESH,
            )

        for step in range(1, shard_size):
            to_shard(step).start()
        for step in range(1, shard_size):
            to_shard(step).wait()
        line_ref[...] = mine_ref[mine] + sum(from_shard[step] for step in range(1, shard_size))

        def to_seq(step):
            return pltpu.make_async_remote_copy(
                src_ref=line_ref,
                dst_ref=from_seq.at[step],
                send_sem=hs.at[step],
                recv_sem=hr.at[step],
                device_id={"seq": jnp.bitwise_xor(me, step)},
                device_id_type=pl.DeviceIdType.MESH,
            )

        for step in range(1, seq_size):
            to_seq(step).start()
        for step in range(1, seq_size):
            to_seq(step).wait()
        gain_ref[...] = line_ref[...] + sum(from_seq[step] for step in range(1, seq_size))
        scatter.finish()

    return pl.pallas_call(
        kernel,
        name="inputs_back",
        out_shape=[
            jax.ShapeDtypeStruct((rows, width), bf16),
            jax.ShapeDtypeStruct((8, part), f32),
        ],
        in_specs=[in_vmem()] * 10,
        out_specs=[in_vmem()] * 2,
        scratch_shapes=[
            VMEM((chips, 2, rows, width), bf16),
            VMEM((seq_size, rows, width), bf16),
            VMEM((rows, width), f32),
            VMEM((shard_size, 8, part), f32),
            VMEM((shard_size, 8, part), f32),
            VMEM((8, part), f32),
            VMEM((seq_size, 8, part), f32),
        ]
        + [DMA((seq_size,))] * 2
        + [DMA((shard_size,))] * 2
        + [DMA((seq_size,))] * 2,
        compiler_params=kernel_params(5),
    )(dq, dk, dv, wq, wk, wv, x, d_hidden, gains_all, d_gain_two)


def rotation_table(position_ids):
    half = HD // 2
    freqs = theta_base ** (-(jnp.arange(half, dtype=f32) * 2.0) / HD)
    angles = position_ids.astype(f32)[:, None] * freqs[None, :]
    cosine, sine = jnp.cos(angles), jnp.sin(angles)
    return jnp.concatenate([cosine, cosine, -sine, sine], axis=1)


def shard_gather(block):
    return lax.all_gather(block, "shard", axis=0, tiled=False)


def shard_sum(terms):
    return lax.psum_scatter(terms, "shard", scatter_dimension=0, tiled=False).astype(f32)


def body(
    inputs,
    positions,
    attn_gain,
    w_query,
    w_key,
    w_value,
    w_output,
    mlp_gain,
    w_gate,
    w_up,
    w_down,
    cotangent,
):
    seq_size, shard_size = lax.axis_size("seq"), lax.axis_size("shard")
    x, cot = inputs[0], cotangent[0]
    rows, width = x.shape
    length = rows * seq_size
    gains = jnp.pad(jnp.stack([attn_gain, mlp_gain]).astype(f32), ((0, 6), (0, 0)))
    table = rotation_table(positions[0])
    wo = shard_gather(w_output)
    wg = shard_gather(w_gate).reshape(width, -1)
    wu = shard_gather(w_up).reshape(width, -1)
    wd = shard_gather(w_down)
    normed_one, tables, cot_all, gains_all, wq, wk, wv = group_a(
        seq_size, shard_size, x, gains, table, cot, w_query, w_key, w_value
    )
    normed_one = normed_one.reshape(length, width)
    tables = tables.reshape(length, -1)
    cot_all = cot_all.reshape(length, width)
    q, k, v, mixed, lse = attend(
        normed_one, tables, wq.reshape(width, -1), wk.reshape(width, -1), wv.reshape(width, -1)
    )
    hidden, normed_two = merge_attention(seq_size, shard_size, mixed, wo, x, gains_all)
    normed_two = normed_two.reshape(length, width)
    activ, d_gate, d_up, g_gate, g_up, g_down = mlp_chunk(normed_two, cot_all, wg, wu, wd)
    d_hidden, d_gain_two, d_attn = mlp_back(
        seq_size, shard_size, d_gate, d_up, wg, wu, hidden, cot, gains_all
    )
    d_attn = d_attn.reshape(length, width)
    output = mlp_out(seq_size, shard_size, activ, wd, hidden)
    dq, dk, dv, g_query, g_key, g_value, g_output = attend_back(
        d_attn, wo, mixed, q, k, v, lse, tables, normed_one, wq, wk, wv
    )
    d_inputs, gain_sums = inputs_back(
        seq_size, shard_size, dq, dk, dv, wq, wk, wv, x, d_hidden, gains_all, d_gain_two
    )
    return (
        output[None],
        d_inputs[None],
        gain_sums[0],
        shard_sum(g_query).T,
        shard_sum(g_key).T,
        shard_sum(g_value).T,
        shard_sum(g_output),
        gain_sums[1],
        shard_sum(g_gate).T,
        shard_sum(g_up).T,
        shard_sum(g_down),
    )


def solution(mesh):
    in_specs = (
        P("shard", "seq", None),
        P("shard", "seq"),
        P("shard"),
        P("shard", "seq"),
        P("shard", "seq"),
        P("shard", "seq"),
        P("seq", "shard"),
        P("shard"),
        P("shard", "seq"),
        P("shard", "seq"),
        P("seq", "shard"),
        P("shard", "seq", None),
    )
    out_specs = (
        P("shard", "seq", None),
        P("shard", "seq", None),
        P("shard"),
        P("shard", "seq"),
        P("shard", "seq"),
        P("shard", "seq"),
        P("seq", "shard"),
        P("shard"),
        P("shard", "seq"),
        P("shard", "seq"),
        P("seq", "shard"),
    )
    return jax.shard_map(body, mesh=mesh, in_specs=in_specs, out_specs=out_specs, check_vma=False)
```

```python
import math

import jax
import jax.numpy as jnp
from jax import lax
from jax.experimental import pallas as pl
from jax.experimental.pallas import tpu as pltpu
from jax.sharding import PartitionSpec as P

HD = 64
epsilon = 1e-05
theta_base = 130000.0
bf16 = jnp.bfloat16
f32 = jnp.float32
VMEM = pltpu.VMEM
DMA = pltpu.SemaphoreType.DMA
MESH = pl.DeviceIdType.MESH


def dot_nn(a, b):
    return jnp.dot(a, b, preferred_element_type=f32)


def dot_nt(a, b):
    return lax.dot_general(a, b, (((1,), (1,)), ((), ())), preferred_element_type=f32)


def in_vmem(count):
    return [pl.BlockSpec(memory_space=VMEM)] * count


def in_any(count):
    return [pl.BlockSpec(memory_space=pl.ANY)] * count


def array(shape, dtype=bf16):
    return jax.ShapeDtypeStruct(shape, dtype)


def kernel_params(collective_id=None, limit=62):
    if collective_id is None:
        return pltpu.CompilerParams(vmem_limit_bytes=limit << 20)
    return pltpu.CompilerParams(
        collective_id=collective_id, has_side_effects=True, vmem_limit_bytes=limit << 20
    )


def popcount(mask):
    return bin(mask).count("1")


def chip_masks(size):
    return sorted(range(0, size, 2), key=lambda m: (popcount(m), m))


def chip_bits(size):
    return [1 << b for b in range(1, size.bit_length() - 1)]


def last_hop(mask, core):
    set_bits = [1 << b for b in range(1, mask.bit_length()) if mask >> b & 1]
    return set_bits[-1] if core == 0 else set_bits[0]


def further_masks(mask, core, size):
    return [
        mask | hop
        for hop in chip_bits(size)
        if not mask & hop and last_hop(mask | hop, core) == hop
    ]


def seq_neighbours(size):
    return [1] + chip_bits(size)


def entry_barrier(seq_masks, shard_size):
    barrier = pltpu.get_barrier_semaphore()
    me, mine = lax.axis_index("seq"), lax.axis_index("shard")
    for mask in seq_masks:
        pl.semaphore_signal(
            barrier, inc=1, device_id={"seq": jnp.bitwise_xor(me, mask)}, device_id_type=MESH
        )
    for step in range(1, shard_size):
        pl.semaphore_signal(
            barrier, inc=1, device_id={"shard": lax.rem(mine + step, shard_size)},
            device_id_type=MESH,
        )
    pl.semaphore_wait(barrier, len(seq_masks) + max(shard_size - 1, 0))


class SeqGather:
    def __init__(self, size, out, rows, send_sem, recv_sem, own=None):
        self.size, self.out, self.rows = size, out, rows
        self.send_sem, self.recv_sem = send_sem, recv_sem
        self.me = lax.axis_index("seq")
        self.core = lax.rem(self.me, 2)
        self.own = own

    def block(self, index):
        return self.out.at[pl.ds(pl.multiple_of(index * self.rows, self.rows), self.rows), :]

    def copy(self, arrives, hop):
        block = self.block(jnp.bitwise_xor(self.me, arrives ^ hop))
        src = self.own if arrives == hop and self.own is not None else block
        return pltpu.make_async_remote_copy(
            src_ref=src,
            dst_ref=block,
            send_sem=self.send_sem.at[arrives],
            recv_sem=self.recv_sem.at[arrives],
            device_id={"seq": jnp.bitwise_xor(self.me, hop)},
            device_id_type=MESH,
        )

    def wait_recv(self, mask):
        block = self.block(jnp.bitwise_xor(self.me, mask))
        pltpu.make_async_remote_copy(
            src_ref=block,
            dst_ref=block,
            send_sem=self.send_sem.at[mask],
            recv_sem=self.recv_sem.at[mask],
            device_id={"seq": jnp.bitwise_xor(self.me, 1)},
            device_id_type=MESH,
        ).wait_recv()

    def start(self):
        for hop in reversed(seq_neighbours(self.size)):
            self.copy(hop, hop).start()

    def forward(self, mask):
        self.wait_recv(mask)
        for core in (0, 1):
            for more in further_masks(mask, core, self.size):

                @pl.when(self.core == core)
                def _():
                    self.copy(more, more ^ mask).start()

        self.copy(mask | 1, 1).start()

    def forwards(self):
        for mask in chip_masks(self.size)[1:]:
            self.forward(mask)

    def finish(self):
        for mask in chip_masks(self.size):
            self.wait_recv(mask | 1)
        for mask in range(1, self.size):
            self.copy(mask, 1 if mask & 1 else mask & -mask).wait_send()


def height(mask, core, size):
    return max([0] + [1 + height(m, core, size) for m in further_masks(mask, core, size)])


class SeqScatter:
    def __init__(self, size, terms, arrived, send_sem, recv_sem):
        self.size, self.terms, self.arrived = size, terms, arrived
        self.send_sem, self.recv_sem = send_sem, recv_sem
        self.me = lax.axis_index("seq")
        self.core = lax.rem(self.me, 2)
        self.masks = chip_masks(size)[::-1]
        self.order = [
            sorted(self.masks, key=lambda m: (height(m, core, size), -popcount(m)))
            for core in (0, 1)
        ]
        self.leaves = size // 4
        self.merged = 0

    def copy(self, mask, hop):
        core = 1 - self.core if mask & 1 else self.core
        return pltpu.make_async_remote_copy(
            src_ref=self.terms.at[mask // 2, core],
            dst_ref=self.arrived.at[mask - 1],
            send_sem=self.send_sem.at[mask],
            recv_sem=self.recv_sem.at[mask],
            device_id={"seq": jnp.bitwise_xor(self.me, hop)},
            device_id_type=MESH,
        )

    def tokens(self, mask, base=0):
        pair = 2 * self.terms.shape[2]
        start = jnp.bitwise_xor(self.me, mask) // 2 * pair + base
        return pl.ds(pl.multiple_of(start, pair), pair)

    def put(self, mask, lanes, total):
        rows = self.terms.shape[2]
        self.terms[mask // 2, :, :, lanes] = total.astype(bf16).reshape(2, rows, -1)

    def add(self, mask, source, write):
        rows = self.terms.shape[2]
        step = 32 if rows % 32 == 0 else 16

        @pl.loop(0, rows // step)
        def _(i):
            part = pl.ds(pl.multiple_of(i * step, step), step)
            total = self.terms[mask // 2, self.core, part, :].astype(f32)
            for s in source:
                total = total + self.arrived[s - 1, part, :].astype(f32)
            write(part, total)

    def merge(self, result=None):
        for core in (0, 1):
            mask = self.order[core][self.merged]
            further = further_masks(mask, core, self.size)

            def keep(part, total, mask=mask):
                if mask:
                    self.terms[mask // 2, self.core, part, :] = total.astype(bf16)
                else:
                    result[part, :] = total.astype(result.dtype)

            @pl.when(self.core == core)
            def _(mask=mask, further=further, keep=keep, core=core):
                for m in [mask | 1] + further:
                    self.copy(m, 1).wait_recv()
                self.add(mask, [mask | 1] + further, keep)
                if mask:
                    self.copy(mask, last_hop(mask, core)).start()

        self.merged += 1

    def send_terms(self, compute, merge=False):
        done = set()
        for mask in self.masks:
            compute(mask)
            self.copy(mask | 1, 1).start()
            if merge and self.merged < self.leaves:
                if all(order[self.merged] in done for order in self.order):
                    self.merge()
            done.add(mask)
        if merge:
            self.merge_leaves()

    def merge_leaves(self):
        while self.merged < self.leaves:
            self.merge()

    def merge_inner(self):
        while self.merged < len(self.masks) - 1:
            self.merge()

    def run(self, compute, result):
        self.send_terms(compute, merge=True)
        self.merge_inner()
        self.merge(result)

    def finish(self):
        for mask in range(1, self.size):
            self.copy(mask, 1).wait_send()


def scatter_scratch(seq_size, rows, width):
    return [
        VMEM((seq_size // 2, 2, rows, width), bf16),
        VMEM((seq_size - 1, rows, width), bf16),
        DMA((seq_size,)),
        DMA((seq_size,)),
    ]


class LineGather:
    def __init__(self, size, own, out, send_sem, recv_sem, copy_sem):
        self.size, self.own, self.out = size, own, out
        self.send_sem, self.recv_sem, self.copy_sem = send_sem, recv_sem, copy_sem
        self.k = lax.axis_index("shard")

    def sent(self, way, step):
        block = self.k - step if way == 0 else self.k + step
        valid = (
            jnp.logical_and(self.k < self.size - 1, block >= 0)
            if way == 0
            else jnp.logical_and(self.k > 0, block <= self.size - 1)
        )
        safe = jnp.clip(block, 0, self.size - 1)
        target = jnp.clip(self.k + 1 if way == 0 else self.k - 1, 0, self.size - 1)
        return valid, pltpu.make_async_remote_copy(
            src_ref=self.own if step == 0 else self.out.at[safe],
            dst_ref=self.out.at[safe],
            send_sem=self.send_sem.at[way, step],
            recv_sem=self.recv_sem.at[way, step],
            device_id={"shard": target},
            device_id_type=MESH,
        )

    def received(self, way, step):
        block = self.k - 1 - step if way == 0 else self.k + 1 + step
        valid = block >= 0 if way == 0 else block <= self.size - 1
        safe = jnp.clip(block, 0, self.size - 1)
        return valid, pltpu.make_async_remote_copy(
            src_ref=self.own,
            dst_ref=self.out.at[safe],
            send_sem=self.send_sem.at[way, step],
            recv_sem=self.recv_sem.at[way, step],
            device_id={"shard": lax.rem(self.k + 1, self.size)},
            device_id_type=MESH,
        )

    def local(self):
        return pltpu.make_async_copy(self.own, self.out.at[self.k], self.copy_sem)

    def step(self, step):
        if step == 0:
            self.local().start()
        if step == self.size - 1:
            self.local().wait()
        for way in (0, 1):
            if step > 0:
                valid, copy = self.received(way, step - 1)

                @pl.when(valid)
                def _():
                    copy.wait_recv()

            if step < self.size - 1:
                valid, copy = self.sent(way, step)

                @pl.when(valid)
                def _():
                    copy.start()

    def finish(self):
        for step in range(self.size - 1):
            for way in (0, 1):
                valid, copy = self.sent(way, step)

                @pl.when(valid)
                def _():
                    copy.wait_send()


class ShardExchange:
    def __init__(self, size, source, out, send_sem, recv_sem):
        self.size, self.source, self.out = size, source, out
        self.send_sem, self.recv_sem = send_sem, recv_sem
        self.k = lax.axis_index("shard")

    def copy(self, step):
        target = lax.rem(self.k + step, self.size)
        return pltpu.make_async_remote_copy(
            src_ref=self.source(target),
            dst_ref=self.out.at[self.k],
            send_sem=self.send_sem.at[step],
            recv_sem=self.recv_sem.at[step],
            device_id={"shard": target},
            device_id_type=MESH,
        )

    def arrival(self, step):
        return pltpu.make_async_remote_copy(
            src_ref=self.out.at[self.k],
            dst_ref=self.out.at[lax.rem(self.k + self.size - step, self.size)],
            send_sem=self.send_sem.at[step],
            recv_sem=self.recv_sem.at[step],
            device_id={"shard": lax.rem(self.k + step, self.size)},
            device_id_type=MESH,
        )

    def local(self):
        return pltpu.make_async_copy(
            self.source(self.k), self.out.at[self.k], self.send_sem.at[0]
        )

    def start(self):
        self.local().start()
        for step in range(1, self.size):
            self.copy(step).start()

    def wait_recv(self):
        self.local().wait()
        for step in range(1, self.size):
            self.arrival(step).wait_recv()

    def wait_send(self):
        for step in range(1, self.size):
            self.copy(step).wait_send()

    def wait(self):
        self.wait_recv()
        self.wait_send()


class PairReduce:
    def __init__(self, size, terms, first, middle_terms, second, sems):
        self.size, self.terms, self.first, self.second = size, terms, first, second
        self.middle_terms = middle_terms
        self.sems = sems
        self.k = lax.axis_index("shard")
        self.pairs = size // 2

    def swap(self, pair):
        target = 2 * pair + 1 - lax.rem(self.k, 2)
        return pltpu.make_async_remote_copy(
            src_ref=self.terms.at[target],
            dst_ref=self.first.at[pair],
            send_sem=self.sems.at[0, pair],
            recv_sem=self.sems.at[1, pair],
            device_id={"shard": jnp.bitwise_xor(self.k, 1)},
            device_id_type=MESH,
        )

    def cross(self, step):
        mine = self.k // 2
        pair = lax.rem(mine + step, self.pairs)
        target = 2 * pair + lax.rem(self.k, 2)
        return pair, target, pltpu.make_async_remote_copy(
            src_ref=self.middle_terms.at[step],
            dst_ref=self.second.at[step],
            send_sem=self.sems.at[2, step],
            recv_sem=self.sems.at[3, step],
            device_id={"shard": target},
            device_id_type=MESH,
        )

    def start(self):
        for pair in range(self.pairs):
            self.swap(pair).start()

    def middle(self):
        for pair in range(self.pairs):
            self.swap(pair).wait_recv()
        for step in range(1, self.pairs):
            pair, target, copy = self.cross(step)
            total = self.terms[target].astype(f32) + self.first[pair].astype(f32)
            self.middle_terms[step] = total.astype(bf16)
            copy.start()

    def total(self):
        for step in range(1, self.pairs):
            self.cross(step)[2].wait_recv()
        total = self.terms[self.k].astype(f32) + self.first[self.k // 2].astype(f32)
        for step in range(1, self.pairs):
            total = total + self.second[step].astype(f32)
        return total

    def finish(self):
        for pair in range(self.pairs):
            self.swap(pair).wait_send()
        for step in range(1, self.pairs):
            self.cross(step)[2].wait_send()


class PairSwap:
    def __init__(self, source, out, sems):
        mine = lax.axis_index("shard")
        self.copy = pltpu.make_async_remote_copy(
            src_ref=source,
            dst_ref=out,
            send_sem=sems.at[0],
            recv_sem=sems.at[1],
            device_id={"shard": jnp.bitwise_xor(mine, 1)},
            device_id_type=MESH,
        )


class Refs:
    def __init__(self, refs):
        self.refs = list(refs)

    def __call__(self, count):
        out, self.refs = self.refs[:count], self.refs[count:]
        return out


def inverse_rms(values):
    return lax.rsqrt(jnp.mean(values * values, axis=-1, keepdims=True) + epsilon)


def norm_back(values, inverse, gain, d_normed):
    scaled = d_normed * gain
    d_values = inverse * scaled - values * (inverse * inverse * inverse) * jnp.mean(
        scaled * values, axis=-1, keepdims=True
    )
    return d_values, jnp.sum(d_normed * values * inverse, axis=0, keepdims=True)


def head_lanes(head, shape):
    lane = lax.broadcasted_iota(jnp.int32, shape, 1)
    return lane < HD if head == 0 else lane >= HD


def turn(values, table, back):
    width = values.shape[1]
    cosine = jnp.concatenate([table[:, :HD]] * (width // HD), axis=1)
    sine = jnp.concatenate([table[:, HD:]] * (width // HD), axis=1)
    lane = lax.broadcasted_iota(jnp.int32, values.shape, 1)
    half = HD // 2
    partner = jnp.where(
        lane % HD < half,
        pltpu.roll(values, width - half, 1),
        pltpu.roll(values, half, 1),
    )
    if back:
        return values * cosine - partner * sine
    return values * cosine + partner * sine


def row_step(length, most):
    return most if length % most == 0 else length


def rows_at(index, step):
    return pl.ds(pl.multiple_of(index * step, step), step)


def weight_pieces(chunks):
    return [(c, kind) for c in range(chunks) for kind in ("gate", "up", "down")]


def piece_shape(kind, shards, part, block):
    return (shards, block, part) if kind == "down" else (shards, part, block)


def piece_source(kind, refs, chunk, block):
    ref = refs[kind]
    half = (ref.shape[0] if kind == "down" else ref.shape[1]) // 2

    def source(j):
        start = pl.multiple_of(lax.rem(j, 2) * half + chunk * block, block)
        if kind == "down":
            return ref.at[pl.ds(start, block), :]
        return ref.at[:, pl.ds(start, block)]

    return source


def split_masks(size):
    masks = chip_masks(size)[1:]
    return [m for m in masks if popcount(m) == 1], [m for m in masks if popcount(m) > 1]


def forward(x, gains, table, cot, attn_weights, mlp_weights, pieces, block):
    seq_size, shard_size = lax.axis_size("seq"), lax.axis_size("shard")
    rows, width = x.shape
    part, cols = attn_weights[0].shape
    length = rows * seq_size
    big = row_step(length, 512)
    query = row_step(length, 256 if length <= 2048 else 128)
    pair = 2 * HD
    scale = 1.0 / math.sqrt(HD)

    def kernel(*refs):
        take = Refs(refs)
        x_ref, gains_ref, table_ref, cot_ref = take(4)
        own_weights = take(4)
        mlp_refs = dict(zip(("gate", "up", "down"), take(3)))
        normed_all, table_all, gains_all = take(3)
        full_weights = take(4)
        q_ref, k_ref, v_ref, o_ref, lse_ref, hidden_ref = take(6)
        cot_all, cot_other, tok_all, tok_other = take(4)
        piece_refs = take(len(pieces))
        terms, arrived, ss, sr = take(4)
        normed_ref = take(1)[0]
        ns, nr, ts, tr, cs, cr, ds, dr, ms, mr = take(10)
        gs, gr, wo_s, wo_r, line_s, line_r, line_c, piece_s, piece_r, local_sem, swap_sem = take(11)

        me, mine = lax.axis_index("seq"), lax.axis_index("shard")
        entry_barrier(seq_neighbours(seq_size), shard_size)
        gain = ShardExchange(shard_size, lambda j: gains_ref, gains_all, gs, gr)
        gain.start()
        lines = [
            LineGather(shard_size, own, out, line_s.at[i], line_r.at[i], line_c.at[i])
            for i, (own, out) in enumerate(zip(own_weights[:3], full_weights))
        ]
        wq_all, wk_all, wv_all, wo_all = full_weights
        exchanges = [
            ShardExchange(
                shard_size, piece_source(kind, mlp_refs, c, block), out, piece_s.at[i], piece_r.at[i]
            )
            for i, ((c, kind), out) in enumerate(zip(pieces, piece_refs))
        ]
        mine_rows = rows_at(me, rows)
        own_cot = pltpu.make_async_copy(cot_ref, cot_all.at[mine_rows, :], local_sem.at[0])
        tables = SeqGather(seq_size, table_all, rows, ts, tr)
        normed = SeqGather(seq_size, normed_all, rows, ns, nr)
        cots = SeqGather(seq_size, cot_all, rows, cs, cr, own=cot_ref)
        cots_other = SeqGather(seq_size, cot_other, rows, ds, dr)
        swap_cot = PairSwap(cot_ref, cot_other.at[mine_rows, :], swap_sem.at[0]).copy
        wo_move = ShardExchange(shard_size, lambda j: own_weights[3], wo_all, wo_s, wo_r)
        if SWAP_FIRST:
            swap_cot.start()
        for line in lines:
            line.step(0)
        own_cot.start()
        table_all[mine_rows, :] = table_ref[...]
        tables.start()
        gain.wait_recv()
        values = x_ref[...].astype(f32)
        scaled = values * inverse_rms(values)
        for z in range(shard_size):
            lanes = slice(z * part, (z + 1) * part)
            normed_all[mine_rows, lanes] = (scaled[:, lanes] * gains_all[z, 0:1, :]).astype(bf16)
        normed.start()
        tables.forwards()
        for line in lines:
            line.step(1)
        near, far = split_masks(seq_size)
        for mask in near:
            normed.forward(mask)
        cots.start()
        for step in range(2, shard_size):
            for line in lines:
                line.step(step)
            if step == 2:
                wo_move.start()
                if not SWAP_FIRST:
                    swap_cot.start()
                for exchange in exchanges[:3]:
                    exchange.start()
                for mask in far:
                    normed.forward(mask)
        tables.finish()
        normed.finish()
        for mask in near:
            cots.forward(mask)
        if SWAP_FIRST:
            swap_cot.wait_recv()
            cots_other.start()

        wq, wk, wv = (w.reshape(width, cols) for w in (wq_all, wk_all, wv_all))

        @pl.loop(0, length // big)
        def _(i):
            r = rows_at(i, big)
            tokens = normed_all[r, :]
            tab = table_all[r, :]
            q = turn(dot_nn(tokens, wq[...]), tab, False).astype(bf16)
            q_ref[r, :] = q * jnp.asarray(scale, bf16)
            k_ref[r, :] = turn(dot_nn(tokens, wk[...]), tab, False).astype(bf16)
            v_ref[r, :] = dot_nn(tokens, wv[...]).astype(bf16)

        for mask in far:
            cots.forward(mask)

        @pl.loop(0, cols // pair)
        def _(hp):
            lanes = rows_at(hp, pair)
            for i in range(length // query):
                first, last = i * query, (i + 1) * query
                q2 = q_ref[first:last, lanes]
                out = None
                for head in (0, 1):
                    keep = head_lanes(head, q2.shape)
                    qm = jnp.where(keep, q2, jnp.zeros_like(q2))
                    s = dot_nt(qm, k_ref[:last, lanes])
                    r = lax.broadcasted_iota(jnp.int32, (query, query), 0)
                    c = lax.broadcasted_iota(jnp.int32, (query, query), 1)
                    tail = jnp.where(c <= r, s[:, first:], -1e30)
                    s = tail if i == 0 else jnp.concatenate([s[:, :first], tail], axis=1)
                    m = jnp.max(s, axis=1, keepdims=True)
                    p = jnp.exp(s - m)
                    total = jnp.sum(p, axis=1, keepdims=True)
                    low = (p * (1.0 / total)).astype(bf16)
                    o = dot_nn(low, v_ref[:last, lanes])
                    out = o if head == 0 else jnp.where(keep, o, out)
                    lse = jnp.transpose(jnp.broadcast_to(m + jnp.log(total), (query, 128)))
                    lse_ref[pl.ds(hp * 2 + head, 1), first:last] = lse[0:1, :]
                o_ref[first:last, lanes] = out.astype(bf16)

        for mask in near:
            if SWAP_FIRST:
                cots_other.forward(mask)
        wo_move.wait_recv()
        scatter = SeqScatter(seq_size, terms, arrived, ss, sr)

        def compute(mask):
            tokens = o_ref[scatter.tokens(mask), :]
            for z in range(shard_size):
                scatter.put(mask, slice(z * part, (z + 1) * part), dot_nn(tokens, wo_all[z]))

        scatter.run(compute, hidden_ref)
        for mask in far:
            if SWAP_FIRST:
                cots_other.forward(mask)
        hidden = hidden_ref[...] + x_ref[...].astype(f32)
        hidden_ref[...] = hidden
        scaled = hidden * inverse_rms(hidden)
        for z in range(shard_size):
            lanes = slice(z * part, (z + 1) * part)
            normed_ref[:, lanes] = (scaled[:, lanes] * gains_all[z, 1:2, :]).astype(bf16)
        swap_tok = PairSwap(normed_ref, tok_other, swap_sem.at[1]).copy
        swap_tok.start()
        toks = SeqGather(seq_size, tok_all, rows, ms, mr, own=normed_ref)
        toks.start()
        own_tok = pltpu.make_async_copy(normed_ref, tok_all.at[mine_rows, :], local_sem.at[1])
        own_tok.start()
        for exchange in exchanges[3:]:
            exchange.start()
        for mask in near:
            toks.forward(mask)
        if not SWAP_FIRST:
            swap_cot.wait_recv()
            cots_other.start()
        for mask in far:
            toks.forward(mask)
        if not SWAP_FIRST:
            cots_other.forwards()
        swap_cot.wait_send()
        wo_move.wait_send()
        gain.wait_send()
        scatter.finish()
        own_cot.wait()
        cots.finish()
        for line in lines:
            line.finish()
        swap_tok.wait()
        own_tok.wait()
        toks.finish()
        cots_other.finish()
        for exchange in exchanges:
            exchange.wait()

    weight = array((shard_size, part, cols))
    out_weight = array((shard_size, cols, part))
    heads = array((length, cols))
    tokens = array((length, width))
    shapes = [piece_shape(kind, shard_size, part, block) for _, kind in pieces]
    count = len(pieces)
    outs = pl.pallas_call(
        kernel,
        name="forward_attention",
        out_shape=[
            tokens,
            array((length, table.shape[1]), f32),
            array((shard_size,) + gains.shape, f32),
            weight,
            weight,
            weight,
            out_weight,
            heads,
            heads,
            heads,
            heads,
            array((max(8, cols // HD), length), f32),
            array((rows, width), f32),
            tokens,
            tokens,
            tokens,
            array((rows, width)),
        ]
        + [array(s) for s in shapes],
        in_specs=in_vmem(3) + in_any(1) + in_vmem(4) + in_any(3),
        out_specs=in_vmem(13) + in_any(4 + count),
        scratch_shapes=scatter_scratch(seq_size, rows, width)
        + [VMEM((rows, width), bf16)]
        + [DMA((seq_size,))] * 10
        + [DMA((shard_size,))] * 4
        + [DMA((3, 2, shard_size - 1))] * 2
        + [DMA((3,))]
        + [DMA((count, shard_size))] * 2
        + [DMA((2,)), DMA((2, 2))],
        compiler_params=kernel_params(1),
    )(x, gains, table, cot, *attn_weights, *mlp_weights)
    return outs[:17], list(outs[17:])


def mlp(tok, tok_other, cot, cot_other, pieces_in, mlp_weights, late, chunks, block, sums):
    seq_size, shard_size = lax.axis_size("seq"), lax.axis_size("shard")
    length, width = tok.shape
    rows = tok_other.shape[0]
    part = width // shard_size
    big = row_step(length, 512)
    steps = length // big
    pieces = weight_pieces(chunks)
    early = pieces[: len(pieces_in)]

    def kernel(*refs):
        take = Refs(refs)
        tok_ref, tok_swap = take(2)
        cots = take(2)
        early_refs = take(len(early))
        mlp_refs = dict(zip(("gate", "up", "down"), take(3)))
        act_ref, dg_ref, du_ref = take(3)
        grads = take(len(pieces))
        late_refs = take(len(late))
        sum_refs = take(sums)
        tok2, cot_rows, cot_cols, xt = take(4)
        weights = take(len(pieces))
        ts, tr, late_s, late_r, sum_s, sum_r, row_sem, col_sem, load_sem = take(9)

        me, mine = lax.axis_index("seq"), lax.axis_index("shard")
        entry_barrier(seq_neighbours(seq_size), shard_size)
        late_moves = [
            ShardExchange(
                shard_size, piece_source(kind, mlp_refs, c, block), out, late_s.at[i], late_r.at[i]
            )
            for i, ((c, kind), out) in enumerate(zip(late, late_refs))
        ]
        for move in late_moves:
            move.start()
        other = SeqGather(seq_size, tok2, rows, ts, tr, own=tok_swap)
        other.start()
        tok2[rows_at(me, rows), :] = tok_swap[...]
        everything = dict(zip(early, early_refs)) | dict(zip(late, late_refs))
        loads = [
            pltpu.make_async_copy(everything[p], w, load_sem.at[i])
            for i, (p, w) in enumerate(zip(pieces, weights))
        ]
        for load in loads[: len(early)]:
            load.start()
        held = dict(zip(pieces, weights))

        def row_copy(plane, i, slot):
            return pltpu.make_async_copy(
                cots[plane].at[rows_at(i, big), :], cot_rows.at[slot], row_sem.at[slot]
            )

        def stage(plane, these, base):
            token_ref = (tok_ref, tok2)[plane]

            @pl.loop(0, steps)
            def _(i):
                slot = lax.rem(i + base, 2)

                @pl.when(i + 1 < steps)
                def _():
                    row_copy(plane, i + 1, 1 - slot).start()

                tokens = token_ref[rows_at(i, big), :]
                row_copy(plane, i, slot).wait()
                r = pl.ds(pl.multiple_of(plane * length + i * big, big), big)
                for c in these:
                    gate_w, up_w = held[c, "gate"], held[c, "up"]
                    gate = dot_nn(tokens, gate_w.reshape(width, block)[...])
                    up = dot_nn(tokens, up_w.reshape(width, block)[...])
                    d_act = dot_nt(cot_rows[slot, :, :part], held[c, "down"][0])
                    for z in range(1, shard_size):
                        lanes = slice(z * part, (z + 1) * part)
                        d_act += dot_nt(cot_rows[slot, :, lanes], held[c, "down"][z])
                    sig = jax.nn.sigmoid(gate)
                    silu = gate * sig
                    act_ref[c, r, :] = (silu * up).astype(bf16)
                    slope = sig * (1.0 + gate * (1.0 - sig))
                    dg_ref[c, r, :] = (d_act * up * slope).astype(bf16)
                    du_ref[c, r, :] = (d_act * silu).astype(bf16)

        def col_copy(z, slot):
            lanes = slice(z * part, (z + 1) * part)
            return [
                pltpu.make_async_copy(
                    cots[plane].at[:, lanes],
                    cot_cols.at[slot, pl.ds(plane * length, length), :],
                    col_sem.at[slot, plane],
                )
                for plane in (0, 1)
            ]

        def grad(c):
            for source, where in ((act_ref, 2), (dg_ref, 0), (du_ref, 1)):
                xt[where] = jnp.transpose(source[c])
            for copy in col_copy(0, 0):
                copy.start()
            for z in range(shard_size):
                lanes = slice(z * part, (z + 1) * part)
                if z + 1 < shard_size:
                    for copy in col_copy(z + 1, (z + 1) % 2):
                        copy.start()
                for which in (0, 1):
                    total = dot_nn(xt[which, :, :length], tok_ref[:, lanes])
                    total += dot_nn(xt[which, :, length:], tok2[:, lanes])
                    grads[3 * c + which][z] = total.astype(bf16)
                for copy in col_copy(z, z % 2):
                    copy.wait()
                grads[3 * c + 2][z] = dot_nn(xt[2], cot_cols[z % 2]).astype(bf16)

        sum_moves = [
            ShardExchange(shard_size, lambda j, g=g: g.at[j], out, sum_s.at[i], sum_r.at[i])
            for i, (g, out) in enumerate(zip(grads, sum_refs))
        ]

        row_copy(0, 0, 0).start()
        first_chunks = [c for c in range(chunks) if all((c, k) in early for k in ("gate", "up", "down"))]
        later_chunks = [c for c in range(chunks) if c not in first_chunks]
        for load in loads[: len(early)]:
            load.wait()
        stage(0, first_chunks, 0)
        row_copy(1, 0, 0).start()
        other.forwards()
        other.finish()
        stage(1, first_chunks, 0)
        for c in first_chunks:
            grad(c)
            for move in sum_moves[3 * c : 3 * c + 3]:
                move.start()
        if later_chunks:
            row_copy(0, 0, 0).start()
            for move in late_moves:
                move.wait_recv()
            for load in loads[len(early) :]:
                load.start()
            for load in loads[len(early) :]:
                load.wait()
            stage(0, later_chunks, 0)
            row_copy(1, 0, 0).start()
            stage(1, later_chunks, 0)
            for c in later_chunks:
                grad(c)
                for move in sum_moves[3 * c : 3 * c + 3]:
                    move.start()
        for move in late_moves:
            move.wait_send()
        for move in sum_moves:
            move.wait()

    piece = array((shard_size, block, part))
    act = array((chunks, 2 * length, block))
    late_shapes = [piece_shape(kind, shard_size, part, block) for _, kind in late]
    all_shapes = [piece_shape(kind, shard_size, part, block) for _, kind in pieces]
    outs = pl.pallas_call(
        kernel,
        name="mlp",
        out_shape=[act] * 3
        + [piece] * len(pieces)
        + [array(s) for s in late_shapes]
        + [piece] * sums,
        in_specs=in_vmem(2) + in_any(2 + len(early) + 3),
        out_specs=in_vmem(3 + len(pieces)) + in_any(len(late) + sums),
        scratch_shapes=[
            VMEM((length, width), bf16),
            VMEM((2, big, width), bf16),
            VMEM((2, 2 * length, part), bf16),
            VMEM((3, block, 2 * length), bf16),
        ]
        + [VMEM(s, bf16) for s in all_shapes]
        + [DMA((seq_size,))] * 2
        + [DMA((max(1, len(late)), shard_size))] * 2
        + [DMA((max(1, sums), shard_size))] * 2
        + [DMA((2,)), DMA((2, 2)), DMA((len(pieces),))],
        compiler_params=kernel_params(2),
    )(tok, tok_other, cot, cot_other, *pieces_in, *mlp_weights)
    outs = list(outs)
    first = 3 + len(pieces)
    second = first + len(late)
    return outs[:3], outs[3:first], outs[first:second], outs[second:]


def mlp_back(d_gate, d_up, gate, up, hidden, cot, gains_all, grads):
    seq_size, shard_size = lax.axis_size("seq"), lax.axis_size("shard")
    rows, width = hidden.shape
    chunks = len(gate)
    length = rows * seq_size
    part = width // shard_size
    count = len(grads)
    shared = length > 2048

    def kernel(*refs):
        take = Refs(refs)
        dg_ref, du_ref, hidden_ref, cot_ref, gains_ref = take(5)
        gate_refs, up_refs = take(chunks), take(chunks)
        grad_refs = take(count)
        d_hidden_ref, d_gain_ref, d_attn_all = take(3)
        sum_refs = take(count)
        terms = take(1 if shared else 2)
        arrived = take(2)
        scatter_sems = [take(2), take(2)]
        other_ref, swap_ref, d_attn_ref = take(3)
        ns, nr, swap_sem, own_sem, sum_s, sum_r = take(6)

        me = lax.axis_index("seq")
        entry_barrier(seq_neighbours(seq_size), shard_size)
        moves = [
            ShardExchange(shard_size, lambda j, g=g: g.at[j], out, sum_s.at[i], sum_r.at[i])
            for i, (g, out) in enumerate(zip(grad_refs, sum_refs))
        ]
        for move in moves[:1]:
            move.start()
        swap = PairSwap(other_ref, swap_ref, swap_sem).copy
        scatters = [
            SeqScatter(seq_size, terms[0 if shared else i], arrived[i], *scatter_sems[i])
            for i in range(2)
        ]

        def term(plane):
            scatter = scatters[plane]

            def compute(mask):
                tokens = scatter.tokens(mask, plane * length)
                for z in range(shard_size):
                    total = None
                    for c in range(chunks):
                        both = dot_nt(dg_ref[c, tokens, :], gate_refs[c][z])
                        both += dot_nt(du_ref[c, tokens, :], up_refs[c][z])
                        total = both if total is None else total + both
                    scatter.put(mask, slice(z * part, (z + 1) * part), total)

            return compute

        here, there = scatters
        there.send_terms(term(1), merge=True)
        if shared:
            there.merge_inner()
            there.merge(other_ref)
            swap.start()
            there.finish()
            here.send_terms(term(0), merge=True)
        else:
            here.send_terms(term(0))
            there.merge_inner()
            here.merge_leaves()
            there.merge(other_ref)
            swap.start()
        for move in moves[1:]:
            move.start()
        here.merge_inner()
        here.merge(d_hidden_ref)
        swap.wait()
        d_normed = d_hidden_ref[...] + swap_ref[...].astype(f32)
        values = hidden_ref[...]
        gain = jnp.concatenate([gains_ref[z, 1:2, :] for z in range(shard_size)], axis=1)
        d_values, d_gain = norm_back(values, inverse_rms(values), gain, d_normed)
        d_hidden = cot_ref[...].astype(f32) + d_values
        d_attn_ref[...] = d_hidden.astype(bf16)
        gather = SeqGather(seq_size, d_attn_all, rows, ns, nr, own=d_attn_ref)
        gather.start()
        own = pltpu.make_async_copy(d_attn_ref, d_attn_all.at[rows_at(me, rows), :], own_sem)
        own.start()
        d_hidden_ref[...] = d_hidden
        d_gain_ref[...] = d_gain
        gather.forwards()
        own.wait()
        gather.finish()
        for scatter in scatters[: 1 if shared else 2]:
            scatter.finish()
        for move in moves:
            move.wait()

    scatter = scatter_scratch(seq_size, rows, width)
    outs = pl.pallas_call(
        kernel,
        name="mlp_back",
        out_shape=[
            array((rows, width), f32),
            array((1, width), f32),
            array((length, width)),
        ]
        + [array(g.shape) for g in grads],
        in_specs=in_vmem(5 + 2 * chunks) + in_any(count),
        out_specs=in_vmem(2) + in_any(1 + count),
        scratch_shapes=scatter[:1] * (1 if shared else 2)
        + scatter[1:2] * 2
        + [DMA((seq_size,))] * 4
        + [VMEM((rows, width), bf16)] * 3
        + [DMA((seq_size,))] * 2
        + [DMA((2,)), DMA]
        + [DMA((max(1, count), shard_size))] * 2,
        compiler_params=kernel_params(3),
    )(d_gate, d_up, hidden, cot, gains_all, *gate, *up, *grads)
    return outs[:3], list(outs[3:])


class OutputSum:
    def __init__(self, scatter, act, down_refs, base=0):
        self.scatter, self.act, self.down_refs, self.base = scatter, act, down_refs, base

    def compute(self, mask):
        tokens = self.scatter.tokens(mask, self.base)
        shards, _, part = self.down_refs[0].shape
        for z in range(shards):
            total = None
            for c, down in enumerate(self.down_refs):
                one = dot_nn(self.act[c, tokens, :], down[z])
                total = one if total is None else total + one
            self.scatter.put(mask, slice(z * part, (z + 1) * part), total)


def attend_back(d_attn, wo, mixed, q, k, v, lse, table, normed, grads, activ, down):
    seq_size, shard_size = lax.axis_size("seq"), lax.axis_size("shard")
    length, width = d_attn.shape
    rows = length // seq_size
    cols = q.shape[1]
    part = wo.shape[2]
    big = row_step(length, 512)
    block = row_step(length, 256)
    scale = 1.0 / math.sqrt(HD)
    pair = 2 * HD
    count = len(grads)
    chunks = len(down)

    def kernel(*refs):
        take = Refs(refs)
        da_ref, wo_ref, mixed_ref, q_ref, k_ref, v_ref, lse_ref, t_ref, n_ref = take(9)
        down_refs = take(chunks)
        grad_refs = take(count)
        act_all = take(1)[0] if chunks else None
        dq_ref, dk_ref, dv_ref, gq_ref, gk_ref, gv_ref = take(6)
        if chunks:
            swap_ref = take(1)[0]
        sum_refs = take(count + 1)
        do_ref, kt_ref, dk_acc, dv_acc, xt_ref, go_ref, sum_s, sum_r = take(8)

        if chunks:
            terms, arrived, ss, sr, act_ref, other_ref, act_sem, swap_sem = take(8)
            act_copy = pltpu.make_async_copy(
                act_all.at[:, pl.ds(length, length), :], act_ref, act_sem
            )
            act_copy.start()
        entry_barrier(seq_neighbours(seq_size) if chunks else [], shard_size)
        moves = [
            ShardExchange(shard_size, lambda j, g=g: g.at[j], out, sum_s.at[i], sum_r.at[i])
            for i, (g, out) in enumerate(zip(grad_refs + [go_ref], sum_refs))
        ]
        for move in moves[:-1]:
            move.start()
        if chunks:
            swap = PairSwap(other_ref, swap_ref, swap_sem).copy
            act_copy.wait()
            out_sum = OutputSum(SeqScatter(seq_size, terms, arrived, ss, sr), act_ref, down_refs)
            out_sum.scatter.send_terms(out_sum.compute, merge=True)

        xt_ref[...] = jnp.transpose(mixed_ref[...])
        for z in range(shard_size):
            go_ref[z] = dot_nn(xt_ref[...], da_ref[:, z * part : (z + 1) * part]).astype(bf16)
        if not chunks:
            moves[-1].start()

        @pl.loop(0, length // big)
        def _(i):
            r = rows_at(i, big)
            total = dot_nt(da_ref[r, :part], wo_ref[0])
            for z in range(1, shard_size):
                total += dot_nt(da_ref[r, z * part : (z + 1) * part], wo_ref[z])
            do_ref[r, :] = total.astype(bf16)

        kt_ref[...] = jnp.transpose(k_ref[...])
        if chunks:
            out_sum.scatter.merge_inner()

        def heads(hp, lanes):
            dk_acc[...] = jnp.zeros_like(dk_acc)
            dv_acc[...] = jnp.zeros_like(dv_acc)
            for i in range(length // block):
                first, last = i * block, (i + 1) * block
                q2 = q_ref[first:last, lanes]
                do2 = do_ref[first:last, lanes]
                keys = k_ref[:last, lanes]
                values = v_ref[:last, lanes]
                dqt, dk_add, dv_add = None, None, None
                for head in (0, 1):
                    keep = head_lanes(head, q2.shape)
                    qm = jnp.where(keep, q2, jnp.zeros_like(q2))
                    dom = jnp.where(keep, do2, jnp.zeros_like(do2))
                    st = dot_nt(keys, qm)
                    row = lse_ref[pl.ds(hp * 2 + head, 1), first:last]
                    p = jnp.exp(st - row)
                    r = lax.broadcasted_iota(jnp.int32, (block, block), 0)
                    c = lax.broadcasted_iota(jnp.int32, (block, block), 1)
                    tail = jnp.where(r <= c, p[first:], 0.0)
                    p = tail if i == 0 else jnp.concatenate([p[:first], tail], axis=0)
                    dp = dot_nt(values, dom)
                    inner = jnp.sum(dp * p, axis=0, keepdims=True)
                    ds = (p * (dp - inner)).astype(bf16)
                    dv_one = dot_nn(p.astype(bf16), dom)
                    dk_one = dot_nn(ds, qm)
                    dv_add = dv_one if head == 0 else dv_add + dv_one
                    dk_add = dk_one if head == 0 else dk_add + dk_one
                    dqt_one = dot_nn(kt_ref[lanes, :last], ds)
                    if head == 0:
                        dqt = dqt_one
                    else:
                        sub = lax.broadcasted_iota(jnp.int32, dqt.shape, 0)
                        dqt = jnp.where(sub < HD, dqt, dqt_one)
                dk_acc[:last, :] += dk_add
                dv_acc[:last, :] += dv_add
                dq = (jnp.transpose(dqt) * scale).astype(bf16).astype(f32)
                dq_ref[first:last, lanes] = turn(dq, t_ref[first:last, :], True).astype(bf16)
            dv_ref[:, lanes] = dv_acc[...].astype(bf16)

            @pl.loop(0, length // big)
            def _(i):
                r = rows_at(i, big)
                dk = dk_acc[r, :].astype(bf16).astype(f32)
                dk_ref[r, lanes] = turn(dk, t_ref[r, :], True).astype(bf16)

        if chunks:
            for hp in range(cols // pair):
                heads(hp, slice(hp * pair, (hp + 1) * pair))
                if hp == 0:
                    out_sum.scatter.merge(other_ref)
                    swap.start()
                    moves[-1].start()
        else:

            @pl.loop(0, cols // pair)
            def _(hp):
                heads(hp, rows_at(hp, pair))

        for source, out in ((dq_ref, gq_ref), (dk_ref, gk_ref), (dv_ref, gv_ref)):
            xt_ref[...] = jnp.transpose(source[...])
            for z in range(shard_size):
                out[z] = dot_nn(xt_ref[...], n_ref[:, z * part : (z + 1) * part]).astype(bf16)
        if chunks:
            swap.wait()
            out_sum.scatter.finish()
        for move in moves:
            move.wait()

    grad = array((shard_size, cols, part))
    scratch = [
        VMEM((length, cols), bf16),
        VMEM((cols, length), bf16),
        VMEM((length, pair), f32),
        VMEM((length, pair), f32),
        VMEM((cols, length), bf16),
        VMEM((shard_size, cols, part), bf16),
    ] + [DMA((count + 1, shard_size))] * 2
    if chunks:
        scratch += scatter_scratch(seq_size, rows, width)
        scratch += [VMEM((chunks, length, activ.shape[2]), bf16), VMEM((rows, width), bf16)]
        scratch += [DMA, DMA((2,))]
    outs = pl.pallas_call(
        kernel,
        name="attend_back",
        out_shape=[array((length, cols))] * 3
        + [grad] * 3
        + [array((rows, width))] * (1 if chunks else 0)
        + [array(g.shape) for g in grads]
        + [grad],
        in_specs=in_vmem(9 + chunks) + in_any(count + (1 if chunks else 0)),
        out_specs=in_vmem(7 if chunks else 6) + in_any(count + 1),
        scratch_shapes=scratch,
        compiler_params=kernel_params(4),
    )(d_attn, wo, mixed, q, k, v, lse, table, normed, *down, *grads, *([activ] if chunks else []))
    outs = list(outs)
    other = outs.pop(6) if chunks else None
    return outs[:3], outs[3:6], other, outs[6:]


def output_parts(activ, down, hidden):
    seq_size, shard_size = lax.axis_size("seq"), lax.axis_size("shard")
    rows, width = hidden.shape
    length = rows * seq_size
    chunks = len(down)

    def kernel(*refs):
        take = Refs(refs)
        act_ref, hidden_ref = take(2)
        down_refs = take(chunks)
        out_ref, terms, first, second = take(4)
        sems = [take(2), take(2)]
        total_ref, other_ref, swap_ref, swap_sem = take(4)
        entry_barrier(seq_neighbours(seq_size), shard_size)
        there, here = (
            OutputSum(SeqScatter(seq_size, terms, arrived, *sem), act_ref, down_refs, base)
            for arrived, sem, base in ((first, sems[0], length), (second, sems[1], 0))
        )
        there.scatter.run(there.compute, other_ref)
        swap = PairSwap(other_ref, swap_ref, swap_sem).copy
        swap.start()
        there.scatter.finish()
        here.scatter.run(here.compute, total_ref)
        swap.wait()
        out_ref[...] = (total_ref[...] + swap_ref[...].astype(f32) + hidden_ref[...]).astype(bf16)
        here.scatter.finish()

    scatter = scatter_scratch(seq_size, rows, width)
    return pl.pallas_call(
        kernel,
        name="output_parts",
        out_shape=array((rows, width)),
        in_specs=in_vmem(2 + chunks),
        out_specs=in_vmem(1)[0],
        scratch_shapes=scatter[:2]
        + scatter[1:2]
        + [DMA((seq_size,))] * 4
        + [VMEM((rows, width), f32), VMEM((rows, width), bf16), VMEM((rows, width), bf16)]
        + [DMA((2,))],
        compiler_params=kernel_params(6),
    )(activ, hidden, *down)


def finish(
    d_qkv, attn_weights, g_qkv, x, d_hidden, gains_all, d_gain_two, sums, g_output, block,
    output_of,
):
    seq_size, shard_size = lax.axis_size("seq"), lax.axis_size("shard")
    rows, width = x.shape
    part = width // shard_size
    cols = d_qkv[0].shape[1]
    length = rows * seq_size
    pieces = len(sums)
    half = pieces // 3 * block
    activ, down, hidden, other = output_of or (None, [], None, None)
    chunks = len(down)
    pairs = shard_size // 2

    def kernel(*refs):
        take = Refs(refs)
        x_ref, d_hidden_ref, gains_ref, gain2_ref = take(4)
        d_refs, w_refs, g_refs = take(3), take(3), take(3)
        down_refs = take(chunks)
        hidden_ref, other_ref = take(2) if chunks else (None, None)
        act_all = take(1)[0] if chunks else None
        sum_refs, go_ref = take(pieces), take(1)[0]
        d_inputs_ref, gain_ref = take(2)
        qkv_refs = take(3)
        output_ref = take(1)[0] if chunks else None
        wo_ref, wg_ref, wu_ref, wd_ref = take(4)
        total_ref, gain_mine, gain_shards, gain_line, gain_seq = take(5)
        gs, gr, hs, hr = take(4)
        in_terms, in_arrived, in_s, in_r = take(4)
        firsts, middles, seconds, reduce_sems = take(4)
        held, wide, tall, load_sem, store_sem = take(5)
        if chunks:
            out_terms, out_arrived, out_s, out_r, act_ref, act_sem, out_total = take(7)
            act_copy = pltpu.make_async_copy(act_all.at[:, pl.ds(0, length), :], act_ref, act_sem)
            act_copy.start()

        me = lax.axis_index("seq")
        entry_barrier(range(1, seq_size), shard_size)
        reduces = [
            PairReduce(
                shard_size, g_refs[i], firsts.at[i], middles.at[i], seconds.at[i], reduce_sems.at[i]
            )
            for i in range(3)
        ]
        for reduce in reduces:
            reduce.start()
        in_sum = SeqScatter(seq_size, in_terms, in_arrived, in_s, in_r)

        def inputs_term(mask):
            tokens = in_sum.tokens(mask)
            for z in range(shard_size):
                total = None
                for d_ref, w_ref in zip(d_refs, w_refs):
                    term = dot_nt(d_ref[tokens, :], w_ref[z])
                    total = term if total is None else total + term
                in_sum.put(mask, slice(z * part, (z + 1) * part), total)

        in_sum.send_terms(inputs_term, merge=True)
        if chunks:
            act_copy.wait()
            out_sum = OutputSum(
                SeqScatter(seq_size, out_terms, out_arrived, out_s, out_r), act_ref, down_refs
            )
            out_sum.scatter.send_terms(out_sum.compute)

        loads = [
            pltpu.make_async_copy(source, held.at[i % 2], load_sem.at[i % 2])
            for i, source in enumerate(sum_refs)
        ]
        stores = []

        def store(staging, target, value):
            turn_of = sum(1 for s in stores if s[0] is staging)
            slot = turn_of % 2
            sem = store_sem.at[0 if staging is wide else 1, slot]
            if turn_of >= 2:
                [s for s in stores if s[0] is staging][-2][1].wait()
            staging[slot] = value
            copy = pltpu.make_async_copy(staging.at[slot], target, sem)
            copy.start()
            stores.append((staging, copy))

        def collect(i):
            if i + 1 < pieces:
                loads[i + 1].start()
            loads[i].wait()
            for parity in (0, 1):
                total = held[i % 2, parity].astype(f32)
                for p in range(1, pairs):
                    total = total + held[i % 2, 2 * p + parity].astype(f32)
                start = parity * half + i // 3 * block
                if i % 3 == 2:
                    store(wide, wd_ref.at[start : start + block, :], total)
                else:
                    target = (wg_ref, wu_ref)[i % 3]
                    store(tall, target.at[:, start : start + block], jnp.transpose(total))

        loads[0].start()
        third = (pieces + 2) // 3
        in_sum.merge_inner()
        reduces[0].middle()
        if chunks:
            out_sum.scatter.merge_leaves()
        for i in range(third):
            collect(i)
        reduces[1].middle()
        in_sum.merge(total_ref)
        values = x_ref[...].astype(f32)
        gain = jnp.concatenate([gains_ref[z, 0:1, :] for z in range(shard_size)], axis=1)
        d_values, d_gain = norm_back(values, inverse_rms(values), gain, total_ref[...])
        d_inputs_ref[...] = (d_hidden_ref[...] + d_values).astype(bf16)
        for z in range(shard_size):
            lanes = slice(z * part, (z + 1) * part)
            gain_mine[z, 0:1, :] = d_gain[:, lanes]
            gain_mine[z, 1:2, :] = gain2_ref[0:1, lanes]
            gain_mine[z, 2:, :] = jnp.zeros((6, part), f32)
        line = ShardExchange(shard_size, lambda j: gain_mine.at[j], gain_shards, gs, gr)
        line.start()
        for i in range(third, 2 * third):
            collect(i)
        reduces[2].middle()
        if chunks:
            out_sum.scatter.merge_inner()
        line.wait()
        gain_line[...] = sum(gain_shards[z] for z in range(shard_size))

        def to_seq(step):
            return pltpu.make_async_remote_copy(
                src_ref=gain_line,
                dst_ref=gain_seq.at[step],
                send_sem=hs.at[step],
                recv_sem=hr.at[step],
                device_id={"seq": jnp.bitwise_xor(me, step)},
                device_id_type=MESH,
            )

        for step in range(1, seq_size):
            to_seq(step).start()
        for i in range(2 * third, pieces):
            collect(i)
        wo_ref[...] = sum(go_ref[z].astype(f32) for z in range(shard_size))
        if chunks:
            out_sum.scatter.merge(out_total)
            output_ref[...] = (
                out_total[...] + other_ref[...].astype(f32) + hidden_ref[...]
            ).astype(bf16)
        for reduce, out in zip(reduces, qkv_refs):
            out[...] = jnp.transpose(reduce.total())
        for step in range(1, seq_size):
            to_seq(step).wait()
        gain_ref[...] = gain_line[...] + sum(gain_seq[step] for step in range(1, seq_size))
        for staging in (wide, tall):
            for _, copy in [s for s in stores if s[0] is staging][-2:]:
                copy.wait()
        for reduce in reduces:
            reduce.finish()
        in_sum.finish()
        if chunks:
            out_sum.scatter.finish()

    scratch = [
        VMEM((rows, width), f32),
        VMEM((shard_size, 8, part), f32),
        VMEM((shard_size, 8, part), f32),
        VMEM((8, part), f32),
        VMEM((seq_size, 8, part), f32),
    ]
    scratch += [DMA((shard_size,))] * 2 + [DMA((seq_size,))] * 2
    scratch += scatter_scratch(seq_size, rows, width)
    scratch += [VMEM((3, pairs, cols, part), bf16)] * 3 + [DMA((3, 4, pairs))]
    scratch += [
        VMEM((2, shard_size, block, part), bf16),
        VMEM((2, block, part), f32),
        VMEM((2, part, block), f32),
        DMA((2,)),
        DMA((2, 2)),
    ]
    if chunks:
        scratch += scatter_scratch(seq_size, rows, width)
        scratch += [VMEM((chunks, length, block), bf16), DMA, VMEM((rows, width), f32)]
    extra = 1 if chunks else 0
    units = 2 * half
    outs = pl.pallas_call(
        kernel,
        name="finish",
        out_shape=[array((rows, width)), array((8, part), f32)]
        + [array((part, cols), f32)] * 3
        + [array((rows, width))] * extra
        + [array((cols, part), f32)]
        + [array((part, units), f32)] * 2
        + [array((units, part), f32)],
        in_specs=in_vmem(13 + chunks + 2 * extra) + in_any(extra + pieces) + in_vmem(1),
        out_specs=in_vmem(6 + extra) + in_any(3),
        scratch_shapes=scratch,
        compiler_params=kernel_params(5),
    )(
        x, d_hidden, gains_all, d_gain_two, *d_qkv, *attn_weights, *g_qkv, *down,
        *([hidden, other, activ] if chunks else []), *sums, g_output,
    )
    outs = list(outs)
    output = outs.pop(5) if chunks else None
    return outs, output


def rotation_table(position_ids):
    half = HD // 2
    freqs = theta_base ** (-(jnp.arange(half, dtype=f32) * 2.0) / HD)
    angles = position_ids.astype(f32)[:, None] * freqs[None, :]
    cosine, sine = jnp.cos(angles), jnp.sin(angles)
    return jnp.concatenate([cosine, cosine, -sine, sine], axis=1)


EARLY = 4
SUMS = (1, 4)
SWAP_FIRST = False


def body(
    inputs,
    positions,
    attn_gain,
    w_query,
    w_key,
    w_value,
    w_output,
    mlp_gain,
    w_gate,
    w_up,
    w_down,
    cotangent,
):
    shard_size = lax.axis_size("shard")
    x, cot = inputs[0], cotangent[0]
    gains = jnp.pad(jnp.stack([attn_gain, mlp_gain]).astype(f32), ((0, 6), (0, 0)))
    table = rotation_table(positions[0])
    half = w_gate.shape[1] // 2
    block = row_step(half, 256)
    chunks = half // block
    pieces = weight_pieces(chunks)
    early, late = pieces[:EARLY], pieces[EARLY:]
    mlp_weights = (w_gate, w_up, w_down)
    held, early_weights = forward(
        x, gains, table, cot, (w_query, w_key, w_value, w_output), mlp_weights, early, block
    )
    normed, tables, gains_all, wq, wk, wv, wo, q, k, v, mixed, lse, hidden = held[:13]
    cot_all, cot_other, tok, tok_other = held[13:]
    acts, grads, late_weights, sums = mlp(
        tok, tok_other, cot_all, cot_other, early_weights, mlp_weights, late, chunks, block,
        min(SUMS[0], len(pieces)),
    )
    activ, d_gate, d_up = acts
    weights = dict(zip(pieces, early_weights + late_weights))

    def kind(name):
        return [weights[c, name] for c in range(chunks)]

    done = len(sums)
    more = min(SUMS[1], len(pieces) - done)
    (d_hidden, d_gain_two, d_attn), moved = mlp_back(
        d_gate, d_up, kind("gate"), kind("up"), hidden, cot, gains_all, grads[done : done + more]
    )
    sums += moved
    done += more
    down = kind("down")
    together = tok.shape[0] <= 2048
    d_qkv, g_qkv, other, moved = attend_back(
        d_attn, wo, mixed, q, k, v, lse, tables, normed, grads[done:], activ,
        down if together else [],
    )
    sums += moved[:-1]
    results, output = finish(
        d_qkv, (wq, wk, wv), g_qkv, x, d_hidden, gains_all, d_gain_two, sums, moved[-1], block,
        (activ, down, hidden, other) if together else None,
    )
    if not together:
        output = output_parts(activ, down, hidden)
    d_inputs, gain_sums, g_query, g_key, g_value, g_output, g_gate, g_up, g_down = results
    return (
        output[None],
        d_inputs[None],
        gain_sums[0],
        g_query,
        g_key,
        g_value,
        g_output,
        gain_sums[1],
        g_gate,
        g_up,
        g_down,
    )


def solution(mesh):
    in_specs = (
        P("shard", "seq", None),
        P("shard", "seq"),
        P("shard"),
        P("shard", "seq"),
        P("shard", "seq"),
        P("shard", "seq"),
        P("seq", "shard"),
        P("shard"),
        P("shard", "seq"),
        P("shard", "seq"),
        P("seq", "shard"),
        P("shard", "seq", None),
    )
    out_specs = (
        P("shard", "seq", None),
        P("shard", "seq", None),
        P("shard"),
        P("shard", "seq"),
        P("shard", "seq"),
        P("shard", "seq"),
        P("seq", "shard"),
        P("shard"),
        P("shard", "seq"),
        P("shard", "seq"),
        P("seq", "shard"),
    )
    return jax.shard_map(body, mesh=mesh, in_specs=in_specs, out_specs=out_specs, check_vma=False)
```

```python
import math

import jax
import jax.numpy as jnp
from jax import lax
from jax.experimental import pallas as pl
from jax.experimental.pallas import tpu as pltpu
from jax.sharding import PartitionSpec as P

HD = 64
epsilon = 1e-05
theta_base = 130000.0
bf16 = jnp.bfloat16
f32 = jnp.float32
VMEM = pltpu.VMEM
DMA = pltpu.SemaphoreType.DMA
MESH = pl.DeviceIdType.MESH


def dot_nn(a, b):
    return jnp.dot(a, b, preferred_element_type=f32)


def dot_nt(a, b):
    return lax.dot_general(a, b, (((1,), (1,)), ((), ())), preferred_element_type=f32)


def in_vmem(count):
    return [pl.BlockSpec(memory_space=VMEM)] * count


def in_any(count):
    return [pl.BlockSpec(memory_space=pl.ANY)] * count


def array(shape, dtype=bf16):
    return jax.ShapeDtypeStruct(shape, dtype)


def kernel_params(collective_id=None, limit=62):
    if collective_id is None:
        return pltpu.CompilerParams(vmem_limit_bytes=limit << 20)
    return pltpu.CompilerParams(
        collective_id=collective_id, has_side_effects=True, vmem_limit_bytes=limit << 20
    )


def popcount(mask):
    return bin(mask).count("1")


def chip_masks(size):
    return sorted(range(0, size, 2), key=lambda m: (popcount(m), m))


def chip_bits(size):
    return [1 << b for b in range(1, size.bit_length() - 1)]


def last_hop(mask, core):
    set_bits = [1 << b for b in range(1, mask.bit_length()) if mask >> b & 1]
    return set_bits[-1] if core == 0 else set_bits[0]


def further_masks(mask, core, size):
    return [
        mask | hop
        for hop in chip_bits(size)
        if not mask & hop and last_hop(mask | hop, core) == hop
    ]


def seq_neighbours(size):
    return [1] + chip_bits(size)


def entry_barrier(seq_masks, shard_size):
    barrier = pltpu.get_barrier_semaphore()
    me, mine = lax.axis_index("seq"), lax.axis_index("shard")
    for mask in seq_masks:
        pl.semaphore_signal(
            barrier, inc=1, device_id={"seq": jnp.bitwise_xor(me, mask)}, device_id_type=MESH
        )
    for step in range(1, shard_size):
        pl.semaphore_signal(
            barrier, inc=1, device_id={"shard": lax.rem(mine + step, shard_size)},
            device_id_type=MESH,
        )
    pl.semaphore_wait(barrier, len(seq_masks) + max(shard_size - 1, 0))


class SeqGather:
    def __init__(self, size, out, rows, send_sem, recv_sem, own=None):
        self.size, self.out, self.rows = size, out, rows
        self.send_sem, self.recv_sem = send_sem, recv_sem
        self.me = lax.axis_index("seq")
        self.core = lax.rem(self.me, 2)
        self.own = own

    def block(self, index):
        return self.out.at[pl.ds(pl.multiple_of(index * self.rows, self.rows), self.rows), :]

    def copy(self, arrives, hop):
        block = self.block(jnp.bitwise_xor(self.me, arrives ^ hop))
        src = self.own if arrives == hop and self.own is not None else block
        return pltpu.make_async_remote_copy(
            src_ref=src,
            dst_ref=block,
            send_sem=self.send_sem.at[arrives],
            recv_sem=self.recv_sem.at[arrives],
            device_id={"seq": jnp.bitwise_xor(self.me, hop)},
            device_id_type=MESH,
        )

    def wait_recv(self, mask):
        block = self.block(jnp.bitwise_xor(self.me, mask))
        pltpu.make_async_remote_copy(
            src_ref=block,
            dst_ref=block,
            send_sem=self.send_sem.at[mask],
            recv_sem=self.recv_sem.at[mask],
            device_id={"seq": jnp.bitwise_xor(self.me, 1)},
            device_id_type=MESH,
        ).wait_recv()

    def start(self):
        for hop in reversed(seq_neighbours(self.size)):
            self.copy(hop, hop).start()

    def forward(self, mask):
        self.wait_recv(mask)
        for core in (0, 1):
            for more in further_masks(mask, core, self.size):

                @pl.when(self.core == core)
                def _():
                    self.copy(more, more ^ mask).start()

        self.copy(mask | 1, 1).start()

    def forwards(self):
        for mask in chip_masks(self.size)[1:]:
            self.forward(mask)

    def finish(self):
        for mask in chip_masks(self.size):
            self.wait_recv(mask | 1)
        for mask in range(1, self.size):
            self.copy(mask, 1 if mask & 1 else mask & -mask).wait_send()


def height(mask, core, size):
    return max([0] + [1 + height(m, core, size) for m in further_masks(mask, core, size)])


class SeqScatter:
    def __init__(self, size, terms, arrived, send_sem, recv_sem):
        self.size, self.terms, self.arrived = size, terms, arrived
        self.send_sem, self.recv_sem = send_sem, recv_sem
        self.me = lax.axis_index("seq")
        self.core = lax.rem(self.me, 2)
        self.masks = chip_masks(size)[::-1]
        self.order = [
            sorted(self.masks, key=lambda m: (height(m, core, size), -popcount(m)))
            for core in (0, 1)
        ]
        self.leaves = size // 4
        self.merged = 0

    def copy(self, mask, hop):
        core = 1 - self.core if mask & 1 else self.core
        return pltpu.make_async_remote_copy(
            src_ref=self.terms.at[mask // 2, core],
            dst_ref=self.arrived.at[mask - 1],
            send_sem=self.send_sem.at[mask],
            recv_sem=self.recv_sem.at[mask],
            device_id={"seq": jnp.bitwise_xor(self.me, hop)},
            device_id_type=MESH,
        )

    def tokens(self, mask, base=0):
        pair = 2 * self.terms.shape[2]
        start = jnp.bitwise_xor(self.me, mask) // 2 * pair + base
        return pl.ds(pl.multiple_of(start, pair), pair)

    def put(self, mask, lanes, total):
        rows = self.terms.shape[2]
        self.terms[mask // 2, :, :, lanes] = total.astype(bf16).reshape(2, rows, -1)

    def add(self, mask, source, write):
        rows = self.terms.shape[2]
        step = 32 if rows % 32 == 0 else 16

        @pl.loop(0, rows // step)
        def _(i):
            part = pl.ds(pl.multiple_of(i * step, step), step)
            total = self.terms[mask // 2, self.core, part, :].astype(f32)
            for s in source:
                total = total + self.arrived[s - 1, part, :].astype(f32)
            write(part, total)

    def merge(self, result=None):
        for core in (0, 1):
            mask = self.order[core][self.merged]
            further = further_masks(mask, core, self.size)

            def keep(part, total, mask=mask):
                if mask:
                    self.terms[mask // 2, self.core, part, :] = total.astype(bf16)
                else:
                    result[part, :] = total.astype(result.dtype)

            @pl.when(self.core == core)
            def _(mask=mask, further=further, keep=keep, core=core):
                for m in [mask | 1] + further:
                    self.copy(m, 1).wait_recv()
                self.add(mask, [mask | 1] + further, keep)
                if mask:
                    self.copy(mask, last_hop(mask, core)).start()

        self.merged += 1

    def send_terms(self, compute, merge=False):
        done = set()
        for mask in self.masks:
            compute(mask)
            self.copy(mask | 1, 1).start()
            if merge and self.merged < self.leaves:
                if all(order[self.merged] in done for order in self.order):
                    self.merge()
            done.add(mask)
        if merge:
            self.merge_leaves()

    def merge_leaves(self):
        while self.merged < self.leaves:
            self.merge()

    def merge_inner(self):
        while self.merged < len(self.masks) - 1:
            self.merge()

    def run(self, compute, result):
        self.send_terms(compute, merge=True)
        self.merge_inner()
        self.merge(result)

    def finish(self):
        for mask in range(1, self.size):
            self.copy(mask, 1).wait_send()


def scatter_scratch(seq_size, rows, width):
    return [
        VMEM((seq_size // 2, 2, rows, width), bf16),
        VMEM((seq_size - 1, rows, width), bf16),
        DMA((seq_size,)),
        DMA((seq_size,)),
    ]


class LineGather:
    def __init__(self, size, own, out, send_sem, recv_sem, copy_sem):
        self.size, self.own, self.out = size, own, out
        self.send_sem, self.recv_sem, self.copy_sem = send_sem, recv_sem, copy_sem
        self.k = lax.axis_index("shard")

    def sent(self, way, step):
        block = self.k - step if way == 0 else self.k + step
        valid = (
            jnp.logical_and(self.k < self.size - 1, block >= 0)
            if way == 0
            else jnp.logical_and(self.k > 0, block <= self.size - 1)
        )
        safe = jnp.clip(block, 0, self.size - 1)
        target = jnp.clip(self.k + 1 if way == 0 else self.k - 1, 0, self.size - 1)
        return valid, pltpu.make_async_remote_copy(
            src_ref=self.own if step == 0 else self.out.at[safe],
            dst_ref=self.out.at[safe],
            send_sem=self.send_sem.at[way, step],
            recv_sem=self.recv_sem.at[way, step],
            device_id={"shard": target},
            device_id_type=MESH,
        )

    def received(self, way, step):
        block = self.k - 1 - step if way == 0 else self.k + 1 + step
        valid = block >= 0 if way == 0 else block <= self.size - 1
        safe = jnp.clip(block, 0, self.size - 1)
        return valid, pltpu.make_async_remote_copy(
            src_ref=self.own,
            dst_ref=self.out.at[safe],
            send_sem=self.send_sem.at[way, step],
            recv_sem=self.recv_sem.at[way, step],
            device_id={"shard": lax.rem(self.k + 1, self.size)},
            device_id_type=MESH,
        )

    def local(self):
        return pltpu.make_async_copy(self.own, self.out.at[self.k], self.copy_sem)

    def step(self, step):
        if step == 0:
            self.local().start()
        if step == self.size - 1:
            self.local().wait()
        for way in (0, 1):
            if step > 0:
                valid, copy = self.received(way, step - 1)

                @pl.when(valid)
                def _():
                    copy.wait_recv()

            if step < self.size - 1:
                valid, copy = self.sent(way, step)

                @pl.when(valid)
                def _():
                    copy.start()

    def finish(self):
        for step in range(self.size - 1):
            for way in (0, 1):
                valid, copy = self.sent(way, step)

                @pl.when(valid)
                def _():
                    copy.wait_send()


class ShardExchange:
    def __init__(self, size, source, out, send_sem, recv_sem):
        self.size, self.source, self.out = size, source, out
        self.send_sem, self.recv_sem = send_sem, recv_sem
        self.k = lax.axis_index("shard")

    def copy(self, step):
        target = lax.rem(self.k + step, self.size)
        return pltpu.make_async_remote_copy(
            src_ref=self.source(target),
            dst_ref=self.out.at[self.k],
            send_sem=self.send_sem.at[step],
            recv_sem=self.recv_sem.at[step],
            device_id={"shard": target},
            device_id_type=MESH,
        )

    def arrival(self, step):
        return pltpu.make_async_remote_copy(
            src_ref=self.out.at[self.k],
            dst_ref=self.out.at[lax.rem(self.k + self.size - step, self.size)],
            send_sem=self.send_sem.at[step],
            recv_sem=self.recv_sem.at[step],
            device_id={"shard": lax.rem(self.k + step, self.size)},
            device_id_type=MESH,
        )

    def local(self):
        return pltpu.make_async_copy(
            self.source(self.k), self.out.at[self.k], self.send_sem.at[0]
        )

    def inner(self, step):
        target = lax.rem(self.k + step, self.size)
        beside = jnp.abs(target - self.k) == 1
        return jnp.logical_and(beside, target // 2 != self.k // 2)

    def start_inner(self):
        for step in (1, self.size - 1):

            @pl.when(self.inner(step))
            def _():
                self.copy(step).start()

    def start_outer(self):
        self.local().start()
        for step in range(1, self.size):

            @pl.when(jnp.logical_not(self.inner(step)))
            def _():
                self.copy(step).start()

    def start(self):
        self.local().start()
        for step in range(1, self.size):
            self.copy(step).start()

    def wait_recv(self):
        self.local().wait()
        for step in range(1, self.size):
            self.arrival(step).wait_recv()

    def wait_send(self):
        for step in range(1, self.size):
            self.copy(step).wait_send()

    def wait(self):
        self.wait_recv()
        self.wait_send()


class PairReduce:
    def __init__(self, size, terms, first, middle_terms, second, sems):
        self.size, self.terms, self.first, self.second = size, terms, first, second
        self.middle_terms = middle_terms
        self.sems = sems
        self.k = lax.axis_index("shard")
        self.pairs = size // 2

    def swap(self, pair):
        target = 2 * pair + 1 - lax.rem(self.k, 2)
        return pltpu.make_async_remote_copy(
            src_ref=self.terms.at[target],
            dst_ref=self.first.at[pair],
            send_sem=self.sems.at[0, pair],
            recv_sem=self.sems.at[1, pair],
            device_id={"shard": jnp.bitwise_xor(self.k, 1)},
            device_id_type=MESH,
        )

    def cross(self, step):
        mine = self.k // 2
        pair = lax.rem(mine + step, self.pairs)
        target = 2 * pair + lax.rem(self.k, 2)
        return pair, target, pltpu.make_async_remote_copy(
            src_ref=self.middle_terms.at[step],
            dst_ref=self.second.at[step],
            send_sem=self.sems.at[2, step],
            recv_sem=self.sems.at[3, step],
            device_id={"shard": target},
            device_id_type=MESH,
        )

    def start(self):
        for pair in range(self.pairs):
            self.swap(pair).start()

    def middle(self):
        for pair in range(self.pairs):
            self.swap(pair).wait_recv()
        for step in range(1, self.pairs):
            pair, target, copy = self.cross(step)
            total = self.terms[target].astype(f32) + self.first[pair].astype(f32)
            self.middle_terms[step] = total.astype(bf16)
            copy.start()

    def total(self):
        for step in range(1, self.pairs):
            self.cross(step)[2].wait_recv()
        total = self.terms[self.k].astype(f32) + self.first[self.k // 2].astype(f32)
        for step in range(1, self.pairs):
            total = total + self.second[step].astype(f32)
        return total

    def finish(self):
        for pair in range(self.pairs):
            self.swap(pair).wait_send()
        for step in range(1, self.pairs):
            self.cross(step)[2].wait_send()


class PairSwap:
    def __init__(self, source, out, sems):
        mine = lax.axis_index("shard")
        self.copy = pltpu.make_async_remote_copy(
            src_ref=source,
            dst_ref=out,
            send_sem=sems.at[0],
            recv_sem=sems.at[1],
            device_id={"shard": jnp.bitwise_xor(mine, 1)},
            device_id_type=MESH,
        )


class Moves:
    def __init__(self, sems):
        self.sems, self.copies = sems, []

    def start(self, source, target):
        copy = pltpu.make_async_copy(source, target, self.sems.at[len(self.copies)])
        copy.start()
        self.copies.append(copy)
        return copy

    def wait(self, count=None):
        count = len(self.copies) if count is None else count
        for copy in [c for c in self.copies if c is not None][:count]:
            copy.wait()
        left = [i for i, c in enumerate(self.copies) if c is not None][:count]
        for i in left:
            self.copies[i] = None


def held(arrays):
    return [VMEM(a.shape, a.dtype) for a in arrays]


class Refs:
    def __init__(self, refs):
        self.refs = list(refs)

    def __call__(self, count):
        out, self.refs = self.refs[:count], self.refs[count:]
        return out


def inverse_rms(values):
    return lax.rsqrt(jnp.mean(values * values, axis=-1, keepdims=True) + epsilon)


def norm_back(values, inverse, gain, d_normed):
    scaled = d_normed * gain
    d_values = inverse * scaled - values * (inverse * inverse * inverse) * jnp.mean(
        scaled * values, axis=-1, keepdims=True
    )
    return d_values, jnp.sum(d_normed * values * inverse, axis=0, keepdims=True)


def head_lanes(head, shape):
    lane = lax.broadcasted_iota(jnp.int32, shape, 1)
    return lane < HD if head == 0 else lane >= HD


def turn(values, table, back):
    width = values.shape[1]
    cosine = jnp.concatenate([table[:, :HD]] * (width // HD), axis=1)
    sine = jnp.concatenate([table[:, HD:]] * (width // HD), axis=1)
    lane = lax.broadcasted_iota(jnp.int32, values.shape, 1)
    half = HD // 2
    partner = jnp.where(
        lane % HD < half,
        pltpu.roll(values, width - half, 1),
        pltpu.roll(values, half, 1),
    )
    if back:
        return values * cosine - partner * sine
    return values * cosine + partner * sine


def row_step(length, most):
    return most if length % most == 0 else length


def rows_at(index, step):
    return pl.ds(pl.multiple_of(index * step, step), step)


def weight_pieces(chunks):
    return [(c, kind) for c in range(chunks) for kind in ("gate", "up", "down")]


def piece_shape(kind, shards, part, block):
    return (shards, block, part) if kind == "down" else (shards, part, block)


def piece_source(kind, refs, chunk, block):
    ref = refs[kind]
    half = (ref.shape[0] if kind == "down" else ref.shape[1]) // 2

    def source(j):
        start = pl.multiple_of(lax.rem(j, 2) * half + chunk * block, block)
        if kind == "down":
            return ref.at[pl.ds(start, block), :]
        return ref.at[:, pl.ds(start, block)]

    return source


def split_masks(size):
    masks = chip_masks(size)[1:]
    return [m for m in masks if popcount(m) == 1], [m for m in masks if popcount(m) > 1]


def forward(x, gains, table, cot, attn_weights, mlp_weights, pieces, block):
    seq_size, shard_size = lax.axis_size("seq"), lax.axis_size("shard")
    rows, width = x.shape
    part, cols = attn_weights[0].shape
    length = rows * seq_size
    big = row_step(length, 512)
    query = row_step(length, 256 if length <= 2048 else 128)
    pair = 2 * HD
    scale = 1.0 / math.sqrt(HD)

    def kernel(*refs):
        take = Refs(refs)
        x_ref, gains_ref, table_ref, cot_ref = take(4)
        own_weights = take(4)
        mlp_refs = dict(zip(("gate", "up", "down"), take(3)))
        normed_out, table_all, gains_all = take(3)
        weights_out = take(4)
        heads_out = take(4)
        lse_ref, hidden_ref = take(2)
        cot_all, cot_other, tok_all, tok_other = take(4)
        piece_refs = take(len(pieces))
        terms, arrived, ss, sr = take(4)
        normed_ref, normed_all = take(2)
        full_weights, heads_held = take(4), take(4)
        q_ref, k_ref, v_ref, o_ref = heads_held
        out_sems = take(1)[0]
        ns, nr, ts, tr, cs, cr, ds, dr, ms, mr = take(10)
        gs, gr, line_s, line_r, line_c, piece_s, piece_r, local_sem, swap_sem = take(9)

        me, mine = lax.axis_index("seq"), lax.axis_index("shard")
        entry_barrier(seq_neighbours(seq_size), shard_size)
        gain = ShardExchange(shard_size, lambda j: gains_ref, gains_all, gs, gr)
        gain.start()
        lines = [
            LineGather(shard_size, own, out, line_s.at[i], line_r.at[i], line_c.at[i])
            for i, (own, out) in enumerate(zip(own_weights, full_weights))
        ]
        wq_all, wk_all, wv_all, wo_all = full_weights
        exchanges = [
            ShardExchange(
                shard_size, piece_source(kind, mlp_refs, c, block), out, piece_s.at[i], piece_r.at[i]
            )
            for i, ((c, kind), out) in enumerate(zip(pieces, piece_refs))
        ]
        mine_rows = rows_at(me, rows)
        own_cot = pltpu.make_async_copy(cot_ref, cot_all.at[mine_rows, :], local_sem.at[0])
        tables = SeqGather(seq_size, table_all, rows, ts, tr)
        normed = SeqGather(seq_size, normed_all, rows, ns, nr)
        cots = SeqGather(seq_size, cot_all, rows, cs, cr, own=cot_ref)
        cots_other = SeqGather(seq_size, cot_other, rows, ds, dr)
        swap_cot = PairSwap(cot_ref, cot_other.at[mine_rows, :], swap_sem.at[0]).copy
        for line in lines[:3]:
            line.step(0)
        own_cot.start()
        table_all[mine_rows, :] = table_ref[...]
        tables.start()
        gain.wait_recv()
        values = x_ref[...].astype(f32)
        scaled = values * inverse_rms(values)
        for z in range(shard_size):
            lanes = slice(z * part, (z + 1) * part)
            normed_all[mine_rows, lanes] = (scaled[:, lanes] * gains_all[z, 0:1, :]).astype(bf16)
        normed.start()
        tables.forwards()
        for line in lines[:3]:
            line.step(1)
        for exchange in exchanges:
            exchange.start_inner()
        near, far = split_masks(seq_size)
        for mask in near:
            normed.forward(mask)
        cots.start()
        for step in range(2, shard_size):
            for line in lines[:3]:
                line.step(step)
            if step == 2:
                swap_cot.start()
                lines[3].step(0)
                for mask in far:
                    normed.forward(mask)
        tables.finish()
        normed.finish()
        outs = Moves(out_sems)
        outs.start(normed_all, normed_out)
        for held_weight, out in list(zip(full_weights, weights_out))[:3]:
            outs.start(held_weight, out)
        for mask in near:
            cots.forward(mask)
        lines[3].step(1)

        def start_pieces(point):
            if point == START:
                for exchange in exchanges[:AHEAD]:
                    exchange.start_outer()

        start_pieces(0)

        wq, wk, wv = (w.reshape(width, cols) for w in (wq_all, wk_all, wv_all))

        @pl.loop(0, length // big)
        def _(i):
            r = rows_at(i, big)
            tokens = normed_all[r, :]
            tab = table_all[r, :]
            q = turn(dot_nn(tokens, wq[...]), tab, False).astype(bf16)
            q_ref[r, :] = q * jnp.asarray(scale, bf16)
            k_ref[r, :] = turn(dot_nn(tokens, wk[...]), tab, False).astype(bf16)
            v_ref[r, :] = dot_nn(tokens, wv[...]).astype(bf16)

        for mask in far:
            cots.forward(mask)
        start_pieces(1)
        for step in range(2, shard_size - 1):
            lines[3].step(step)

        def attend(hp, lanes):
            for i in range(length // query):
                first, last = i * query, (i + 1) * query
                q2 = q_ref[first:last, lanes]
                out = None
                for head in (0, 1):
                    keep = head_lanes(head, q2.shape)
                    qm = jnp.where(keep, q2, jnp.zeros_like(q2))
                    s = dot_nt(qm, k_ref[:last, lanes])
                    r = lax.broadcasted_iota(jnp.int32, (query, query), 0)
                    c = lax.broadcasted_iota(jnp.int32, (query, query), 1)
                    tail = jnp.where(c <= r, s[:, first:], -1e30)
                    s = tail if i == 0 else jnp.concatenate([s[:, :first], tail], axis=1)
                    m = jnp.max(s, axis=1, keepdims=True)
                    p = jnp.exp(s - m)
                    total = jnp.sum(p, axis=1, keepdims=True)
                    low = (p * (1.0 / total)).astype(bf16)
                    o = dot_nn(low, v_ref[:last, lanes])
                    out = o if head == 0 else jnp.where(keep, o, out)
                    lse = jnp.transpose(jnp.broadcast_to(m + jnp.log(total), (query, 128)))
                    lse_ref[pl.ds(hp * 2 + head, 1), first:last] = lse[0:1, :]
                o_ref[first:last, lanes] = out.astype(bf16)

        if cols == 2 * pair:
            attend(0, slice(0, pair))
            swap_cot.wait_recv()
            cots_other.start()
            start_pieces(2)
            attend(1, slice(pair, cols))
        else:

            @pl.loop(0, cols // pair)
            def _(hp):
                attend(hp, rows_at(hp, pair))

            swap_cot.wait_recv()
            cots_other.start()
            start_pieces(2)
        lines[3].step(shard_size - 1)
        start_pieces(3)
        outs.start(full_weights[3], weights_out[3])
        for held_heads, out in zip(heads_held, heads_out):
            outs.start(held_heads, out)
        scatter = SeqScatter(seq_size, terms, arrived, ss, sr)

        def compute(mask):
            tokens = o_ref[scatter.tokens(mask), :]
            for z in range(shard_size):
                scatter.put(mask, slice(z * part, (z + 1) * part), dot_nn(tokens, wo_all[z]))

        scatter.send_terms(compute, merge=True)
        for mask in near:
            cots_other.forward(mask)
        scatter.merge_inner()
        scatter.merge(hidden_ref)
        for mask in far:
            cots_other.forward(mask)
        hidden = hidden_ref[...] + x_ref[...].astype(f32)
        hidden_ref[...] = hidden
        scaled = hidden * inverse_rms(hidden)
        for z in range(shard_size):
            lanes = slice(z * part, (z + 1) * part)
            normed_ref[:, lanes] = (scaled[:, lanes] * gains_all[z, 1:2, :]).astype(bf16)
        swap_tok = PairSwap(normed_ref, tok_other, swap_sem.at[1]).copy
        swap_tok.start()
        toks = SeqGather(seq_size, tok_all, rows, ms, mr, own=normed_ref)
        toks.start()
        own_tok = pltpu.make_async_copy(normed_ref, tok_all.at[mine_rows, :], local_sem.at[1])
        own_tok.start()
        for exchange in exchanges[AHEAD:]:
            exchange.start_outer()
        for mask in near:
            toks.forward(mask)
        for mask in far:
            toks.forward(mask)
        swap_cot.wait_send()
        gain.wait_send()
        scatter.finish()
        own_cot.wait()
        cots.finish()
        for line in lines:
            line.finish()
        swap_tok.wait()
        own_tok.wait()
        toks.finish()
        cots_other.finish()
        for exchange in exchanges:
            exchange.wait()
        outs.wait()

    weight = array((shard_size, part, cols))
    out_weight = array((shard_size, cols, part))
    heads = array((length, cols))
    tokens = array((length, width))
    shapes = [piece_shape(kind, shard_size, part, block) for _, kind in pieces]
    count = len(pieces)
    outs = pl.pallas_call(
        kernel,
        name="forward_attention",
        out_shape=[
            tokens,
            array((length, table.shape[1]), f32),
            array((shard_size,) + gains.shape, f32),
            weight,
            weight,
            weight,
            out_weight,
            heads,
            heads,
            heads,
            heads,
            array((max(8, cols // HD), length), f32),
            array((rows, width), f32),
            tokens,
            tokens,
            tokens,
            array((rows, width)),
        ]
        + [array(s) for s in shapes],
        in_specs=in_vmem(3) + in_any(1) + in_vmem(4) + in_any(3),
        out_specs=in_any(1) + in_vmem(2) + in_any(8) + in_vmem(2) + in_any(4 + count),
        scratch_shapes=scatter_scratch(seq_size, rows, width)
        + [VMEM((rows, width), bf16), VMEM((length, width), bf16)]
        + held([weight] * 3 + [out_weight] + [heads] * 4)
        + [DMA((9,))]
        + [DMA((seq_size,))] * 10
        + [DMA((shard_size,))] * 2
        + [DMA((4, 2, shard_size - 1))] * 2
        + [DMA((4,))]
        + [DMA((count, shard_size))] * 2
        + [DMA((2,)), DMA((2, 2))],
        compiler_params=kernel_params(1),
    )(x, gains, table, cot, *attn_weights, *mlp_weights)
    return outs[:17], list(outs[17:])


def mlp(tok, tok_other, cot, cot_other, pieces_in, mlp_weights, late, chunks, block, sums):
    seq_size, shard_size = lax.axis_size("seq"), lax.axis_size("shard")
    length, width = tok.shape
    rows = tok_other.shape[0]
    part = width // shard_size
    big = row_step(length, 512)
    steps = length // big
    pieces = weight_pieces(chunks)
    early = pieces[: len(pieces_in)]

    def kernel(*refs):
        take = Refs(refs)
        tok_swap, tok_hbm = take(2)
        cots = take(2)
        early_refs = take(len(early))
        mlp_refs = dict(zip(("gate", "up", "down"), take(3)))
        acts_out = take(3)
        grads_out = take(len(pieces))
        late_refs = take(len(late))
        sum_refs = take(sums)
        tok2, cot_rows, cot_cols, xt = take(4)
        weights = take(len(pieces))
        act_ref, dg_ref, du_ref = take(3)
        grads = take(len(pieces))
        tok_ref, tok_sem, out_sems = take(3)
        tok_copy = pltpu.make_async_copy(tok_hbm, tok_ref, tok_sem)
        tok_copy.start()
        outs = Moves(out_sems)
        ts, tr, late_s, late_r, sum_s, sum_r, row_sem, col_sem, load_sem = take(9)

        me, mine = lax.axis_index("seq"), lax.axis_index("shard")
        entry_barrier(seq_neighbours(seq_size), shard_size)
        late_moves = [
            ShardExchange(
                shard_size, piece_source(kind, mlp_refs, c, block), out, late_s.at[i], late_r.at[i]
            )
            for i, ((c, kind), out) in enumerate(zip(late, late_refs))
        ]
        for move in late_moves:
            move.start()
        other = SeqGather(seq_size, tok2, rows, ts, tr, own=tok_swap)
        other.start()
        tok2[rows_at(me, rows), :] = tok_swap[...]
        everything = dict(zip(early, early_refs)) | dict(zip(late, late_refs))
        loads = [
            pltpu.make_async_copy(everything[p], w, load_sem.at[i])
            for i, (p, w) in enumerate(zip(pieces, weights))
        ]
        for load in loads[: len(early)]:
            load.start()
        held = dict(zip(pieces, weights))

        def row_copy(plane, i, slot):
            return pltpu.make_async_copy(
                cots[plane].at[rows_at(i, big), :], cot_rows.at[slot], row_sem.at[slot]
            )

        def stage(plane, these, base):
            token_ref = (tok_ref, tok2)[plane]

            @pl.loop(0, steps)
            def _(i):
                slot = lax.rem(i + base, 2)

                @pl.when(i + 1 < steps)
                def _():
                    row_copy(plane, i + 1, 1 - slot).start()

                tokens = token_ref[rows_at(i, big), :]
                row_copy(plane, i, slot).wait()
                r = pl.ds(pl.multiple_of(plane * length + i * big, big), big)
                for c in these:
                    gate_w, up_w = held[c, "gate"], held[c, "up"]
                    gate = dot_nn(tokens, gate_w.reshape(width, block)[...])
                    up = dot_nn(tokens, up_w.reshape(width, block)[...])
                    d_act = dot_nt(cot_rows[slot, :, :part], held[c, "down"][0])
                    for z in range(1, shard_size):
                        lanes = slice(z * part, (z + 1) * part)
                        d_act += dot_nt(cot_rows[slot, :, lanes], held[c, "down"][z])
                    sig = jax.nn.sigmoid(gate)
                    silu = gate * sig
                    act_ref[c, r, :] = (silu * up).astype(bf16)
                    slope = sig * (1.0 + gate * (1.0 - sig))
                    dg_ref[c, r, :] = (d_act * up * slope).astype(bf16)
                    du_ref[c, r, :] = (d_act * silu).astype(bf16)

        def col_copy(z, slot):
            lanes = slice(z * part, (z + 1) * part)
            return [
                pltpu.make_async_copy(
                    cots[plane].at[:, lanes],
                    cot_cols.at[slot, pl.ds(plane * length, length), :],
                    col_sem.at[slot, plane],
                )
                for plane in (0, 1)
            ]

        def grad(c):
            for source, where in ((act_ref, 2), (dg_ref, 0), (du_ref, 1)):
                xt[where] = jnp.transpose(source[c])
            for copy in col_copy(0, 0):
                copy.start()
            for z in range(shard_size):
                lanes = slice(z * part, (z + 1) * part)
                if z + 1 < shard_size:
                    for copy in col_copy(z + 1, (z + 1) % 2):
                        copy.start()
                for which in (0, 1):
                    total = dot_nn(xt[which, :, :length], tok_ref[:, lanes])
                    total += dot_nn(xt[which, :, length:], tok2[:, lanes])
                    grads[3 * c + which][z] = total.astype(bf16)
                for copy in col_copy(z, z % 2):
                    copy.wait()
                grads[3 * c + 2][z] = dot_nn(xt[2], cot_cols[z % 2]).astype(bf16)

        def put_acts(these):
            for c in these:
                for ref, out in zip((act_ref, dg_ref, du_ref), acts_out):
                    outs.start(ref.at[c], out.at[c])

        def put_grads(c):
            for i in range(max(sums, 3 * c), 3 * c + 3):
                outs.start(grads[i], grads_out[i])

        sum_moves = [
            ShardExchange(shard_size, lambda j, g=g: g.at[j], out, sum_s.at[i], sum_r.at[i])
            for i, (g, out) in enumerate(zip(grads, sum_refs))
        ]

        row_copy(0, 0, 0).start()
        first_chunks = [c for c in range(chunks) if all((c, k) in early for k in ("gate", "up", "down"))]
        later_chunks = [c for c in range(chunks) if c not in first_chunks]
        for load in loads[: len(early)]:
            load.wait()
        tok_copy.wait()
        stage(0, first_chunks, 0)
        row_copy(1, 0, 0).start()
        other.forwards()
        other.finish()
        stage(1, first_chunks, 0)
        put_acts(first_chunks)
        for c in first_chunks:
            grad(c)
            put_grads(c)
            for move in sum_moves[3 * c : 3 * c + 3]:
                move.start()
        if later_chunks:
            row_copy(0, 0, 0).start()
            for move in late_moves:
                move.wait_recv()
            for load in loads[len(early) :]:
                load.start()
            for load in loads[len(early) :]:
                load.wait()
            stage(0, later_chunks, 0)
            row_copy(1, 0, 0).start()
            stage(1, later_chunks, 0)
            put_acts(later_chunks)
            for c in later_chunks:
                grad(c)
                put_grads(c)
                for move in sum_moves[3 * c : 3 * c + 3]:
                    move.start()
        for move in late_moves:
            move.wait_send()
        for move in sum_moves:
            move.wait()
        outs.wait()

    piece = array((shard_size, block, part))
    act = array((chunks, 2 * length, block))
    late_shapes = [piece_shape(kind, shard_size, part, block) for _, kind in late]
    all_shapes = [piece_shape(kind, shard_size, part, block) for _, kind in pieces]
    outs = pl.pallas_call(
        kernel,
        name="mlp",
        out_shape=[act] * 3
        + [piece] * len(pieces)
        + [array(s) for s in late_shapes]
        + [piece] * sums,
        in_specs=in_vmem(1) + in_any(3 + len(early) + 3),
        out_specs=in_any(3 + len(pieces) + len(late) + sums),
        scratch_shapes=[
            VMEM((length, width), bf16),
            VMEM((2, big, width), bf16),
            VMEM((2, 2 * length, part), bf16),
            VMEM((3, block, 2 * length), bf16),
        ]
        + [VMEM(s, bf16) for s in all_shapes]
        + held([act] * 3 + [piece] * len(pieces))
        + [VMEM((length, width), bf16), DMA, DMA((3 * chunks + len(pieces),))]
        + [DMA((seq_size,))] * 2
        + [DMA((max(1, len(late)), shard_size))] * 2
        + [DMA((max(1, sums), shard_size))] * 2
        + [DMA((2,)), DMA((2, 2)), DMA((len(pieces),))],
        compiler_params=kernel_params(2),
    )(tok_other, tok, cot, cot_other, *pieces_in, *mlp_weights)
    outs = list(outs)
    first = 3 + len(pieces)
    second = first + len(late)
    return outs[:3], outs[3:first], outs[first:second], outs[second:]


def mlp_back(d_gate, d_up, gate, up, hidden, cot, gains_all, grads):
    seq_size, shard_size = lax.axis_size("seq"), lax.axis_size("shard")
    rows, width = hidden.shape
    chunks = len(gate)
    length = rows * seq_size
    part = width // shard_size
    count = len(grads)
    shared = length > 2048

    def kernel(*refs):
        take = Refs(refs)
        sources = take(2 + 2 * chunks)
        hidden_ref, cot_ref, gains_ref = take(3)
        grad_refs = take(count)
        d_hidden_ref, d_gain_ref, d_attn_all = take(3)
        sum_refs = take(count)
        terms = take(1 if shared else 2)
        arrived = take(2)
        scatter_sems = [take(2), take(2)]
        other_ref, swap_ref, d_attn_ref = take(3)
        ns, nr, swap_sem, own_sem, sum_s, sum_r = take(6)
        loaded, load_sems = take(2 + 2 * chunks), take(1)[0]
        dg_ref, du_ref = loaded[:2]
        gate_refs, up_refs = loaded[2 : 2 + chunks], loaded[2 + chunks :]
        loads = Moves(load_sems)
        for source, target in zip(sources, loaded):
            loads.start(source, target)

        me = lax.axis_index("seq")
        entry_barrier(seq_neighbours(seq_size), shard_size)
        moves = [
            ShardExchange(shard_size, lambda j, g=g: g.at[j], out, sum_s.at[i], sum_r.at[i])
            for i, (g, out) in enumerate(zip(grad_refs, sum_refs))
        ]
        for move in moves[:BEFORE]:
            move.start()
        swap = PairSwap(other_ref, swap_ref, swap_sem).copy
        loads.wait()
        scatters = [
            SeqScatter(seq_size, terms[0 if shared else i], arrived[i], *scatter_sems[i])
            for i in range(2)
        ]

        def term(plane):
            scatter = scatters[plane]

            def compute(mask):
                tokens = scatter.tokens(mask, plane * length)
                for z in range(shard_size):
                    total = None
                    for c in range(chunks):
                        both = dot_nt(dg_ref[c, tokens, :], gate_refs[c][z])
                        both += dot_nt(du_ref[c, tokens, :], up_refs[c][z])
                        total = both if total is None else total + both
                    scatter.put(mask, slice(z * part, (z + 1) * part), total)

            return compute

        here, there = scatters
        there.send_terms(term(1), merge=True)
        if shared:
            there.merge_inner()
            there.merge(other_ref)
            swap.start()
            there.finish()
            here.send_terms(term(0), merge=True)
        else:
            here.send_terms(term(0))
            there.merge_inner()
            here.merge_leaves()
            there.merge(other_ref)
            swap.start()
        for move in moves[BEFORE:]:
            move.start()
        here.merge_inner()
        here.merge(d_hidden_ref)
        swap.wait()
        d_normed = d_hidden_ref[...] + swap_ref[...].astype(f32)
        values = hidden_ref[...]
        gain = jnp.concatenate([gains_ref[z, 1:2, :] for z in range(shard_size)], axis=1)
        d_values, d_gain = norm_back(values, inverse_rms(values), gain, d_normed)
        d_hidden = cot_ref[...].astype(f32) + d_values
        d_attn_ref[...] = d_hidden.astype(bf16)
        gather = SeqGather(seq_size, d_attn_all, rows, ns, nr, own=d_attn_ref)
        gather.start()
        own = pltpu.make_async_copy(d_attn_ref, d_attn_all.at[rows_at(me, rows), :], own_sem)
        own.start()
        d_hidden_ref[...] = d_hidden
        d_gain_ref[...] = d_gain
        gather.forwards()
        own.wait()
        gather.finish()
        for scatter in scatters[: 1 if shared else 2]:
            scatter.finish()
        for move in moves:
            move.wait()

    scatter = scatter_scratch(seq_size, rows, width)
    inputs = [d_gate, d_up, *gate, *up]
    outs = pl.pallas_call(
        kernel,
        name="mlp_back",
        out_shape=[
            array((rows, width), f32),
            array((1, width), f32),
            array((length, width)),
        ]
        + [array(g.shape) for g in grads],
        in_specs=in_any(2 + 2 * chunks) + in_vmem(3) + in_any(count),
        out_specs=in_vmem(2) + in_any(1 + count),
        scratch_shapes=scatter[:1] * (1 if shared else 2)
        + scatter[1:2] * 2
        + [DMA((seq_size,))] * 4
        + [VMEM((rows, width), bf16)] * 3
        + [DMA((seq_size,))] * 2
        + [DMA((2,)), DMA]
        + [DMA((max(1, count), shard_size))] * 2
        + held(inputs)
        + [DMA((len(inputs),))],
        compiler_params=kernel_params(3),
    )(*inputs, hidden, cot, gains_all, *grads)
    return outs[:3], list(outs[3:])


class OutputSum:
    def __init__(self, scatter, act, down_refs, base=0):
        self.scatter, self.act, self.down_refs, self.base = scatter, act, down_refs, base

    def compute(self, mask):
        tokens = self.scatter.tokens(mask, self.base)
        shards, _, part = self.down_refs[0].shape
        for z in range(shards):
            total = None
            for c, down in enumerate(self.down_refs):
                one = dot_nn(self.act[c, tokens, :], down[z])
                total = one if total is None else total + one
            self.scatter.put(mask, slice(z * part, (z + 1) * part), total)


def attend_back(d_attn, wo, mixed, q, k, v, lse, table, normed, grads, activ, down):
    seq_size, shard_size = lax.axis_size("seq"), lax.axis_size("shard")
    length, width = d_attn.shape
    rows = length // seq_size
    cols = q.shape[1]
    part = wo.shape[2]
    big = row_step(length, 512)
    block = row_step(length, 256)
    scale = 1.0 / math.sqrt(HD)
    pair = 2 * HD
    count = len(grads)
    chunks = len(down)

    def kernel(*refs):
        take = Refs(refs)
        sources = take(9 + chunks)
        grad_refs = take(count)
        act_all = take(1)[0] if chunks else None
        dq_ref, dk_ref, dv_ref, gq_ref, gk_ref, gv_ref = take(6)
        if chunks:
            swap_ref = take(1)[0]
        sum_refs = take(count + 1)
        do_ref, kt_ref, dk_acc, dv_acc, xt_ref, go_ref, sum_s, sum_r = take(8)
        loaded, load_sems = take(9 + chunks), take(1)[0]
        da_ref, wo_ref, mixed_ref, q_ref, k_ref, v_ref, lse_ref, t_ref, n_ref = loaded[:9]
        down_refs = loaded[9:]
        loads = Moves(load_sems)
        first = list(range(9, 9 + chunks)) + [0, 2]
        for i in first + [1, 3, 4, 5, 6, 7, 8]:
            loads.start(sources[i], loaded[i])

        if chunks:
            terms, arrived, ss, sr, act_ref, other_ref, act_sem, swap_sem = take(8)
            act_copy = pltpu.make_async_copy(
                act_all.at[:, pl.ds(length, length), :], act_ref, act_sem
            )
            act_copy.start()
        entry_barrier(seq_neighbours(seq_size) if chunks else [], shard_size)
        moves = [
            ShardExchange(shard_size, lambda j, g=g: g.at[j], out, sum_s.at[i], sum_r.at[i])
            for i, (g, out) in enumerate(zip(grad_refs + [go_ref], sum_refs))
        ]
        for move in moves[:-1]:
            move.start()
        if chunks:
            swap = PairSwap(other_ref, swap_ref, swap_sem).copy
            act_copy.wait()
            loads.wait(chunks)
            out_sum = OutputSum(SeqScatter(seq_size, terms, arrived, ss, sr), act_ref, down_refs)
            out_sum.scatter.send_terms(out_sum.compute, merge=True)

        loads.wait(2)
        xt_ref[...] = jnp.transpose(mixed_ref[...])
        for z in range(shard_size):
            go_ref[z] = dot_nn(xt_ref[...], da_ref[:, z * part : (z + 1) * part]).astype(bf16)
        moves[-1].start()
        loads.wait(6)

        @pl.loop(0, length // big)
        def _(i):
            r = rows_at(i, big)
            total = dot_nt(da_ref[r, :part], wo_ref[0])
            for z in range(1, shard_size):
                total += dot_nt(da_ref[r, z * part : (z + 1) * part], wo_ref[z])
            do_ref[r, :] = total.astype(bf16)

        kt_ref[...] = jnp.transpose(k_ref[...])
        if chunks:
            out_sum.scatter.merge_inner()

        def heads(hp, lanes):
            dk_acc[...] = jnp.zeros_like(dk_acc)
            dv_acc[...] = jnp.zeros_like(dv_acc)
            for i in range(length // block):
                first, last = i * block, (i + 1) * block
                q2 = q_ref[first:last, lanes]
                do2 = do_ref[first:last, lanes]
                keys = k_ref[:last, lanes]
                values = v_ref[:last, lanes]
                dqt, dk_add, dv_add = None, None, None
                for head in (0, 1):
                    keep = head_lanes(head, q2.shape)
                    qm = jnp.where(keep, q2, jnp.zeros_like(q2))
                    dom = jnp.where(keep, do2, jnp.zeros_like(do2))
                    st = dot_nt(keys, qm)
                    row = lse_ref[pl.ds(hp * 2 + head, 1), first:last]
                    p = jnp.exp(st - row)
                    r = lax.broadcasted_iota(jnp.int32, (block, block), 0)
                    c = lax.broadcasted_iota(jnp.int32, (block, block), 1)
                    tail = jnp.where(r <= c, p[first:], 0.0)
                    p = tail if i == 0 else jnp.concatenate([p[:first], tail], axis=0)
                    dp = dot_nt(values, dom)
                    inner = jnp.sum(dp * p, axis=0, keepdims=True)
                    ds = (p * (dp - inner)).astype(bf16)
                    dv_one = dot_nn(p.astype(bf16), dom)
                    dk_one = dot_nn(ds, qm)
                    dv_add = dv_one if head == 0 else dv_add + dv_one
                    dk_add = dk_one if head == 0 else dk_add + dk_one
                    dqt_one = dot_nn(kt_ref[lanes, :last], ds)
                    if head == 0:
                        dqt = dqt_one
                    else:
                        sub = lax.broadcasted_iota(jnp.int32, dqt.shape, 0)
                        dqt = jnp.where(sub < HD, dqt, dqt_one)
                dk_acc[:last, :] += dk_add
                dv_acc[:last, :] += dv_add
                dq = (jnp.transpose(dqt) * scale).astype(bf16).astype(f32)
                dq_ref[first:last, lanes] = turn(dq, t_ref[first:last, :], True).astype(bf16)
            dv_ref[:, lanes] = dv_acc[...].astype(bf16)

            @pl.loop(0, length // big)
            def _(i):
                r = rows_at(i, big)
                dk = dk_acc[r, :].astype(bf16).astype(f32)
                dk_ref[r, lanes] = turn(dk, t_ref[r, :], True).astype(bf16)

        if chunks:
            for hp in range(cols // pair):
                heads(hp, slice(hp * pair, (hp + 1) * pair))
                if hp == 0:
                    out_sum.scatter.merge(other_ref)
                    swap.start()
        else:

            @pl.loop(0, cols // pair)
            def _(hp):
                heads(hp, rows_at(hp, pair))

        loads.wait()
        for source, out in ((dq_ref, gq_ref), (dk_ref, gk_ref), (dv_ref, gv_ref)):
            xt_ref[...] = jnp.transpose(source[...])
            for z in range(shard_size):
                out[z] = dot_nn(xt_ref[...], n_ref[:, z * part : (z + 1) * part]).astype(bf16)
        if chunks:
            swap.wait()
            out_sum.scatter.finish()
        for move in moves:
            move.wait()

    grad = array((shard_size, cols, part))
    scratch = [
        VMEM((length, cols), bf16),
        VMEM((cols, length), bf16),
        VMEM((length, pair), f32),
        VMEM((length, pair), f32),
        VMEM((cols, length), bf16),
        VMEM((shard_size, cols, part), bf16),
    ] + [DMA((count + 1, shard_size))] * 2
    inputs = [d_attn, wo, mixed, q, k, v, lse, table, normed, *down]
    scratch += held(inputs) + [DMA((len(inputs),))]
    if chunks:
        scratch += scatter_scratch(seq_size, rows, width)
        scratch += [VMEM((chunks, length, activ.shape[2]), bf16), VMEM((rows, width), bf16)]
        scratch += [DMA, DMA((2,))]
    outs = pl.pallas_call(
        kernel,
        name="attend_back",
        out_shape=[array((length, cols))] * 3
        + [grad] * 3
        + [array((rows, width))] * (1 if chunks else 0)
        + [array(g.shape) for g in grads]
        + [grad],
        in_specs=in_any(9 + chunks + count + (1 if chunks else 0)),
        out_specs=in_vmem(7 if chunks else 6) + in_any(count + 1),
        scratch_shapes=scratch,
        compiler_params=kernel_params(4),
    )(*inputs, *grads, *([activ] if chunks else []))
    outs = list(outs)
    other = outs.pop(6) if chunks else None
    return outs[:3], outs[3:6], other, outs[6:]


def output_parts(activ, down, hidden):
    seq_size, shard_size = lax.axis_size("seq"), lax.axis_size("shard")
    rows, width = hidden.shape
    length = rows * seq_size
    chunks = len(down)

    def kernel(*refs):
        take = Refs(refs)
        act_ref, hidden_ref = take(2)
        down_refs = take(chunks)
        out_ref, terms, first, second = take(4)
        sems = [take(2), take(2)]
        total_ref, other_ref, swap_ref, swap_sem = take(4)
        entry_barrier(seq_neighbours(seq_size), shard_size)
        there, here = (
            OutputSum(SeqScatter(seq_size, terms, arrived, *sem), act_ref, down_refs, base)
            for arrived, sem, base in ((first, sems[0], length), (second, sems[1], 0))
        )
        there.scatter.run(there.compute, other_ref)
        swap = PairSwap(other_ref, swap_ref, swap_sem).copy
        swap.start()
        there.scatter.finish()
        here.scatter.run(here.compute, total_ref)
        swap.wait()
        out_ref[...] = (total_ref[...] + swap_ref[...].astype(f32) + hidden_ref[...]).astype(bf16)
        here.scatter.finish()

    scatter = scatter_scratch(seq_size, rows, width)
    return pl.pallas_call(
        kernel,
        name="output_parts",
        out_shape=array((rows, width)),
        in_specs=in_vmem(2 + chunks),
        out_specs=in_vmem(1)[0],
        scratch_shapes=scatter[:2]
        + scatter[1:2]
        + [DMA((seq_size,))] * 4
        + [VMEM((rows, width), f32), VMEM((rows, width), bf16), VMEM((rows, width), bf16)]
        + [DMA((2,))],
        compiler_params=kernel_params(6),
    )(activ, hidden, *down)


def finish(
    d_qkv, attn_weights, g_qkv, x, d_hidden, gains_all, d_gain_two, sums, g_output, block,
    output_of,
):
    seq_size, shard_size = lax.axis_size("seq"), lax.axis_size("shard")
    rows, width = x.shape
    part = width // shard_size
    cols = d_qkv[0].shape[1]
    length = rows * seq_size
    pieces = len(sums)
    half = pieces // 3 * block
    activ, down, hidden, other = output_of or (None, [], None, None)
    chunks = len(down)
    pairs = shard_size // 2

    def kernel(*refs):
        take = Refs(refs)
        x_ref, d_hidden_ref, gains_ref, gain2_ref = take(4)
        sources = take(9 + chunks)
        hidden_ref, other_ref = take(2) if chunks else (None, None)
        act_all = take(1)[0] if chunks else None
        sum_refs, go_ref = take(pieces), take(1)[0]
        d_inputs_ref, gain_ref = take(2)
        qkv_refs = take(3)
        output_ref = take(1)[0] if chunks else None
        wo_ref, wg_ref, wu_ref, wd_ref = take(4)
        total_ref, gain_mine, gain_shards, gain_line, gain_seq = take(5)
        gs, gr, hs, hr = take(4)
        in_terms, in_arrived, in_s, in_r = take(4)
        firsts, middles, seconds, reduce_sems = take(4)
        received, wide, tall, load_sem, store_sem = take(5)
        loaded, in_sems = take(9 + chunks), take(1)[0]
        d_refs, w_refs, g_refs = loaded[:3], loaded[3:6], loaded[6:9]
        down_refs = loaded[9:]
        ins = Moves(in_sems)
        for i in [6, 7, 8, 0, 1, 2, 3, 4, 5] + list(range(9, 9 + chunks)):
            ins.start(sources[i], loaded[i])
        if chunks:
            out_terms, out_arrived, out_s, out_r, act_ref, act_sem, out_total = take(7)
            act_copy = pltpu.make_async_copy(act_all.at[:, pl.ds(0, length), :], act_ref, act_sem)
            act_copy.start()

        me = lax.axis_index("seq")
        entry_barrier(range(1, seq_size), shard_size)
        reduces = [
            PairReduce(
                shard_size, g_refs[i], firsts.at[i], middles.at[i], seconds.at[i], reduce_sems.at[i]
            )
            for i in range(3)
        ]
        ins.wait(3)
        for reduce in reduces:
            reduce.start()
        ins.wait(6)
        in_sum = SeqScatter(seq_size, in_terms, in_arrived, in_s, in_r)

        def inputs_term(mask):
            tokens = in_sum.tokens(mask)
            for z in range(shard_size):
                total = None
                for d_ref, w_ref in zip(d_refs, w_refs):
                    term = dot_nt(d_ref[tokens, :], w_ref[z])
                    total = term if total is None else total + term
                in_sum.put(mask, slice(z * part, (z + 1) * part), total)

        in_sum.send_terms(inputs_term, merge=True)
        if chunks:
            act_copy.wait()
            ins.wait()
            out_sum = OutputSum(
                SeqScatter(seq_size, out_terms, out_arrived, out_s, out_r), act_ref, down_refs
            )
            out_sum.scatter.send_terms(out_sum.compute)

        loads = [
            pltpu.make_async_copy(source, received.at[i % 2], load_sem.at[i % 2])
            for i, source in enumerate(sum_refs)
        ]
        stores = []

        def store(staging, target, value):
            turn_of = sum(1 for s in stores if s[0] is staging)
            slot = turn_of % 2
            sem = store_sem.at[0 if staging is wide else 1, slot]
            if turn_of >= 2:
                [s for s in stores if s[0] is staging][-2][1].wait()
            staging[slot] = value
            copy = pltpu.make_async_copy(staging.at[slot], target, sem)
            copy.start()
            stores.append((staging, copy))

        def collect(i):
            if i + 1 < pieces:
                loads[i + 1].start()
            loads[i].wait()
            for parity in (0, 1):
                total = received[i % 2, parity].astype(f32)
                for p in range(1, pairs):
                    total = total + received[i % 2, 2 * p + parity].astype(f32)
                start = parity * half + i // 3 * block
                if i % 3 == 2:
                    store(wide, wd_ref.at[start : start + block, :], total)
                else:
                    target = (wg_ref, wu_ref)[i % 3]
                    store(tall, target.at[:, start : start + block], jnp.transpose(total))

        loads[0].start()
        third = (pieces + 2) // 3
        in_sum.merge_inner()
        reduces[0].middle()
        if chunks:
            out_sum.scatter.merge_leaves()
        for i in range(third):
            collect(i)
        reduces[1].middle()
        in_sum.merge(total_ref)
        values = x_ref[...].astype(f32)
        gain = jnp.concatenate([gains_ref[z, 0:1, :] for z in range(shard_size)], axis=1)
        d_values, d_gain = norm_back(values, inverse_rms(values), gain, total_ref[...])
        d_inputs_ref[...] = (d_hidden_ref[...] + d_values).astype(bf16)
        for z in range(shard_size):
            lanes = slice(z * part, (z + 1) * part)
            gain_mine[z, 0:1, :] = d_gain[:, lanes]
            gain_mine[z, 1:2, :] = gain2_ref[0:1, lanes]
            gain_mine[z, 2:, :] = jnp.zeros((6, part), f32)
        line = ShardExchange(shard_size, lambda j: gain_mine.at[j], gain_shards, gs, gr)
        line.start()
        for i in range(third, 2 * third):
            collect(i)
        reduces[2].middle()
        if chunks:
            out_sum.scatter.merge_inner()
        line.wait()
        gain_line[...] = sum(gain_shards[z] for z in range(shard_size))

        def to_seq(step):
            return pltpu.make_async_remote_copy(
                src_ref=gain_line,
                dst_ref=gain_seq.at[step],
                send_sem=hs.at[step],
                recv_sem=hr.at[step],
                device_id={"seq": jnp.bitwise_xor(me, step)},
                device_id_type=MESH,
            )

        for step in range(1, seq_size):
            to_seq(step).start()
        for i in range(2 * third, pieces):
            collect(i)
        wo_ref[...] = sum(go_ref[z].astype(f32) for z in range(shard_size))
        if chunks:
            out_sum.scatter.merge(out_total)
            output_ref[...] = (
                out_total[...] + other_ref[...].astype(f32) + hidden_ref[...]
            ).astype(bf16)
        for reduce, out in zip(reduces, qkv_refs):
            out[...] = jnp.transpose(reduce.total())
        for step in range(1, seq_size):
            to_seq(step).wait()
        gain_ref[...] = gain_line[...] + sum(gain_seq[step] for step in range(1, seq_size))
        for staging in (wide, tall):
            for _, copy in [s for s in stores if s[0] is staging][-2:]:
                copy.wait()
        for reduce in reduces:
            reduce.finish()
        in_sum.finish()
        if chunks:
            out_sum.scatter.finish()

    scratch = [
        VMEM((rows, width), f32),
        VMEM((shard_size, 8, part), f32),
        VMEM((shard_size, 8, part), f32),
        VMEM((8, part), f32),
        VMEM((seq_size, 8, part), f32),
    ]
    scratch += [DMA((shard_size,))] * 2 + [DMA((seq_size,))] * 2
    scratch += scatter_scratch(seq_size, rows, width)
    scratch += [VMEM((3, pairs, cols, part), bf16)] * 3 + [DMA((3, 4, pairs))]
    scratch += [
        VMEM((2, shard_size, block, part), bf16),
        VMEM((2, block, part), f32),
        VMEM((2, part, block), f32),
        DMA((2,)),
        DMA((2, 2)),
    ]
    inputs = [*d_qkv, *attn_weights, *g_qkv, *down]
    scratch += held(inputs) + [DMA((len(inputs),))]
    if chunks:
        scratch += scatter_scratch(seq_size, rows, width)
        scratch += [VMEM((chunks, length, block), bf16), DMA, VMEM((rows, width), f32)]
    extra = 1 if chunks else 0
    units = 2 * half
    outs = pl.pallas_call(
        kernel,
        name="finish",
        out_shape=[array((rows, width)), array((8, part), f32)]
        + [array((part, cols), f32)] * 3
        + [array((rows, width))] * extra
        + [array((cols, part), f32)]
        + [array((part, units), f32)] * 2
        + [array((units, part), f32)],
        in_specs=in_vmem(4)
        + in_any(9 + chunks)
        + in_vmem(2 * extra)
        + in_any(extra + pieces)
        + in_vmem(1),
        out_specs=in_vmem(6 + extra) + in_any(3),
        scratch_shapes=scratch,
        compiler_params=kernel_params(5),
    )(
        x, d_hidden, gains_all, d_gain_two, *inputs,
        *([hidden, other, activ] if chunks else []), *sums, g_output,
    )
    outs = list(outs)
    output = outs.pop(5) if chunks else None
    return outs, output


def rotation_table(position_ids):
    half = HD // 2
    freqs = theta_base ** (-(jnp.arange(half, dtype=f32) * 2.0) / HD)
    angles = position_ids.astype(f32)[:, None] * freqs[None, :]
    cosine, sine = jnp.cos(angles), jnp.sin(angles)
    return jnp.concatenate([cosine, cosine, -sine, sine], axis=1)


EARLY = 4
AHEAD = 4
BEFORE = 2
SUMS = (1, 4)
START = 3


def body(
    inputs,
    positions,
    attn_gain,
    w_query,
    w_key,
    w_value,
    w_output,
    mlp_gain,
    w_gate,
    w_up,
    w_down,
    cotangent,
):
    shard_size = lax.axis_size("shard")
    x, cot = inputs[0], cotangent[0]
    gains = jnp.pad(jnp.stack([attn_gain, mlp_gain]).astype(f32), ((0, 6), (0, 0)))
    table = rotation_table(positions[0])
    half = w_gate.shape[1] // 2
    block = row_step(half, 256)
    chunks = half // block
    pieces = weight_pieces(chunks)
    early, late = pieces[:EARLY], pieces[EARLY:]
    mlp_weights = (w_gate, w_up, w_down)
    held, early_weights = forward(
        x, gains, table, cot, (w_query, w_key, w_value, w_output), mlp_weights, early, block
    )
    normed, tables, gains_all, wq, wk, wv, wo, q, k, v, mixed, lse, hidden = held[:13]
    cot_all, cot_other, tok, tok_other = held[13:]
    acts, grads, late_weights, sums = mlp(
        tok, tok_other, cot_all, cot_other, early_weights, mlp_weights, late, chunks, block,
        min(SUMS[0], len(pieces)),
    )
    activ, d_gate, d_up = acts
    weights = dict(zip(pieces, early_weights + late_weights))

    def kind(name):
        return [weights[c, name] for c in range(chunks)]

    done = len(sums)
    more = min(SUMS[1], len(pieces) - done)
    (d_hidden, d_gain_two, d_attn), moved = mlp_back(
        d_gate, d_up, kind("gate"), kind("up"), hidden, cot, gains_all, grads[done : done + more]
    )
    sums += moved
    done += more
    down = kind("down")
    together = tok.shape[0] <= 2048
    d_qkv, g_qkv, other, moved = attend_back(
        d_attn, wo, mixed, q, k, v, lse, tables, normed, grads[done:], activ,
        down if together else [],
    )
    sums += moved[:-1]
    results, output = finish(
        d_qkv, (wq, wk, wv), g_qkv, x, d_hidden, gains_all, d_gain_two, sums, moved[-1], block,
        (activ, down, hidden, other) if together else None,
    )
    if not together:
        output = output_parts(activ, down, hidden)
    d_inputs, gain_sums, g_query, g_key, g_value, g_output, g_gate, g_up, g_down = results
    return (
        output[None],
        d_inputs[None],
        gain_sums[0],
        g_query,
        g_key,
        g_value,
        g_output,
        gain_sums[1],
        g_gate,
        g_up,
        g_down,
    )


def solution(mesh):
    in_specs = (
        P("shard", "seq", None),
        P("shard", "seq"),
        P("shard"),
        P("shard", "seq"),
        P("shard", "seq"),
        P("shard", "seq"),
        P("seq", "shard"),
        P("shard"),
        P("shard", "seq"),
        P("shard", "seq"),
        P("seq", "shard"),
        P("shard", "seq", None),
    )
    out_specs = (
        P("shard", "seq", None),
        P("shard", "seq", None),
        P("shard"),
        P("shard", "seq"),
        P("shard", "seq"),
        P("shard", "seq"),
        P("seq", "shard"),
        P("shard"),
        P("shard", "seq"),
        P("shard", "seq"),
        P("seq", "shard"),
    )
    return jax.shard_map(body, mesh=mesh, in_specs=in_specs, out_specs=out_specs, check_vma=False)
```

```python
import math

import jax
import jax.numpy as jnp
from jax import lax
from jax.experimental import pallas as pl
from jax.experimental.pallas import tpu as pltpu
from jax.sharding import PartitionSpec as P

HD = 64
epsilon = 1e-05
theta_base = 130000.0
bf16 = jnp.bfloat16
f32 = jnp.float32
VMEM = pltpu.VMEM
DMA = pltpu.SemaphoreType.DMA
MESH = pl.DeviceIdType.MESH


def dot_nn(a, b):
    return jnp.dot(a, b, preferred_element_type=f32)


def dot_nt(a, b):
    return lax.dot_general(a, b, (((1,), (1,)), ((), ())), preferred_element_type=f32)


def in_vmem(count):
    return [pl.BlockSpec(memory_space=VMEM)] * count


def in_any(count):
    return [pl.BlockSpec(memory_space=pl.ANY)] * count


def array(shape, dtype=bf16):
    return jax.ShapeDtypeStruct(shape, dtype)


def kernel_params(collective_id=None, limit=62):
    if collective_id is None:
        return pltpu.CompilerParams(vmem_limit_bytes=limit << 20)
    return pltpu.CompilerParams(
        collective_id=collective_id, has_side_effects=True, vmem_limit_bytes=limit << 20
    )


def popcount(mask):
    return bin(mask).count("1")


def chip_masks(size):
    return sorted(range(0, size, 2), key=lambda m: (popcount(m), m))


def chip_bits(size):
    return [1 << b for b in range(1, size.bit_length() - 1)]


def last_hop(mask, core):
    set_bits = [1 << b for b in range(1, mask.bit_length()) if mask >> b & 1]
    return set_bits[-1] if core == 0 else set_bits[0]


def further_masks(mask, core, size):
    return [
        mask | hop
        for hop in chip_bits(size)
        if not mask & hop and last_hop(mask | hop, core) == hop
    ]


def seq_neighbours(size):
    return [1] + chip_bits(size)


def entry_barrier(seq_masks, shard_size):
    barrier = pltpu.get_barrier_semaphore()
    me, mine = lax.axis_index("seq"), lax.axis_index("shard")
    for mask in seq_masks:
        pl.semaphore_signal(
            barrier, inc=1, device_id={"seq": jnp.bitwise_xor(me, mask)}, device_id_type=MESH
        )
    for step in range(1, shard_size):
        pl.semaphore_signal(
            barrier, inc=1, device_id={"shard": lax.rem(mine + step, shard_size)},
            device_id_type=MESH,
        )
    pl.semaphore_wait(barrier, len(seq_masks) + max(shard_size - 1, 0))


class SeqGather:
    def __init__(self, size, out, rows, send_sem, recv_sem, own=None):
        self.size, self.out, self.rows = size, out, rows
        self.send_sem, self.recv_sem = send_sem, recv_sem
        self.me = lax.axis_index("seq")
        self.core = lax.rem(self.me, 2)
        self.own = own

    def block(self, index):
        return self.out.at[pl.ds(pl.multiple_of(index * self.rows, self.rows), self.rows), :]

    def copy(self, arrives, hop):
        block = self.block(jnp.bitwise_xor(self.me, arrives ^ hop))
        src = self.own if arrives == hop and self.own is not None else block
        return pltpu.make_async_remote_copy(
            src_ref=src,
            dst_ref=block,
            send_sem=self.send_sem.at[arrives],
            recv_sem=self.recv_sem.at[arrives],
            device_id={"seq": jnp.bitwise_xor(self.me, hop)},
            device_id_type=MESH,
        )

    def wait_recv(self, mask):
        block = self.block(jnp.bitwise_xor(self.me, mask))
        pltpu.make_async_remote_copy(
            src_ref=block,
            dst_ref=block,
            send_sem=self.send_sem.at[mask],
            recv_sem=self.recv_sem.at[mask],
            device_id={"seq": jnp.bitwise_xor(self.me, 1)},
            device_id_type=MESH,
        ).wait_recv()

    def start(self):
        for hop in reversed(seq_neighbours(self.size)):
            self.copy(hop, hop).start()

    def forward(self, mask):
        self.wait_recv(mask)
        for core in (0, 1):
            for more in further_masks(mask, core, self.size):

                @pl.when(self.core == core)
                def _():
                    self.copy(more, more ^ mask).start()

        self.copy(mask | 1, 1).start()

    def forwards(self):
        for mask in chip_masks(self.size)[1:]:
            self.forward(mask)

    def finish(self):
        for mask in chip_masks(self.size):
            self.wait_recv(mask | 1)
        for mask in range(1, self.size):
            self.copy(mask, 1 if mask & 1 else mask & -mask).wait_send()


def height(mask, core, size):
    return max([0] + [1 + height(m, core, size) for m in further_masks(mask, core, size)])


class SeqScatter:
    def __init__(self, size, terms, arrived, send_sem, recv_sem):
        self.size, self.terms, self.arrived = size, terms, arrived
        self.send_sem, self.recv_sem = send_sem, recv_sem
        self.me = lax.axis_index("seq")
        self.core = lax.rem(self.me, 2)
        self.masks = chip_masks(size)[::-1]
        self.order = [
            sorted(self.masks, key=lambda m: (height(m, core, size), -popcount(m)))
            for core in (0, 1)
        ]
        self.leaves = size // 4
        self.merged = 0

    def copy(self, mask, hop):
        core = 1 - self.core if mask & 1 else self.core
        return pltpu.make_async_remote_copy(
            src_ref=self.terms.at[mask // 2, core],
            dst_ref=self.arrived.at[mask - 1],
            send_sem=self.send_sem.at[mask],
            recv_sem=self.recv_sem.at[mask],
            device_id={"seq": jnp.bitwise_xor(self.me, hop)},
            device_id_type=MESH,
        )

    def tokens(self, mask, base=0):
        pair = 2 * self.terms.shape[2]
        start = jnp.bitwise_xor(self.me, mask) // 2 * pair + base
        return pl.ds(pl.multiple_of(start, pair), pair)

    def put(self, mask, lanes, total):
        rows = self.terms.shape[2]
        self.terms[mask // 2, :, :, lanes] = total.astype(bf16).reshape(2, rows, -1)

    def add(self, mask, source, write):
        rows = self.terms.shape[2]
        step = 32 if rows % 32 == 0 else 16

        @pl.loop(0, rows // step)
        def _(i):
            part = pl.ds(pl.multiple_of(i * step, step), step)
            total = self.terms[mask // 2, self.core, part, :].astype(f32)
            for s in source:
                total = total + self.arrived[s - 1, part, :].astype(f32)
            write(part, total)

    def merge(self, result=None):
        for core in (0, 1):
            mask = self.order[core][self.merged]
            further = further_masks(mask, core, self.size)

            def keep(part, total, mask=mask):
                if mask:
                    self.terms[mask // 2, self.core, part, :] = total.astype(bf16)
                else:
                    result[part, :] = total.astype(result.dtype)

            @pl.when(self.core == core)
            def _(mask=mask, further=further, keep=keep, core=core):
                for m in [mask | 1] + further:
                    self.copy(m, 1).wait_recv()
                self.add(mask, [mask | 1] + further, keep)
                if mask:
                    self.copy(mask, last_hop(mask, core)).start()

        self.merged += 1

    def send_terms(self, compute, merge=False):
        done = set()
        for mask in self.masks:
            compute(mask)
            self.copy(mask | 1, 1).start()
            if merge and self.merged < self.leaves:
                if all(order[self.merged] in done for order in self.order):
                    self.merge()
            done.add(mask)
        if merge:
            self.merge_leaves()

    def merge_leaves(self):
        while self.merged < self.leaves:
            self.merge()

    def merge_inner(self):
        while self.merged < len(self.masks) - 1:
            self.merge()

    def run(self, compute, result):
        self.send_terms(compute, merge=True)
        self.merge_inner()
        self.merge(result)

    def finish(self):
        for mask in range(1, self.size):
            self.copy(mask, 1).wait_send()


def scatter_scratch(seq_size, rows, width):
    return [
        VMEM((seq_size // 2, 2, rows, width), bf16),
        VMEM((seq_size - 1, rows, width), bf16),
        DMA((seq_size,)),
        DMA((seq_size,)),
    ]


class LineGather:
    def __init__(self, size, own, out, send_sem, recv_sem, copy_sem):
        self.size, self.own, self.out = size, own, out
        self.send_sem, self.recv_sem, self.copy_sem = send_sem, recv_sem, copy_sem
        self.k = lax.axis_index("shard")

    def sent(self, way, step):
        block = self.k - step if way == 0 else self.k + step
        valid = (
            jnp.logical_and(self.k < self.size - 1, block >= 0)
            if way == 0
            else jnp.logical_and(self.k > 0, block <= self.size - 1)
        )
        safe = jnp.clip(block, 0, self.size - 1)
        target = jnp.clip(self.k + 1 if way == 0 else self.k - 1, 0, self.size - 1)
        return valid, pltpu.make_async_remote_copy(
            src_ref=self.own if step == 0 else self.out.at[safe],
            dst_ref=self.out.at[safe],
            send_sem=self.send_sem.at[way, step],
            recv_sem=self.recv_sem.at[way, step],
            device_id={"shard": target},
            device_id_type=MESH,
        )

    def received(self, way, step):
        block = self.k - 1 - step if way == 0 else self.k + 1 + step
        valid = block >= 0 if way == 0 else block <= self.size - 1
        safe = jnp.clip(block, 0, self.size - 1)
        return valid, pltpu.make_async_remote_copy(
            src_ref=self.own,
            dst_ref=self.out.at[safe],
            send_sem=self.send_sem.at[way, step],
            recv_sem=self.recv_sem.at[way, step],
            device_id={"shard": lax.rem(self.k + 1, self.size)},
            device_id_type=MESH,
        )

    def local(self):
        return pltpu.make_async_copy(self.own, self.out.at[self.k], self.copy_sem)

    def step(self, step):
        if step == 0:
            self.local().start()
        if step == self.size - 1:
            self.local().wait()
        for way in (0, 1):
            if step > 0:
                valid, copy = self.received(way, step - 1)

                @pl.when(valid)
                def _():
                    copy.wait_recv()

            if step < self.size - 1:
                valid, copy = self.sent(way, step)

                @pl.when(valid)
                def _():
                    copy.start()

    def finish(self):
        for step in range(self.size - 1):
            for way in (0, 1):
                valid, copy = self.sent(way, step)

                @pl.when(valid)
                def _():
                    copy.wait_send()


class ShardExchange:
    def __init__(self, size, source, out, send_sem, recv_sem, bounce=None, bounce_sem=None):
        self.size, self.source, self.out = size, source, out
        self.send_sem, self.recv_sem = send_sem, recv_sem
        self.bounce, self.bounce_sem = bounce, bounce_sem
        self.k = lax.axis_index("shard")

    def copy(self, step):
        target = lax.rem(self.k + step, self.size)
        return pltpu.make_async_remote_copy(
            src_ref=self.source(target),
            dst_ref=self.out.at[self.k],
            send_sem=self.send_sem.at[step],
            recv_sem=self.recv_sem.at[step],
            device_id={"shard": target},
            device_id_type=MESH,
        )

    def arrival(self, step):
        return pltpu.make_async_remote_copy(
            src_ref=self.out.at[self.k],
            dst_ref=self.out.at[lax.rem(self.k + self.size - step, self.size)],
            send_sem=self.send_sem.at[step],
            recv_sem=self.recv_sem.at[step],
            device_id={"shard": lax.rem(self.k + step, self.size)},
            device_id_type=MESH,
        )

    def local(self):
        source = self.source(self.k) if self.bounce is None else self.bounce
        return pltpu.make_async_copy(source, self.out.at[self.k], self.send_sem.at[0])

    def lift(self):
        return pltpu.make_async_copy(self.source(self.k), self.bounce, self.bounce_sem)

    def start_local(self):
        if self.bounce is None:
            self.local().start()
        else:
            self.lift().start()

    def settle(self):
        if self.bounce is not None:
            self.lift().wait()
            self.local().start()

    def inner(self, step):
        target = lax.rem(self.k + step, self.size)
        beside = jnp.abs(target - self.k) == 1
        return jnp.logical_and(beside, target // 2 != self.k // 2)

    def start_inner(self):
        for step in (1, self.size - 1):

            @pl.when(self.inner(step))
            def _():
                self.copy(step).start()

    def start_outer(self):
        self.start_local()
        for step in range(1, self.size):

            @pl.when(jnp.logical_not(self.inner(step)))
            def _():
                self.copy(step).start()

    def start(self):
        self.start_local()
        for step in range(1, self.size):
            self.copy(step).start()

    def wait_recv(self):
        self.local().wait()
        for step in range(1, self.size):
            self.arrival(step).wait_recv()

    def wait_send(self):
        for step in range(1, self.size):
            self.copy(step).wait_send()

    def wait(self):
        self.wait_recv()
        self.wait_send()


class PairReduce:
    def __init__(self, size, terms, first, middle_terms, second, sems):
        self.size, self.terms, self.first, self.second = size, terms, first, second
        self.middle_terms = middle_terms
        self.sems = sems
        self.k = lax.axis_index("shard")
        self.pairs = size // 2

    def swap(self, pair):
        target = 2 * pair + 1 - lax.rem(self.k, 2)
        return pltpu.make_async_remote_copy(
            src_ref=self.terms.at[target],
            dst_ref=self.first.at[pair],
            send_sem=self.sems.at[0, pair],
            recv_sem=self.sems.at[1, pair],
            device_id={"shard": jnp.bitwise_xor(self.k, 1)},
            device_id_type=MESH,
        )

    def cross(self, step):
        mine = self.k // 2
        pair = lax.rem(mine + step, self.pairs)
        target = 2 * pair + lax.rem(self.k, 2)
        return pair, target, pltpu.make_async_remote_copy(
            src_ref=self.middle_terms.at[step],
            dst_ref=self.second.at[step],
            send_sem=self.sems.at[2, step],
            recv_sem=self.sems.at[3, step],
            device_id={"shard": target},
            device_id_type=MESH,
        )

    def start(self):
        for pair in range(self.pairs):
            self.swap(pair).start()

    def middle(self):
        for pair in range(self.pairs):
            self.swap(pair).wait_recv()
        for step in range(1, self.pairs):
            pair, target, copy = self.cross(step)
            total = self.terms[target].astype(f32) + self.first[pair].astype(f32)
            self.middle_terms[step] = total.astype(bf16)
            copy.start()

    def total(self):
        for step in range(1, self.pairs):
            self.cross(step)[2].wait_recv()
        total = self.terms[self.k].astype(f32) + self.first[self.k // 2].astype(f32)
        for step in range(1, self.pairs):
            total = total + self.second[step].astype(f32)
        return total

    def finish(self):
        for pair in range(self.pairs):
            self.swap(pair).wait_send()
        for step in range(1, self.pairs):
            self.cross(step)[2].wait_send()


class PairSwap:
    def __init__(self, source, out, sems):
        mine = lax.axis_index("shard")
        self.copy = pltpu.make_async_remote_copy(
            src_ref=source,
            dst_ref=out,
            send_sem=sems.at[0],
            recv_sem=sems.at[1],
            device_id={"shard": jnp.bitwise_xor(mine, 1)},
            device_id_type=MESH,
        )


class Moves:
    def __init__(self, sems):
        self.sems, self.copies = sems, []

    def start(self, source, target):
        copy = pltpu.make_async_copy(source, target, self.sems.at[len(self.copies)])
        copy.start()
        self.copies.append(copy)
        return copy

    def wait(self, count=None):
        count = len(self.copies) if count is None else count
        for copy in [c for c in self.copies if c is not None][:count]:
            copy.wait()
        left = [i for i, c in enumerate(self.copies) if c is not None][:count]
        for i in left:
            self.copies[i] = None


def held(arrays):
    return [VMEM(a.shape, a.dtype) for a in arrays]


class Refs:
    def __init__(self, refs):
        self.refs = list(refs)

    def __call__(self, count):
        out, self.refs = self.refs[:count], self.refs[count:]
        return out


def inverse_rms(values):
    return lax.rsqrt(jnp.mean(values * values, axis=-1, keepdims=True) + epsilon)


def norm_back(values, inverse, gain, d_normed):
    scaled = d_normed * gain
    d_values = inverse * scaled - values * (inverse * inverse * inverse) * jnp.mean(
        scaled * values, axis=-1, keepdims=True
    )
    return d_values, jnp.sum(d_normed * values * inverse, axis=0, keepdims=True)


def head_lanes(head, shape):
    lane = lax.broadcasted_iota(jnp.int32, shape, 1)
    return lane < HD if head == 0 else lane >= HD


def turn(values, table, back):
    width = values.shape[1]
    cosine = jnp.concatenate([table[:, :HD]] * (width // HD), axis=1)
    sine = jnp.concatenate([table[:, HD:]] * (width // HD), axis=1)
    lane = lax.broadcasted_iota(jnp.int32, values.shape, 1)
    half = HD // 2
    partner = jnp.where(
        lane % HD < half,
        pltpu.roll(values, width - half, 1),
        pltpu.roll(values, half, 1),
    )
    if back:
        return values * cosine - partner * sine
    return values * cosine + partner * sine


def row_step(length, most):
    return most if length % most == 0 else length


def rows_at(index, step):
    return pl.ds(pl.multiple_of(index * step, step), step)


def weight_pieces(chunks):
    return [(c, kind) for c in range(chunks) for kind in ("gate", "up", "down")]


def piece_shape(kind, shards, part, block):
    return (shards, block, part) if kind == "down" else (shards, part, block)


def piece_source(kind, refs, chunk, block):
    ref = refs[kind]
    half = (ref.shape[0] if kind == "down" else ref.shape[1]) // 2

    def source(j):
        start = pl.multiple_of(lax.rem(j, 2) * half + chunk * block, block)
        if kind == "down":
            return ref.at[pl.ds(start, block), :]
        return ref.at[:, pl.ds(start, block)]

    return source


def split_masks(size):
    masks = chip_masks(size)[1:]
    return [m for m in masks if popcount(m) == 1], [m for m in masks if popcount(m) > 1]


def forward(x, gains, table, cot, attn_weights, mlp_weights, pieces, block):
    seq_size, shard_size = lax.axis_size("seq"), lax.axis_size("shard")
    rows, width = x.shape
    part, cols = attn_weights[0].shape
    length = rows * seq_size
    big = row_step(length, 512)
    query = row_step(length, 256 if length <= 2048 else 128)
    pair = 2 * HD
    scale = 1.0 / math.sqrt(HD)

    def kernel(*refs):
        take = Refs(refs)
        x_ref, gains_ref, table_ref, cot_ref = take(4)
        own_weights = take(4)
        mlp_refs = dict(zip(("gate", "up", "down"), take(3)))
        normed_out, table_all, gains_all = take(3)
        weights_out = take(4)
        heads_out = take(4)
        lse_ref, hidden_ref = take(2)
        cot_all, cot_other, tok_all, tok_other = take(4)
        piece_refs = take(len(pieces))
        terms, arrived, ss, sr = take(4)
        normed_ref, normed_all = take(2)
        full_weights, heads_held = take(4), take(4)
        q_ref, k_ref, v_ref, o_ref = heads_held
        out_sems = take(1)[0]
        bounces, bounce_sems = take(len(pieces)), take(1)[0]
        ns, nr, ts, tr, cs, cr, ds, dr, ms, mr = take(10)
        gs, gr, line_s, line_r, line_c, piece_s, piece_r, local_sem, swap_sem = take(9)

        me, mine = lax.axis_index("seq"), lax.axis_index("shard")
        entry_barrier(seq_neighbours(seq_size), shard_size)
        gain = ShardExchange(shard_size, lambda j: gains_ref, gains_all, gs, gr)
        gain.start()
        lines = [
            LineGather(shard_size, own, out, line_s.at[i], line_r.at[i], line_c.at[i])
            for i, (own, out) in enumerate(zip(own_weights, full_weights))
        ]
        wq_all, wk_all, wv_all, wo_all = full_weights
        exchanges = [
            ShardExchange(
                shard_size, piece_source(kind, mlp_refs, c, block), out, piece_s.at[i],
                piece_r.at[i], bounces[i], bounce_sems.at[i],
            )
            for i, ((c, kind), out) in enumerate(zip(pieces, piece_refs))
        ]
        mine_rows = rows_at(me, rows)
        own_cot = pltpu.make_async_copy(cot_ref, cot_all.at[mine_rows, :], local_sem.at[0])
        tables = SeqGather(seq_size, table_all, rows, ts, tr)
        normed = SeqGather(seq_size, normed_all, rows, ns, nr)
        cots = SeqGather(seq_size, cot_all, rows, cs, cr, own=cot_ref)
        cots_other = SeqGather(seq_size, cot_other, rows, ds, dr)
        swap_cot = PairSwap(cot_ref, cot_other.at[mine_rows, :], swap_sem.at[0]).copy
        for line in lines[:3]:
            line.step(0)
        own_cot.start()
        table_all[mine_rows, :] = table_ref[...]
        tables.start()
        gain.wait_recv()
        values = x_ref[...].astype(f32)
        scaled = values * inverse_rms(values)
        for z in range(shard_size):
            lanes = slice(z * part, (z + 1) * part)
            normed_all[mine_rows, lanes] = (scaled[:, lanes] * gains_all[z, 0:1, :]).astype(bf16)
        normed.start()
        tables.forwards()
        for line in lines[:3]:
            line.step(1)
        for exchange in exchanges:
            exchange.start_inner()
        near, far = split_masks(seq_size)
        for mask in near:
            normed.forward(mask)
        cots.start()
        for step in range(2, shard_size):
            for line in lines[:3]:
                line.step(step)
            if step == 2:
                swap_cot.start()
                lines[3].step(0)
                for mask in far:
                    normed.forward(mask)
        tables.finish()
        normed.finish()
        outs = Moves(out_sems)
        outs.start(normed_all, normed_out)
        for held_weight, out in list(zip(full_weights, weights_out))[:3]:
            outs.start(held_weight, out)
        for mask in near:
            cots.forward(mask)
        lines[3].step(1)

        def start_pieces(point):
            if point == START:
                for exchange in exchanges[:AHEAD]:
                    exchange.start_outer()

        start_pieces(0)

        wq, wk, wv = (w.reshape(width, cols) for w in (wq_all, wk_all, wv_all))

        @pl.loop(0, length // big)
        def _(i):
            r = rows_at(i, big)
            tokens = normed_all[r, :]
            tab = table_all[r, :]
            q = turn(dot_nn(tokens, wq[...]), tab, False).astype(bf16)
            q_ref[r, :] = q * jnp.asarray(scale, bf16)
            k_ref[r, :] = turn(dot_nn(tokens, wk[...]), tab, False).astype(bf16)
            v_ref[r, :] = dot_nn(tokens, wv[...]).astype(bf16)

        for mask in far:
            cots.forward(mask)
        start_pieces(1)
        for step in range(2, shard_size - 1):
            lines[3].step(step)

        def attend(hp, lanes):
            for i in range(length // query):
                first, last = i * query, (i + 1) * query
                q2 = q_ref[first:last, lanes]
                out = None
                for head in (0, 1):
                    keep = head_lanes(head, q2.shape)
                    qm = jnp.where(keep, q2, jnp.zeros_like(q2))
                    s = dot_nt(qm, k_ref[:last, lanes])
                    r = lax.broadcasted_iota(jnp.int32, (query, query), 0)
                    c = lax.broadcasted_iota(jnp.int32, (query, query), 1)
                    tail = jnp.where(c <= r, s[:, first:], -1e30)
                    s = tail if i == 0 else jnp.concatenate([s[:, :first], tail], axis=1)
                    m = jnp.max(s, axis=1, keepdims=True)
                    p = jnp.exp(s - m)
                    total = jnp.sum(p, axis=1, keepdims=True)
                    low = (p * (1.0 / total)).astype(bf16)
                    o = dot_nn(low, v_ref[:last, lanes])
                    out = o if head == 0 else jnp.where(keep, o, out)
                    lse = jnp.transpose(jnp.broadcast_to(m + jnp.log(total), (query, 128)))
                    lse_ref[pl.ds(hp * 2 + head, 1), first:last] = lse[0:1, :]
                o_ref[first:last, lanes] = out.astype(bf16)

        if cols == 2 * pair:
            attend(0, slice(0, pair))
            swap_cot.wait_recv()
            cots_other.start()
            start_pieces(2)
            attend(1, slice(pair, cols))
        else:

            @pl.loop(0, cols // pair)
            def _(hp):
                attend(hp, rows_at(hp, pair))

            swap_cot.wait_recv()
            cots_other.start()
            start_pieces(2)
        lines[3].step(shard_size - 1)
        start_pieces(3)
        outs.start(full_weights[3], weights_out[3])
        for held_heads, out in zip(heads_held, heads_out):
            outs.start(held_heads, out)
        scatter = SeqScatter(seq_size, terms, arrived, ss, sr)

        def compute(mask):
            tokens = o_ref[scatter.tokens(mask), :]
            for z in range(shard_size):
                scatter.put(mask, slice(z * part, (z + 1) * part), dot_nn(tokens, wo_all[z]))

        scatter.send_terms(compute, merge=True)
        for mask in near:
            cots_other.forward(mask)
        for exchange in exchanges[:AHEAD]:
            exchange.settle()
        scatter.merge_inner()
        scatter.merge(hidden_ref)
        for mask in far:
            cots_other.forward(mask)
        hidden = hidden_ref[...] + x_ref[...].astype(f32)
        hidden_ref[...] = hidden
        scaled = hidden * inverse_rms(hidden)
        for z in range(shard_size):
            lanes = slice(z * part, (z + 1) * part)
            normed_ref[:, lanes] = (scaled[:, lanes] * gains_all[z, 1:2, :]).astype(bf16)
        swap_tok = PairSwap(normed_ref, tok_other, swap_sem.at[1]).copy
        swap_tok.start()
        toks = SeqGather(seq_size, tok_all, rows, ms, mr, own=normed_ref)
        toks.start()
        own_tok = pltpu.make_async_copy(normed_ref, tok_all.at[mine_rows, :], local_sem.at[1])
        own_tok.start()
        for exchange in exchanges[AHEAD:]:
            exchange.start_outer()
        for mask in near:
            toks.forward(mask)
        for mask in far:
            toks.forward(mask)
        swap_cot.wait_send()
        gain.wait_send()
        scatter.finish()
        own_cot.wait()
        cots.finish()
        for line in lines:
            line.finish()
        swap_tok.wait()
        own_tok.wait()
        toks.finish()
        cots_other.finish()
        for exchange in exchanges[AHEAD:]:
            exchange.settle()
        for exchange in exchanges:
            exchange.wait()
        outs.wait()

    weight = array((shard_size, part, cols))
    out_weight = array((shard_size, cols, part))
    heads = array((length, cols))
    tokens = array((length, width))
    shapes = [piece_shape(kind, shard_size, part, block) for _, kind in pieces]
    count = len(pieces)
    outs = pl.pallas_call(
        kernel,
        name="forward_attention",
        out_shape=[
            tokens,
            array((length, table.shape[1]), f32),
            array((shard_size,) + gains.shape, f32),
            weight,
            weight,
            weight,
            out_weight,
            heads,
            heads,
            heads,
            heads,
            array((max(8, cols // HD), length), f32),
            array((rows, width), f32),
            tokens,
            tokens,
            tokens,
            array((rows, width)),
        ]
        + [array(s) for s in shapes],
        in_specs=in_vmem(8) + in_any(3),
        out_specs=in_any(1) + in_vmem(2) + in_any(8) + in_vmem(2) + in_any(4 + count),
        scratch_shapes=scatter_scratch(seq_size, rows, width)
        + [VMEM((rows, width), bf16), VMEM((length, width), bf16)]
        + held([weight] * 3 + [out_weight] + [heads] * 4)
        + [DMA((9,))]
        + [VMEM(s[1:], bf16) for s in shapes]
        + [DMA((count,))]
        + [DMA((seq_size,))] * 10
        + [DMA((shard_size,))] * 2
        + [DMA((4, 2, shard_size - 1))] * 2
        + [DMA((4,))]
        + [DMA((count, shard_size))] * 2
        + [DMA((2,)), DMA((2, 2))],
        compiler_params=kernel_params(1),
    )(x, gains, table, cot, *attn_weights, *mlp_weights)
    return outs[:17], list(outs[17:])


def mlp(tok, tok_other, cot, cot_other, pieces_in, mlp_weights, late, chunks, block, sums):
    seq_size, shard_size = lax.axis_size("seq"), lax.axis_size("shard")
    length, width = tok.shape
    rows = tok_other.shape[0]
    part = width // shard_size
    big = row_step(length, 512)
    steps = length // big
    pieces = weight_pieces(chunks)
    early = pieces[: len(pieces_in)]

    def kernel(*refs):
        take = Refs(refs)
        tok_swap, tok_hbm = take(2)
        cots = take(2)
        early_refs = take(len(early))
        mlp_refs = dict(zip(("gate", "up", "down"), take(3)))
        acts_out = take(3)
        grads_out = take(len(pieces))
        late_refs = take(len(late))
        sum_refs = take(sums)
        tok2, cot_rows, cot_cols, xt = take(4)
        weights = take(len(pieces))
        act_ref, dg_ref, du_ref = take(3)
        grads = take(len(pieces))
        tok_ref, tok_sem, out_sems = take(3)
        bounces, bounce_sems = take(len(late)), take(1)[0]
        tok_copy = pltpu.make_async_copy(tok_hbm, tok_ref, tok_sem)
        tok_copy.start()
        outs = Moves(out_sems)
        ts, tr, late_s, late_r, sum_s, sum_r, row_sem, col_sem, load_sem = take(9)

        me, mine = lax.axis_index("seq"), lax.axis_index("shard")
        entry_barrier(seq_neighbours(seq_size), shard_size)
        late_moves = [
            ShardExchange(
                shard_size, piece_source(kind, mlp_refs, c, block), out, late_s.at[i], late_r.at[i],
                bounces[i], bounce_sems.at[i],
            )
            for i, ((c, kind), out) in enumerate(zip(late, late_refs))
        ]
        for move in late_moves:
            move.start()
        other = SeqGather(seq_size, tok2, rows, ts, tr, own=tok_swap)
        other.start()
        tok2[rows_at(me, rows), :] = tok_swap[...]
        everything = dict(zip(early, early_refs)) | dict(zip(late, late_refs))
        loads = [
            pltpu.make_async_copy(everything[p], w, load_sem.at[i])
            for i, (p, w) in enumerate(zip(pieces, weights))
        ]
        for load in loads[: len(early)]:
            load.start()
        held = dict(zip(pieces, weights))

        def row_copy(plane, i, slot):
            return pltpu.make_async_copy(
                cots[plane].at[rows_at(i, big), :], cot_rows.at[slot], row_sem.at[slot]
            )

        def stage(plane, these, base):
            token_ref = (tok_ref, tok2)[plane]

            @pl.loop(0, steps)
            def _(i):
                slot = lax.rem(i + base, 2)

                @pl.when(i + 1 < steps)
                def _():
                    row_copy(plane, i + 1, 1 - slot).start()

                tokens = token_ref[rows_at(i, big), :]
                row_copy(plane, i, slot).wait()
                r = pl.ds(pl.multiple_of(plane * length + i * big, big), big)
                for c in these:
                    gate_w, up_w = held[c, "gate"], held[c, "up"]
                    gate = dot_nn(tokens, gate_w.reshape(width, block)[...])
                    up = dot_nn(tokens, up_w.reshape(width, block)[...])
                    d_act = dot_nt(cot_rows[slot, :, :part], held[c, "down"][0])
                    for z in range(1, shard_size):
                        lanes = slice(z * part, (z + 1) * part)
                        d_act += dot_nt(cot_rows[slot, :, lanes], held[c, "down"][z])
                    sig = jax.nn.sigmoid(gate)
                    silu = gate * sig
                    act_ref[c, r, :] = (silu * up).astype(bf16)
                    slope = sig * (1.0 + gate * (1.0 - sig))
                    dg_ref[c, r, :] = (d_act * up * slope).astype(bf16)
                    du_ref[c, r, :] = (d_act * silu).astype(bf16)

        def col_copy(z, slot):
            lanes = slice(z * part, (z + 1) * part)
            return [
                pltpu.make_async_copy(
                    cots[plane].at[:, lanes],
                    cot_cols.at[slot, pl.ds(plane * length, length), :],
                    col_sem.at[slot, plane],
                )
                for plane in (0, 1)
            ]

        def grad(c):
            for source, where in ((act_ref, 2), (dg_ref, 0), (du_ref, 1)):
                xt[where] = jnp.transpose(source[c])
            for copy in col_copy(0, 0):
                copy.start()
            for z in range(shard_size):
                lanes = slice(z * part, (z + 1) * part)
                if z + 1 < shard_size:
                    for copy in col_copy(z + 1, (z + 1) % 2):
                        copy.start()
                for which in (0, 1):
                    total = dot_nn(xt[which, :, :length], tok_ref[:, lanes])
                    total += dot_nn(xt[which, :, length:], tok2[:, lanes])
                    grads[3 * c + which][z] = total.astype(bf16)
                for copy in col_copy(z, z % 2):
                    copy.wait()
                grads[3 * c + 2][z] = dot_nn(xt[2], cot_cols[z % 2]).astype(bf16)

        def put_acts(these):
            for c in these:
                for ref, out in zip((act_ref, dg_ref, du_ref), acts_out):
                    outs.start(ref.at[c], out.at[c])

        def put_grads(c):
            for i in range(max(sums, 3 * c), 3 * c + 3):
                outs.start(grads[i], grads_out[i])

        sum_moves = [
            ShardExchange(shard_size, lambda j, g=g: g.at[j], out, sum_s.at[i], sum_r.at[i])
            for i, (g, out) in enumerate(zip(grads, sum_refs))
        ]

        row_copy(0, 0, 0).start()
        first_chunks = [c for c in range(chunks) if all((c, k) in early for k in ("gate", "up", "down"))]
        later_chunks = [c for c in range(chunks) if c not in first_chunks]
        for load in loads[: len(early)]:
            load.wait()
        tok_copy.wait()
        for move in late_moves:
            move.settle()
        stage(0, first_chunks, 0)
        row_copy(1, 0, 0).start()
        other.forwards()
        other.finish()
        stage(1, first_chunks, 0)
        put_acts(first_chunks)
        for c in first_chunks:
            grad(c)
            put_grads(c)
            for move in sum_moves[3 * c : 3 * c + 3]:
                move.start()
        if later_chunks:
            row_copy(0, 0, 0).start()
            for move in late_moves:
                move.wait_recv()
            for load in loads[len(early) :]:
                load.start()
            for load in loads[len(early) :]:
                load.wait()
            stage(0, later_chunks, 0)
            row_copy(1, 0, 0).start()
            stage(1, later_chunks, 0)
            put_acts(later_chunks)
            for c in later_chunks:
                grad(c)
                put_grads(c)
                for move in sum_moves[3 * c : 3 * c + 3]:
                    move.start()
        for move in late_moves:
            move.wait_send()
        for move in sum_moves:
            move.wait()
        outs.wait()

    piece = array((shard_size, block, part))
    act = array((chunks, 2 * length, block))
    late_shapes = [piece_shape(kind, shard_size, part, block) for _, kind in late]
    all_shapes = [piece_shape(kind, shard_size, part, block) for _, kind in pieces]
    outs = pl.pallas_call(
        kernel,
        name="mlp",
        out_shape=[act] * 3
        + [piece] * len(pieces)
        + [array(s) for s in late_shapes]
        + [piece] * sums,
        in_specs=in_vmem(1) + in_any(3 + len(early) + 3),
        out_specs=in_any(3 + len(pieces) + len(late) + sums),
        scratch_shapes=[
            VMEM((length, width), bf16),
            VMEM((2, big, width), bf16),
            VMEM((2, 2 * length, part), bf16),
            VMEM((3, block, 2 * length), bf16),
        ]
        + [VMEM(s, bf16) for s in all_shapes]
        + held([act] * 3 + [piece] * len(pieces))
        + [VMEM((length, width), bf16), DMA, DMA((3 * chunks + len(pieces),))]
        + [VMEM(s[1:], bf16) for s in late_shapes]
        + [DMA((max(1, len(late)),))]
        + [DMA((seq_size,))] * 2
        + [DMA((max(1, len(late)), shard_size))] * 2
        + [DMA((max(1, sums), shard_size))] * 2
        + [DMA((2,)), DMA((2, 2)), DMA((len(pieces),))],
        compiler_params=kernel_params(2),
    )(tok_other, tok, cot, cot_other, *pieces_in, *mlp_weights)
    outs = list(outs)
    first = 3 + len(pieces)
    second = first + len(late)
    return outs[:3], outs[3:first], outs[first:second], outs[second:]


def mlp_back(d_gate, d_up, gate, up, hidden, cot, gains_all, grads):
    seq_size, shard_size = lax.axis_size("seq"), lax.axis_size("shard")
    rows, width = hidden.shape
    chunks = len(gate)
    length = rows * seq_size
    part = width // shard_size
    count = len(grads)
    shared = length > 2048

    def kernel(*refs):
        take = Refs(refs)
        sources = take(2 + 2 * chunks)
        hidden_ref, cot_ref, gains_ref = take(3)
        grad_refs = take(count)
        d_hidden_ref, d_gain_ref, d_attn_all = take(3)
        sum_refs = take(count)
        terms = take(1 if shared else 2)
        arrived = take(2)
        scatter_sems = [take(2), take(2)]
        other_ref, swap_ref, d_attn_ref = take(3)
        ns, nr, swap_sem, own_sem, sum_s, sum_r = take(6)
        loaded, load_sems = take(2 + 2 * chunks), take(1)[0]
        bounces, bounce_sems = take(count), take(1)[0]
        dg_ref, du_ref = loaded[:2]
        gate_refs, up_refs = loaded[2 : 2 + chunks], loaded[2 + chunks :]
        loads = Moves(load_sems)
        for source, target in zip(sources, loaded):
            loads.start(source, target)

        me = lax.axis_index("seq")
        entry_barrier(seq_neighbours(seq_size), shard_size)
        moves = [
            ShardExchange(
                shard_size, lambda j, g=g: g.at[j], out, sum_s.at[i], sum_r.at[i], bounces[i],
                bounce_sems.at[i],
            )
            for i, (g, out) in enumerate(zip(grad_refs, sum_refs))
        ]
        for move in moves[:BEFORE]:
            move.start_outer()
        swap = PairSwap(other_ref, swap_ref, swap_sem).copy
        loads.wait()
        scatters = [
            SeqScatter(seq_size, terms[0 if shared else i], arrived[i], *scatter_sems[i])
            for i in range(2)
        ]

        def term(plane):
            scatter = scatters[plane]

            def compute(mask):
                tokens = scatter.tokens(mask, plane * length)
                for z in range(shard_size):
                    total = None
                    for c in range(chunks):
                        both = dot_nt(dg_ref[c, tokens, :], gate_refs[c][z])
                        both += dot_nt(du_ref[c, tokens, :], up_refs[c][z])
                        total = both if total is None else total + both
                    scatter.put(mask, slice(z * part, (z + 1) * part), total)

            return compute

        here, there = scatters
        there.send_terms(term(1), merge=True)
        if shared:
            there.merge_inner()
            there.merge(other_ref)
            swap.start()
            there.finish()
            here.send_terms(term(0), merge=True)
        else:
            here.send_terms(term(0))
            there.merge_inner()
            here.merge_leaves()
            there.merge(other_ref)
            swap.start()
        for move in moves:
            move.start_inner()
        for move in moves[BEFORE:]:
            move.start_outer()
        here.merge_inner()
        here.merge(d_hidden_ref)
        swap.wait()
        d_normed = d_hidden_ref[...] + swap_ref[...].astype(f32)
        values = hidden_ref[...]
        gain = jnp.concatenate([gains_ref[z, 1:2, :] for z in range(shard_size)], axis=1)
        d_values, d_gain = norm_back(values, inverse_rms(values), gain, d_normed)
        d_hidden = cot_ref[...].astype(f32) + d_values
        d_attn_ref[...] = d_hidden.astype(bf16)
        gather = SeqGather(seq_size, d_attn_all, rows, ns, nr, own=d_attn_ref)
        gather.start()
        for move in moves:
            move.settle()
        own = pltpu.make_async_copy(d_attn_ref, d_attn_all.at[rows_at(me, rows), :], own_sem)
        own.start()
        d_hidden_ref[...] = d_hidden
        d_gain_ref[...] = d_gain
        gather.forwards()
        own.wait()
        gather.finish()
        for scatter in scatters[: 1 if shared else 2]:
            scatter.finish()
        for move in moves:
            move.wait()

    scatter = scatter_scratch(seq_size, rows, width)
    inputs = [d_gate, d_up, *gate, *up]
    outs = pl.pallas_call(
        kernel,
        name="mlp_back",
        out_shape=[
            array((rows, width), f32),
            array((1, width), f32),
            array((length, width)),
        ]
        + [array(g.shape) for g in grads],
        in_specs=in_any(2 + 2 * chunks) + in_vmem(3) + in_any(count),
        out_specs=in_vmem(2) + in_any(1 + count),
        scratch_shapes=scatter[:1] * (1 if shared else 2)
        + scatter[1:2] * 2
        + [DMA((seq_size,))] * 4
        + [VMEM((rows, width), bf16)] * 3
        + [DMA((seq_size,))] * 2
        + [DMA((2,)), DMA]
        + [DMA((max(1, count), shard_size))] * 2
        + held(inputs)
        + [DMA((len(inputs),))]
        + [VMEM(g.shape[1:], bf16) for g in grads]
        + [DMA((max(1, count),))],
        compiler_params=kernel_params(3),
    )(*inputs, hidden, cot, gains_all, *grads)
    return outs[:3], list(outs[3:])


class OutputSum:
    def __init__(self, scatter, act, down_refs, base=0):
        self.scatter, self.act, self.down_refs, self.base = scatter, act, down_refs, base

    def compute(self, mask):
        tokens = self.scatter.tokens(mask, self.base)
        shards, _, part = self.down_refs[0].shape
        for z in range(shards):
            total = None
            for c, down in enumerate(self.down_refs):
                one = dot_nn(self.act[c, tokens, :], down[z])
                total = one if total is None else total + one
            self.scatter.put(mask, slice(z * part, (z + 1) * part), total)


def attend_back(d_attn, wo, mixed, q, k, v, lse, table, normed, grads, activ, down):
    seq_size, shard_size = lax.axis_size("seq"), lax.axis_size("shard")
    length, width = d_attn.shape
    rows = length // seq_size
    cols = q.shape[1]
    part = wo.shape[2]
    big = row_step(length, 512)
    block = row_step(length, 256)
    scale = 1.0 / math.sqrt(HD)
    pair = 2 * HD
    count = len(grads)
    chunks = len(down)

    def kernel(*refs):
        take = Refs(refs)
        sources = take(9 + chunks)
        grad_refs = take(count)
        act_all = take(1)[0] if chunks else None
        dq_ref, dk_ref, dv_ref, gq_ref, gk_ref, gv_ref = take(6)
        if chunks:
            swap_ref = take(1)[0]
        sum_refs = take(count + 1)
        do_ref, kt_ref, dk_acc, dv_acc, xt_ref, go_ref, sum_s, sum_r = take(8)
        loaded, load_sems = take(9 + chunks), take(1)[0]
        bounces, bounce_sems = take(count), take(1)[0]
        da_ref, wo_ref, mixed_ref, q_ref, k_ref, v_ref, lse_ref, t_ref, n_ref = loaded[:9]
        down_refs = loaded[9:]
        loads = Moves(load_sems)
        first = list(range(9, 9 + chunks)) + [0, 2]
        for i in first + [1, 3, 4, 5, 6, 7, 8]:
            loads.start(sources[i], loaded[i])

        if chunks:
            terms, arrived, ss, sr, act_ref, other_ref, act_sem, swap_sem = take(8)
            act_copy = pltpu.make_async_copy(
                act_all.at[:, pl.ds(length, length), :], act_ref, act_sem
            )
            act_copy.start()
        entry_barrier(seq_neighbours(seq_size) if chunks else [], shard_size)
        moves = [
            ShardExchange(
                shard_size, lambda j, g=g: g.at[j], out, sum_s.at[i], sum_r.at[i], bounce,
                bounce_sems.at[i],
            )
            for i, (g, out, bounce) in enumerate(
                zip(grad_refs + [go_ref], sum_refs, bounces + [None])
            )
        ]
        for move in moves[:-1]:
            move.start_outer()
        if chunks:
            swap = PairSwap(other_ref, swap_ref, swap_sem).copy
            act_copy.wait()
            loads.wait(chunks)
            out_sum = OutputSum(SeqScatter(seq_size, terms, arrived, ss, sr), act_ref, down_refs)
            out_sum.scatter.send_terms(out_sum.compute, merge=True)

        loads.wait(2)
        xt_ref[...] = jnp.transpose(mixed_ref[...])
        for z in range(shard_size):
            go_ref[z] = dot_nn(xt_ref[...], da_ref[:, z * part : (z + 1) * part]).astype(bf16)
        moves[-1].start_outer()
        loads.wait(6)

        @pl.loop(0, length // big)
        def _(i):
            r = rows_at(i, big)
            total = dot_nt(da_ref[r, :part], wo_ref[0])
            for z in range(1, shard_size):
                total += dot_nt(da_ref[r, z * part : (z + 1) * part], wo_ref[z])
            do_ref[r, :] = total.astype(bf16)

        kt_ref[...] = jnp.transpose(k_ref[...])
        for move in moves:
            move.settle()
        if chunks:
            out_sum.scatter.merge_inner()

        def heads(hp, lanes):
            dk_acc[...] = jnp.zeros_like(dk_acc)
            dv_acc[...] = jnp.zeros_like(dv_acc)
            for i in range(length // block):
                first, last = i * block, (i + 1) * block
                q2 = q_ref[first:last, lanes]
                do2 = do_ref[first:last, lanes]
                keys = k_ref[:last, lanes]
                values = v_ref[:last, lanes]
                dqt, dk_add, dv_add = None, None, None
                for head in (0, 1):
                    keep = head_lanes(head, q2.shape)
                    qm = jnp.where(keep, q2, jnp.zeros_like(q2))
                    dom = jnp.where(keep, do2, jnp.zeros_like(do2))
                    st = dot_nt(keys, qm)
                    row = lse_ref[pl.ds(hp * 2 + head, 1), first:last]
                    p = jnp.exp(st - row)
                    r = lax.broadcasted_iota(jnp.int32, (block, block), 0)
                    c = lax.broadcasted_iota(jnp.int32, (block, block), 1)
                    tail = jnp.where(r <= c, p[first:], 0.0)
                    p = tail if i == 0 else jnp.concatenate([p[:first], tail], axis=0)
                    dp = dot_nt(values, dom)
                    inner = jnp.sum(dp * p, axis=0, keepdims=True)
                    ds = (p * (dp - inner)).astype(bf16)
                    dv_one = dot_nn(p.astype(bf16), dom)
                    dk_one = dot_nn(ds, qm)
                    dv_add = dv_one if head == 0 else dv_add + dv_one
                    dk_add = dk_one if head == 0 else dk_add + dk_one
                    dqt_one = dot_nn(kt_ref[lanes, :last], ds)
                    if head == 0:
                        dqt = dqt_one
                    else:
                        sub = lax.broadcasted_iota(jnp.int32, dqt.shape, 0)
                        dqt = jnp.where(sub < HD, dqt, dqt_one)
                dk_acc[:last, :] += dk_add
                dv_acc[:last, :] += dv_add
                dq = (jnp.transpose(dqt) * scale).astype(bf16).astype(f32)
                dq_ref[first:last, lanes] = turn(dq, t_ref[first:last, :], True).astype(bf16)
            dv_ref[:, lanes] = dv_acc[...].astype(bf16)

            @pl.loop(0, length // big)
            def _(i):
                r = rows_at(i, big)
                dk = dk_acc[r, :].astype(bf16).astype(f32)
                dk_ref[r, lanes] = turn(dk, t_ref[r, :], True).astype(bf16)

        if chunks:
            for hp in range(cols // pair):
                heads(hp, slice(hp * pair, (hp + 1) * pair))
                if hp == 0:
                    out_sum.scatter.merge(other_ref)
                    swap.start()
                    for move in moves:
                        move.start_inner()
        else:
            for move in moves:
                move.start_inner()

            @pl.loop(0, cols // pair)
            def _(hp):
                heads(hp, rows_at(hp, pair))

        loads.wait()
        for source, out in ((dq_ref, gq_ref), (dk_ref, gk_ref), (dv_ref, gv_ref)):
            xt_ref[...] = jnp.transpose(source[...])
            for z in range(shard_size):
                out[z] = dot_nn(xt_ref[...], n_ref[:, z * part : (z + 1) * part]).astype(bf16)
        if chunks:
            swap.wait()
            out_sum.scatter.finish()
        for move in moves:
            move.wait()

    grad = array((shard_size, cols, part))
    scratch = [
        VMEM((length, cols), bf16),
        VMEM((cols, length), bf16),
        VMEM((length, pair), f32),
        VMEM((length, pair), f32),
        VMEM((cols, length), bf16),
        VMEM((shard_size, cols, part), bf16),
    ] + [DMA((count + 1, shard_size))] * 2
    inputs = [d_attn, wo, mixed, q, k, v, lse, table, normed, *down]
    scratch += held(inputs) + [DMA((len(inputs),))]
    scratch += [VMEM(g.shape[1:], bf16) for g in grads] + [DMA((count + 1,))]
    if chunks:
        scratch += scatter_scratch(seq_size, rows, width)
        scratch += [VMEM((chunks, length, activ.shape[2]), bf16), VMEM((rows, width), bf16)]
        scratch += [DMA, DMA((2,))]
    outs = pl.pallas_call(
        kernel,
        name="attend_back",
        out_shape=[array((length, cols))] * 3
        + [grad] * 3
        + [array((rows, width))] * (1 if chunks else 0)
        + [array(g.shape) for g in grads]
        + [grad],
        in_specs=in_any(9 + chunks + count + (1 if chunks else 0)),
        out_specs=in_vmem(7 if chunks else 6) + in_any(count + 1),
        scratch_shapes=scratch,
        compiler_params=kernel_params(4),
    )(*inputs, *grads, *([activ] if chunks else []))
    outs = list(outs)
    other = outs.pop(6) if chunks else None
    return outs[:3], outs[3:6], other, outs[6:]


def output_parts(activ, down, hidden):
    seq_size, shard_size = lax.axis_size("seq"), lax.axis_size("shard")
    rows, width = hidden.shape
    length = rows * seq_size
    chunks = len(down)

    def kernel(*refs):
        take = Refs(refs)
        act_ref, hidden_ref = take(2)
        down_refs = take(chunks)
        out_ref, terms, first, second = take(4)
        sems = [take(2), take(2)]
        total_ref, other_ref, swap_ref, swap_sem = take(4)
        entry_barrier(seq_neighbours(seq_size), shard_size)
        there, here = (
            OutputSum(SeqScatter(seq_size, terms, arrived, *sem), act_ref, down_refs, base)
            for arrived, sem, base in ((first, sems[0], length), (second, sems[1], 0))
        )
        there.scatter.run(there.compute, other_ref)
        swap = PairSwap(other_ref, swap_ref, swap_sem).copy
        swap.start()
        there.scatter.finish()
        here.scatter.run(here.compute, total_ref)
        swap.wait()
        out_ref[...] = (total_ref[...] + swap_ref[...].astype(f32) + hidden_ref[...]).astype(bf16)
        here.scatter.finish()

    scatter = scatter_scratch(seq_size, rows, width)
    return pl.pallas_call(
        kernel,
        name="output_parts",
        out_shape=array((rows, width)),
        in_specs=in_vmem(2 + chunks),
        out_specs=in_vmem(1)[0],
        scratch_shapes=scatter[:2]
        + scatter[1:2]
        + [DMA((seq_size,))] * 4
        + [VMEM((rows, width), f32), VMEM((rows, width), bf16), VMEM((rows, width), bf16)]
        + [DMA((2,))],
        compiler_params=kernel_params(6),
    )(activ, hidden, *down)


def finish(
    d_qkv, attn_weights, g_qkv, x, d_hidden, gains_all, d_gain_two, sums, g_output, block,
    output_of,
):
    seq_size, shard_size = lax.axis_size("seq"), lax.axis_size("shard")
    rows, width = x.shape
    part = width // shard_size
    cols = d_qkv[0].shape[1]
    length = rows * seq_size
    pieces = len(sums)
    half = pieces // 3 * block
    activ, down, hidden, other = output_of or (None, [], None, None)
    chunks = len(down)
    pairs = shard_size // 2

    def kernel(*refs):
        take = Refs(refs)
        x_ref, d_hidden_ref, gains_ref, gain2_ref = take(4)
        sources = take(9 + chunks)
        hidden_ref, other_ref = take(2) if chunks else (None, None)
        act_all = take(1)[0] if chunks else None
        sum_refs, go_ref = take(pieces), take(1)[0]
        d_inputs_ref, gain_ref = take(2)
        qkv_refs = take(3)
        output_ref = take(1)[0] if chunks else None
        wo_ref, wg_ref, wu_ref, wd_ref = take(4)
        total_ref, gain_mine, gain_shards, gain_line, gain_seq = take(5)
        gs, gr, hs, hr = take(4)
        in_terms, in_arrived, in_s, in_r = take(4)
        firsts, middles, seconds, reduce_sems = take(4)
        received, wide, tall, load_sem, store_sem = take(5)
        loaded, in_sems = take(9 + chunks), take(1)[0]
        d_refs, w_refs, g_refs = loaded[:3], loaded[3:6], loaded[6:9]
        down_refs = loaded[9:]
        ins = Moves(in_sems)
        for i in [6, 7, 8, 0, 1, 2, 3, 4, 5] + list(range(9, 9 + chunks)):
            ins.start(sources[i], loaded[i])
        if chunks:
            out_terms, out_arrived, out_s, out_r, act_ref, act_sem, out_total = take(7)
            act_copy = pltpu.make_async_copy(act_all.at[:, pl.ds(0, length), :], act_ref, act_sem)
            act_copy.start()

        me = lax.axis_index("seq")
        entry_barrier(range(1, seq_size), shard_size)
        reduces = [
            PairReduce(
                shard_size, g_refs[i], firsts.at[i], middles.at[i], seconds.at[i], reduce_sems.at[i]
            )
            for i in range(3)
        ]
        ins.wait(3)
        for reduce in reduces:
            reduce.start()
        ins.wait(6)
        in_sum = SeqScatter(seq_size, in_terms, in_arrived, in_s, in_r)

        def inputs_term(mask):
            tokens = in_sum.tokens(mask)
            for z in range(shard_size):
                total = None
                for d_ref, w_ref in zip(d_refs, w_refs):
                    term = dot_nt(d_ref[tokens, :], w_ref[z])
                    total = term if total is None else total + term
                in_sum.put(mask, slice(z * part, (z + 1) * part), total)

        in_sum.send_terms(inputs_term, merge=True)
        if chunks:
            act_copy.wait()
            ins.wait()
            out_sum = OutputSum(
                SeqScatter(seq_size, out_terms, out_arrived, out_s, out_r), act_ref, down_refs
            )
            out_sum.scatter.send_terms(out_sum.compute)

        loads = [
            pltpu.make_async_copy(source, received.at[i % 2], load_sem.at[i % 2])
            for i, source in enumerate(sum_refs)
        ]
        stores = []

        def store(staging, target, value):
            turn_of = sum(1 for s in stores if s[0] is staging)
            slot = turn_of % 2
            sem = store_sem.at[0 if staging is wide else 1, slot]
            if turn_of >= 2:
                [s for s in stores if s[0] is staging][-2][1].wait()
            staging[slot] = value.astype(bf16)
            copy = pltpu.make_async_copy(staging.at[slot], target, sem)
            copy.start()
            stores.append((staging, copy))

        def collect(i):
            if i + 1 < pieces:
                loads[i + 1].start()
            loads[i].wait()
            for parity in (0, 1):
                total = received[i % 2, parity].astype(f32)
                for p in range(1, pairs):
                    total = total + received[i % 2, 2 * p + parity].astype(f32)
                start = parity * half + i // 3 * block
                if i % 3 == 2:
                    store(wide, wd_ref.at[start : start + block, :], total)
                else:
                    target = (wg_ref, wu_ref)[i % 3]
                    store(tall, target.at[:, start : start + block], jnp.transpose(total))

        loads[0].start()
        third = (pieces + 2) // 3
        in_sum.merge_inner()
        reduces[0].middle()
        if chunks:
            out_sum.scatter.merge_leaves()
        for i in range(third):
            collect(i)
        reduces[1].middle()
        in_sum.merge(total_ref)
        values = x_ref[...].astype(f32)
        gain = jnp.concatenate([gains_ref[z, 0:1, :] for z in range(shard_size)], axis=1)
        d_values, d_gain = norm_back(values, inverse_rms(values), gain, total_ref[...])
        d_inputs_ref[...] = (d_hidden_ref[...] + d_values).astype(bf16)
        for z in range(shard_size):
            lanes = slice(z * part, (z + 1) * part)
            gain_mine[z, 0:1, :] = d_gain[:, lanes]
            gain_mine[z, 1:2, :] = gain2_ref[0:1, lanes]
            gain_mine[z, 2:, :] = jnp.zeros((6, part), f32)
        line = ShardExchange(shard_size, lambda j: gain_mine.at[j], gain_shards, gs, gr)
        line.start()
        for i in range(third, 2 * third):
            collect(i)
        reduces[2].middle()
        if chunks:
            out_sum.scatter.merge_inner()
        line.wait()
        gain_line[...] = sum(gain_shards[z] for z in range(shard_size))

        def to_seq(step):
            return pltpu.make_async_remote_copy(
                src_ref=gain_line,
                dst_ref=gain_seq.at[step],
                send_sem=hs.at[step],
                recv_sem=hr.at[step],
                device_id={"seq": jnp.bitwise_xor(me, step)},
                device_id_type=MESH,
            )

        for step in range(1, seq_size):
            to_seq(step).start()
        for i in range(2 * third, pieces):
            collect(i)
        wo_ref[...] = sum(go_ref[z].astype(f32) for z in range(shard_size)).astype(bf16)
        if chunks:
            out_sum.scatter.merge(out_total)
            output_ref[...] = (
                out_total[...] + other_ref[...].astype(f32) + hidden_ref[...]
            ).astype(bf16)
        for reduce, out in zip(reduces, qkv_refs):
            out[...] = jnp.transpose(reduce.total()).astype(bf16)
        for step in range(1, seq_size):
            to_seq(step).wait()
        gain_ref[...] = gain_line[...] + sum(gain_seq[step] for step in range(1, seq_size))
        for staging in (wide, tall):
            for _, copy in [s for s in stores if s[0] is staging][-2:]:
                copy.wait()
        for reduce in reduces:
            reduce.finish()
        in_sum.finish()
        if chunks:
            out_sum.scatter.finish()

    scratch = [
        VMEM((rows, width), f32),
        VMEM((shard_size, 8, part), f32),
        VMEM((shard_size, 8, part), f32),
        VMEM((8, part), f32),
        VMEM((seq_size, 8, part), f32),
    ]
    scratch += [DMA((shard_size,))] * 2 + [DMA((seq_size,))] * 2
    scratch += scatter_scratch(seq_size, rows, width)
    scratch += [VMEM((3, pairs, cols, part), bf16)] * 3 + [DMA((3, 4, pairs))]
    scratch += [
        VMEM((2, shard_size, block, part), bf16),
        VMEM((2, block, part), bf16),
        VMEM((2, part, block), bf16),
        DMA((2,)),
        DMA((2, 2)),
    ]
    inputs = [*d_qkv, *attn_weights, *g_qkv, *down]
    scratch += held(inputs) + [DMA((len(inputs),))]
    if chunks:
        scratch += scatter_scratch(seq_size, rows, width)
        scratch += [VMEM((chunks, length, block), bf16), DMA, VMEM((rows, width), f32)]
    extra = 1 if chunks else 0
    units = 2 * half
    outs = pl.pallas_call(
        kernel,
        name="finish",
        out_shape=[array((rows, width)), array((8, part), f32)]
        + [array((part, cols))] * 3
        + [array((rows, width))] * extra
        + [array((cols, part))]
        + [array((part, units))] * 2
        + [array((units, part))],
        in_specs=in_vmem(4)
        + in_any(9 + chunks)
        + in_vmem(2 * extra)
        + in_any(extra + pieces)
        + in_vmem(1),
        out_specs=in_vmem(6 + extra) + in_any(3),
        scratch_shapes=scratch,
        compiler_params=kernel_params(5),
    )(
        x, d_hidden, gains_all, d_gain_two, *inputs,
        *([hidden, other, activ] if chunks else []), *sums, g_output,
    )
    outs = list(outs)
    output = outs.pop(5) if chunks else None
    return outs, output


def widen(rows, grads, gains):
    part = gains.shape[1]

    def kernel(*refs):
        take = Refs(refs)
        grad_refs, row_refs, gain_ref = take(len(grads)), take(len(rows)), take(1)[0]
        row_outs, grad_outs, gain_outs = take(len(rows)), take(len(grads)), take(2)
        low, high, load_sems, store_sems = take(len(grads)), take(len(grads)), *take(2)
        loads, stores = Moves(load_sems), Moves(store_sems)
        for source, target in zip(grad_refs, low):
            loads.start(source, target)
        for source, target in zip(row_refs, row_outs):
            target[...] = source[...]
        for i, out in enumerate(gain_outs):
            out[...] = gain_ref[i : i + 1, :]
        for a, b, out in zip(low, high, grad_outs):
            loads.wait(1)
            b[...] = a[...].astype(f32)
            stores.start(b, out)
        stores.wait()

    wide = [array(g.shape, f32) for g in grads]
    return pl.pallas_call(
        kernel,
        name="widen",
        out_shape=[array(r.shape) for r in rows] + wide + [array((1, part), f32)] * 2,
        in_specs=in_any(len(grads)) + in_vmem(len(rows) + 1),
        out_specs=in_vmem(len(rows)) + in_any(len(grads)) + in_vmem(2),
        scratch_shapes=held(grads) + held(wide) + [DMA((len(grads),)), DMA((len(grads),))],
        compiler_params=kernel_params(),
    )(*grads, *rows, gains)


def rotation_table(position_ids):
    half = HD // 2
    freqs = theta_base ** (-(jnp.arange(half, dtype=f32) * 2.0) / HD)
    angles = position_ids.astype(f32)[:, None] * freqs[None, :]
    cosine, sine = jnp.cos(angles), jnp.sin(angles)
    return jnp.concatenate([cosine, cosine, -sine, sine], axis=1)


EARLY = 4
AHEAD = 4
BEFORE = 2
SUMS = (1, 4)
START = 3


def body(
    inputs,
    positions,
    attn_gain,
    w_query,
    w_key,
    w_value,
    w_output,
    mlp_gain,
    w_gate,
    w_up,
    w_down,
    cotangent,
):
    shard_size = lax.axis_size("shard")
    x, cot = inputs[0], cotangent[0]
    gains = jnp.pad(jnp.stack([attn_gain, mlp_gain]).astype(f32), ((0, 6), (0, 0)))
    table = rotation_table(positions[0])
    half = w_gate.shape[1] // 2
    block = row_step(half, 256)
    chunks = half // block
    pieces = weight_pieces(chunks)
    early, late = pieces[:EARLY], pieces[EARLY:]
    mlp_weights = (w_gate, w_up, w_down)
    held, early_weights = forward(
        x, gains, table, cot, (w_query, w_key, w_value, w_output), mlp_weights, early, block
    )
    normed, tables, gains_all, wq, wk, wv, wo, q, k, v, mixed, lse, hidden = held[:13]
    cot_all, cot_other, tok, tok_other = held[13:]
    acts, grads, late_weights, sums = mlp(
        tok, tok_other, cot_all, cot_other, early_weights, mlp_weights, late, chunks, block,
        min(SUMS[0], len(pieces)),
    )
    activ, d_gate, d_up = acts
    weights = dict(zip(pieces, early_weights + late_weights))

    def kind(name):
        return [weights[c, name] for c in range(chunks)]

    done = len(sums)
    more = min(SUMS[1], len(pieces) - done)
    (d_hidden, d_gain_two, d_attn), moved = mlp_back(
        d_gate, d_up, kind("gate"), kind("up"), hidden, cot, gains_all, grads[done : done + more]
    )
    sums += moved
    done += more
    down = kind("down")
    together = tok.shape[0] <= 2048
    d_qkv, g_qkv, other, moved = attend_back(
        d_attn, wo, mixed, q, k, v, lse, tables, normed, grads[done:], activ,
        down if together else [],
    )
    sums += moved[:-1]
    results, output = finish(
        d_qkv, (wq, wk, wv), g_qkv, x, d_hidden, gains_all, d_gain_two, sums, moved[-1], block,
        (activ, down, hidden, other) if together else None,
    )
    if not together:
        output = output_parts(activ, down, hidden)
    d_inputs, gain_sums, *grads = results
    output, d_inputs, *grads, gain_one, gain_two = widen([output, d_inputs], grads, gain_sums)
    return (
        output[None],
        d_inputs[None],
        gain_one.reshape(-1),
        *grads[:4],
        gain_two.reshape(-1),
        *grads[4:],
    )


def solution(mesh):
    in_specs = (
        P("shard", "seq", None),
        P("shard", "seq"),
        P("shard"),
        P("shard", "seq"),
        P("shard", "seq"),
        P("shard", "seq"),
        P("seq", "shard"),
        P("shard"),
        P("shard", "seq"),
        P("shard", "seq"),
        P("seq", "shard"),
        P("shard", "seq", None),
    )
    out_specs = (
        P("shard", "seq", None),
        P("shard", "seq", None),
        P("shard"),
        P("shard", "seq"),
        P("shard", "seq"),
        P("shard", "seq"),
        P("seq", "shard"),
        P("shard"),
        P("shard", "seq"),
        P("shard", "seq"),
        P("seq", "shard"),
    )
    return jax.shard_map(body, mesh=mesh, in_specs=in_specs, out_specs=out_specs, check_vma=False)
```

```python
import math

import jax
import jax.numpy as jnp
from jax import lax
from jax.experimental import pallas as pl
from jax.experimental.pallas import tpu as pltpu
from jax.sharding import PartitionSpec as P

HD = 64
epsilon = 1e-05
theta_base = 130000.0
bf16 = jnp.bfloat16
f32 = jnp.float32
VMEM = pltpu.VMEM
DMA = pltpu.SemaphoreType.DMA
MESH = pl.DeviceIdType.MESH


def dot_nn(a, b):
    return jnp.dot(a, b, preferred_element_type=f32)


def dot_nt(a, b):
    return lax.dot_general(a, b, (((1,), (1,)), ((), ())), preferred_element_type=f32)


def in_vmem(count):
    return [pl.BlockSpec(memory_space=VMEM)] * count


def in_any(count):
    return [pl.BlockSpec(memory_space=pl.ANY)] * count


def array(shape, dtype=bf16):
    return jax.ShapeDtypeStruct(shape, dtype)


def kernel_params(collective_id=None, limit=62):
    if collective_id is None:
        return pltpu.CompilerParams(vmem_limit_bytes=limit << 20)
    return pltpu.CompilerParams(
        collective_id=collective_id, has_side_effects=True, vmem_limit_bytes=limit << 20
    )


def popcount(mask):
    return bin(mask).count("1")


def chip_masks(size):
    return sorted(range(0, size, 2), key=lambda m: (popcount(m), m))


def chip_bits(size):
    return [1 << b for b in range(1, size.bit_length() - 1)]


def last_hop(mask, core):
    set_bits = [1 << b for b in range(1, mask.bit_length()) if mask >> b & 1]
    return set_bits[-1] if core == 0 else set_bits[0]


def further_masks(mask, core, size):
    return [
        mask | hop
        for hop in chip_bits(size)
        if not mask & hop and last_hop(mask | hop, core) == hop
    ]


def seq_neighbours(size):
    return [1] + chip_bits(size)


def entry_barrier(seq_masks, shard_size):
    barrier = pltpu.get_barrier_semaphore()
    me, mine = lax.axis_index("seq"), lax.axis_index("shard")
    for mask in seq_masks:
        pl.semaphore_signal(
            barrier, inc=1, device_id={"seq": jnp.bitwise_xor(me, mask)}, device_id_type=MESH
        )
    for step in range(1, shard_size):
        pl.semaphore_signal(
            barrier, inc=1, device_id={"shard": lax.rem(mine + step, shard_size)},
            device_id_type=MESH,
        )
    pl.semaphore_wait(barrier, len(seq_masks) + max(shard_size - 1, 0))


class SeqGather:
    def __init__(self, size, out, rows, send_sem, recv_sem, own=None):
        self.size, self.out, self.rows = size, out, rows
        self.send_sem, self.recv_sem = send_sem, recv_sem
        self.me = lax.axis_index("seq")
        self.core = lax.rem(self.me, 2)
        self.own = own

    def block(self, index):
        return self.out.at[pl.ds(pl.multiple_of(index * self.rows, self.rows), self.rows), :]

    def copy(self, arrives, hop):
        block = self.block(jnp.bitwise_xor(self.me, arrives ^ hop))
        src = self.own if arrives == hop and self.own is not None else block
        return pltpu.make_async_remote_copy(
            src_ref=src,
            dst_ref=block,
            send_sem=self.send_sem.at[arrives],
            recv_sem=self.recv_sem.at[arrives],
            device_id={"seq": jnp.bitwise_xor(self.me, hop)},
            device_id_type=MESH,
        )

    def wait_recv(self, mask):
        block = self.block(jnp.bitwise_xor(self.me, mask))
        pltpu.make_async_remote_copy(
            src_ref=block,
            dst_ref=block,
            send_sem=self.send_sem.at[mask],
            recv_sem=self.recv_sem.at[mask],
            device_id={"seq": jnp.bitwise_xor(self.me, 1)},
            device_id_type=MESH,
        ).wait_recv()

    def start(self):
        for hop in reversed(seq_neighbours(self.size)):
            self.copy(hop, hop).start()

    def forward(self, mask):
        self.wait_recv(mask)
        for core in (0, 1):
            for more in further_masks(mask, core, self.size):

                @pl.when(self.core == core)
                def _():
                    self.copy(more, more ^ mask).start()

        self.copy(mask | 1, 1).start()

    def forwards(self):
        for mask in chip_masks(self.size)[1:]:
            self.forward(mask)

    def finish(self):
        for mask in chip_masks(self.size):
            self.wait_recv(mask | 1)
        for mask in range(1, self.size):
            self.copy(mask, 1 if mask & 1 else mask & -mask).wait_send()


def height(mask, core, size):
    return max([0] + [1 + height(m, core, size) for m in further_masks(mask, core, size)])


class SeqScatter:
    def __init__(self, size, terms, arrived, send_sem, recv_sem):
        self.size, self.terms, self.arrived = size, terms, arrived
        self.send_sem, self.recv_sem = send_sem, recv_sem
        self.me = lax.axis_index("seq")
        self.core = lax.rem(self.me, 2)
        self.masks = chip_masks(size)[::-1]
        self.order = [
            sorted(self.masks, key=lambda m: (height(m, core, size), -popcount(m)))
            for core in (0, 1)
        ]
        self.leaves = size // 4
        self.merged = 0

    def copy(self, mask, hop):
        core = 1 - self.core if mask & 1 else self.core
        return pltpu.make_async_remote_copy(
            src_ref=self.terms.at[mask // 2, core],
            dst_ref=self.arrived.at[mask - 1],
            send_sem=self.send_sem.at[mask],
            recv_sem=self.recv_sem.at[mask],
            device_id={"seq": jnp.bitwise_xor(self.me, hop)},
            device_id_type=MESH,
        )

    def tokens(self, mask, base=0):
        pair = 2 * self.terms.shape[2]
        start = jnp.bitwise_xor(self.me, mask) // 2 * pair + base
        return pl.ds(pl.multiple_of(start, pair), pair)

    def put(self, mask, lanes, total):
        rows = self.terms.shape[2]
        self.terms[mask // 2, :, :, lanes] = total.astype(bf16).reshape(2, rows, -1)

    def add(self, mask, source, write):
        rows = self.terms.shape[2]
        step = 32 if rows % 32 == 0 else 16

        @pl.loop(0, rows // step)
        def _(i):
            part = pl.ds(pl.multiple_of(i * step, step), step)
            total = self.terms[mask // 2, self.core, part, :].astype(f32)
            for s in source:
                total = total + self.arrived[s - 1, part, :].astype(f32)
            write(part, total)

    def merge(self, result=None):
        for core in (0, 1):
            mask = self.order[core][self.merged]
            further = further_masks(mask, core, self.size)

            def keep(part, total, mask=mask):
                if mask:
                    self.terms[mask // 2, self.core, part, :] = total.astype(bf16)
                else:
                    result[part, :] = total.astype(result.dtype)

            @pl.when(self.core == core)
            def _(mask=mask, further=further, keep=keep, core=core):
                for m in [mask | 1] + further:
                    self.copy(m, 1).wait_recv()
                self.add(mask, [mask | 1] + further, keep)
                if mask:
                    self.copy(mask, last_hop(mask, core)).start()

        self.merged += 1

    def send_terms(self, compute, merge=False):
        done = set()
        for mask in self.masks:
            compute(mask)
            self.copy(mask | 1, 1).start()
            if merge and self.merged < self.leaves:
                if all(order[self.merged] in done for order in self.order):
                    self.merge()
            done.add(mask)
        if merge:
            self.merge_leaves()

    def merge_leaves(self):
        while self.merged < self.leaves:
            self.merge()

    def merge_inner(self):
        while self.merged < len(self.masks) - 1:
            self.merge()

    def run(self, compute, result):
        self.send_terms(compute, merge=True)
        self.merge_inner()
        self.merge(result)

    def finish(self):
        for mask in range(1, self.size):
            self.copy(mask, 1).wait_send()


def scatter_scratch(seq_size, rows, width):
    return [
        VMEM((seq_size // 2, 2, rows, width), bf16),
        VMEM((seq_size - 1, rows, width), bf16),
        DMA((seq_size,)),
        DMA((seq_size,)),
    ]


class LineGather:
    def __init__(self, size, own, out, send_sem, recv_sem, copy_sem):
        self.size, self.own, self.out = size, own, out
        self.send_sem, self.recv_sem, self.copy_sem = send_sem, recv_sem, copy_sem
        self.k = lax.axis_index("shard")

    def sent(self, way, step):
        block = self.k - step if way == 0 else self.k + step
        valid = (
            jnp.logical_and(self.k < self.size - 1, block >= 0)
            if way == 0
            else jnp.logical_and(self.k > 0, block <= self.size - 1)
        )
        safe = jnp.clip(block, 0, self.size - 1)
        target = jnp.clip(self.k + 1 if way == 0 else self.k - 1, 0, self.size - 1)
        return valid, pltpu.make_async_remote_copy(
            src_ref=self.own if step == 0 else self.out.at[safe],
            dst_ref=self.out.at[safe],
            send_sem=self.send_sem.at[way, step],
            recv_sem=self.recv_sem.at[way, step],
            device_id={"shard": target},
            device_id_type=MESH,
        )

    def received(self, way, step):
        block = self.k - 1 - step if way == 0 else self.k + 1 + step
        valid = block >= 0 if way == 0 else block <= self.size - 1
        safe = jnp.clip(block, 0, self.size - 1)
        return valid, pltpu.make_async_remote_copy(
            src_ref=self.own,
            dst_ref=self.out.at[safe],
            send_sem=self.send_sem.at[way, step],
            recv_sem=self.recv_sem.at[way, step],
            device_id={"shard": lax.rem(self.k + 1, self.size)},
            device_id_type=MESH,
        )

    def local(self):
        return pltpu.make_async_copy(self.own, self.out.at[self.k], self.copy_sem)

    def step(self, step):
        if step == 0:
            self.local().start()
        if step == self.size - 1:
            self.local().wait()
        for way in (0, 1):
            if step > 0:
                valid, copy = self.received(way, step - 1)

                @pl.when(valid)
                def _():
                    copy.wait_recv()

            if step < self.size - 1:
                valid, copy = self.sent(way, step)

                @pl.when(valid)
                def _():
                    copy.start()

    def finish(self):
        for step in range(self.size - 1):
            for way in (0, 1):
                valid, copy = self.sent(way, step)

                @pl.when(valid)
                def _():
                    copy.wait_send()


class ShardExchange:
    def __init__(self, size, source, out, send_sem, recv_sem, bounce=None, bounce_sem=None):
        self.size, self.source, self.out = size, source, out
        self.send_sem, self.recv_sem = send_sem, recv_sem
        self.bounce, self.bounce_sem = bounce, bounce_sem
        self.k = lax.axis_index("shard")

    def copy(self, step):
        target = lax.rem(self.k + step, self.size)
        return pltpu.make_async_remote_copy(
            src_ref=self.source(target),
            dst_ref=self.out.at[self.k],
            send_sem=self.send_sem.at[step],
            recv_sem=self.recv_sem.at[step],
            device_id={"shard": target},
            device_id_type=MESH,
        )

    def arrival(self, step):
        return pltpu.make_async_remote_copy(
            src_ref=self.out.at[self.k],
            dst_ref=self.out.at[lax.rem(self.k + self.size - step, self.size)],
            send_sem=self.send_sem.at[step],
            recv_sem=self.recv_sem.at[step],
            device_id={"shard": lax.rem(self.k + step, self.size)},
            device_id_type=MESH,
        )

    def local(self):
        source = self.source(self.k) if self.bounce is None else self.bounce
        return pltpu.make_async_copy(source, self.out.at[self.k], self.send_sem.at[0])

    def lift(self):
        return pltpu.make_async_copy(self.source(self.k), self.bounce, self.bounce_sem)

    def start_local(self):
        if self.bounce is None:
            self.local().start()
        else:
            self.lift().start()

    def settle(self):
        if self.bounce is not None:
            self.lift().wait()
            self.local().start()

    def inner(self, step):
        target = lax.rem(self.k + step, self.size)
        beside = jnp.abs(target - self.k) == 1
        return jnp.logical_and(beside, target // 2 != self.k // 2)

    def start_inner(self):
        for step in (1, self.size - 1):

            @pl.when(self.inner(step))
            def _():
                self.copy(step).start()

    def start_outer(self):
        self.start_local()
        for step in range(1, self.size):

            @pl.when(jnp.logical_not(self.inner(step)))
            def _():
                self.copy(step).start()

    def start(self):
        self.start_local()
        for step in range(1, self.size):
            self.copy(step).start()

    def wait_recv(self):
        self.local().wait()
        for step in range(1, self.size):
            self.arrival(step).wait_recv()

    def wait_send(self):
        for step in range(1, self.size):
            self.copy(step).wait_send()

    def wait(self):
        self.wait_recv()
        self.wait_send()


class PairReduce:
    def __init__(self, size, terms, first, middle_terms, second, sems):
        self.size, self.terms, self.first, self.second = size, terms, first, second
        self.middle_terms = middle_terms
        self.sems = sems
        self.k = lax.axis_index("shard")
        self.pairs = size // 2

    def swap(self, pair):
        target = 2 * pair + 1 - lax.rem(self.k, 2)
        return pltpu.make_async_remote_copy(
            src_ref=self.terms.at[target],
            dst_ref=self.first.at[pair],
            send_sem=self.sems.at[0, pair],
            recv_sem=self.sems.at[1, pair],
            device_id={"shard": jnp.bitwise_xor(self.k, 1)},
            device_id_type=MESH,
        )

    def cross(self, step):
        mine = self.k // 2
        pair = lax.rem(mine + step, self.pairs)
        target = 2 * pair + lax.rem(self.k, 2)
        return pair, target, pltpu.make_async_remote_copy(
            src_ref=self.middle_terms.at[step],
            dst_ref=self.second.at[step],
            send_sem=self.sems.at[2, step],
            recv_sem=self.sems.at[3, step],
            device_id={"shard": target},
            device_id_type=MESH,
        )

    def start(self):
        for pair in range(self.pairs):
            self.swap(pair).start()

    def middle(self):
        for pair in range(self.pairs):
            self.swap(pair).wait_recv()
        for step in range(1, self.pairs):
            pair, target, copy = self.cross(step)
            total = self.terms[target].astype(f32) + self.first[pair].astype(f32)
            self.middle_terms[step] = total.astype(bf16)
            copy.start()

    def total(self):
        for step in range(1, self.pairs):
            self.cross(step)[2].wait_recv()
        total = self.terms[self.k].astype(f32) + self.first[self.k // 2].astype(f32)
        for step in range(1, self.pairs):
            total = total + self.second[step].astype(f32)
        return total

    def finish(self):
        for pair in range(self.pairs):
            self.swap(pair).wait_send()
        for step in range(1, self.pairs):
            self.cross(step)[2].wait_send()


class PairSwap:
    def __init__(self, source, out, sems):
        mine = lax.axis_index("shard")
        self.copy = pltpu.make_async_remote_copy(
            src_ref=source,
            dst_ref=out,
            send_sem=sems.at[0],
            recv_sem=sems.at[1],
            device_id={"shard": jnp.bitwise_xor(mine, 1)},
            device_id_type=MESH,
        )


class Moves:
    def __init__(self, sems):
        self.sems, self.copies = sems, []

    def start(self, source, target):
        copy = pltpu.make_async_copy(source, target, self.sems.at[len(self.copies)])
        copy.start()
        self.copies.append(copy)
        return copy

    def wait(self, count=None):
        count = len(self.copies) if count is None else count
        for copy in [c for c in self.copies if c is not None][:count]:
            copy.wait()
        left = [i for i, c in enumerate(self.copies) if c is not None][:count]
        for i in left:
            self.copies[i] = None


def held(arrays):
    return [VMEM(a.shape, a.dtype) for a in arrays]


class Refs:
    def __init__(self, refs):
        self.refs = list(refs)

    def __call__(self, count):
        out, self.refs = self.refs[:count], self.refs[count:]
        return out


def inverse_rms(values):
    return lax.rsqrt(jnp.mean(values * values, axis=-1, keepdims=True) + epsilon)


def norm_back(values, inverse, gain, d_normed):
    scaled = d_normed * gain
    d_values = inverse * scaled - values * (inverse * inverse * inverse) * jnp.mean(
        scaled * values, axis=-1, keepdims=True
    )
    return d_values, jnp.sum(d_normed * values * inverse, axis=0, keepdims=True)


def head_lanes(head, shape):
    lane = lax.broadcasted_iota(jnp.int32, shape, 1)
    return lane < HD if head == 0 else lane >= HD


def turn(values, table, back):
    width = values.shape[1]
    cosine = jnp.concatenate([table[:, :HD]] * (width // HD), axis=1)
    sine = jnp.concatenate([table[:, HD:]] * (width // HD), axis=1)
    lane = lax.broadcasted_iota(jnp.int32, values.shape, 1)
    half = HD // 2
    partner = jnp.where(
        lane % HD < half,
        pltpu.roll(values, width - half, 1),
        pltpu.roll(values, half, 1),
    )
    if back:
        return values * cosine - partner * sine
    return values * cosine + partner * sine


def row_step(length, most):
    return most if length % most == 0 else length


def rows_at(index, step):
    return pl.ds(pl.multiple_of(index * step, step), step)


def weight_pieces(chunks):
    return [(c, kind) for c in range(chunks) for kind in ("gate", "up", "down")]


def piece_shape(kind, shards, part, block):
    return (shards, block, part) if kind == "down" else (shards, part, block)


def piece_source(kind, refs, chunk, block):
    ref = refs[kind]
    half = (ref.shape[0] if kind == "down" else ref.shape[1]) // 2

    def source(j):
        start = pl.multiple_of(lax.rem(j, 2) * half + chunk * block, block)
        if kind == "down":
            return ref.at[pl.ds(start, block), :]
        return ref.at[:, pl.ds(start, block)]

    return source


def split_masks(size):
    masks = chip_masks(size)[1:]
    return [m for m in masks if popcount(m) == 1], [m for m in masks if popcount(m) > 1]


def forward(x, gains, table, cot, attn_weights, mlp_weights, pieces, block):
    seq_size, shard_size = lax.axis_size("seq"), lax.axis_size("shard")
    rows, width = x.shape
    part, cols = attn_weights[0].shape
    length = rows * seq_size
    big = row_step(length, 512)
    query = row_step(length, 256 if length <= 2048 else 128)
    pair = 2 * HD
    scale = 1.0 / math.sqrt(HD)

    def kernel(*refs):
        take = Refs(refs)
        x_ref, gains_ref, table_ref, cot_ref = take(4)
        own_weights = take(4)
        mlp_refs = dict(zip(("gate", "up", "down"), take(3)))
        normed_out, table_all, gains_all = take(3)
        weights_out = take(4)
        heads_out = take(4)
        lse_ref, hidden_ref = take(2)
        cot_all, cot_other, tok_all, tok_other = take(4)
        piece_refs = take(len(pieces))
        terms, arrived, ss, sr = take(4)
        normed_ref, normed_all = take(2)
        full_weights, heads_held = take(4), take(4)
        q_ref, k_ref, v_ref, o_ref = heads_held
        out_sems = take(1)[0]
        bounces, bounce_sems = take(len(pieces)), take(1)[0]
        ns, nr, ts, tr, cs, cr, ds, dr, ms, mr = take(10)
        gs, gr, line_s, line_r, line_c, piece_s, piece_r, local_sem, swap_sem = take(9)

        me, mine = lax.axis_index("seq"), lax.axis_index("shard")
        entry_barrier(seq_neighbours(seq_size), shard_size)
        gain = ShardExchange(shard_size, lambda j: gains_ref, gains_all, gs, gr)
        gain.start()
        lines = [
            LineGather(shard_size, own, out, line_s.at[i], line_r.at[i], line_c.at[i])
            for i, (own, out) in enumerate(zip(own_weights, full_weights))
        ]
        wq_all, wk_all, wv_all, wo_all = full_weights
        exchanges = [
            ShardExchange(
                shard_size, piece_source(kind, mlp_refs, c, block), out, piece_s.at[i],
                piece_r.at[i], bounces[i], bounce_sems.at[i],
            )
            for i, ((c, kind), out) in enumerate(zip(pieces, piece_refs))
        ]
        mine_rows = rows_at(me, rows)
        own_cot = pltpu.make_async_copy(cot_ref, cot_all.at[mine_rows, :], local_sem.at[0])
        tables = SeqGather(seq_size, table_all, rows, ts, tr)
        normed = SeqGather(seq_size, normed_all, rows, ns, nr)
        cots = SeqGather(seq_size, cot_all, rows, cs, cr, own=cot_ref)
        cots_other = SeqGather(seq_size, cot_other, rows, ds, dr)
        swap_cot = PairSwap(cot_ref, cot_other.at[mine_rows, :], swap_sem.at[0]).copy
        for line in lines[:3]:
            line.step(0)
        swap_cot.start()
        own_cot.start()
        table_all[mine_rows, :] = table_ref[...]
        tables.start()
        gain.wait_recv()
        values = x_ref[...].astype(f32)
        scaled = values * inverse_rms(values)
        for z in range(shard_size):
            lanes = slice(z * part, (z + 1) * part)
            normed_all[mine_rows, lanes] = (scaled[:, lanes] * gains_all[z, 0:1, :]).astype(bf16)
        normed.start()
        tables.forwards()
        for line in lines[:3]:
            line.step(1)
        for exchange in exchanges:
            exchange.start_inner()
        near, far = split_masks(seq_size)
        for mask in near:
            normed.forward(mask)
        cots.start()
        for step in range(2, shard_size):
            for line in lines[:3]:
                line.step(step)
            if step == 2:
                lines[3].step(0)
                for mask in far:
                    normed.forward(mask)
                swap_cot.wait_recv()
                cots_other.start()
        tables.finish()
        normed.finish()
        outs = Moves(out_sems)
        outs.start(normed_all, normed_out)
        for held_weight, out in list(zip(full_weights, weights_out))[:3]:
            outs.start(held_weight, out)
        for mask in near:
            cots.forward(mask)
        lines[3].step(1)

        def start_pieces(point):
            if point == START:
                for exchange in exchanges[:AHEAD]:
                    exchange.start_outer()

        start_pieces(0)

        wq, wk, wv = (w.reshape(width, cols) for w in (wq_all, wk_all, wv_all))

        @pl.loop(0, length // big)
        def _(i):
            r = rows_at(i, big)
            tokens = normed_all[r, :]
            tab = table_all[r, :]
            q = turn(dot_nn(tokens, wq[...]), tab, False).astype(bf16)
            q_ref[r, :] = q * jnp.asarray(scale, bf16)
            k_ref[r, :] = turn(dot_nn(tokens, wk[...]), tab, False).astype(bf16)
            v_ref[r, :] = dot_nn(tokens, wv[...]).astype(bf16)

        for mask in far:
            cots.forward(mask)
        start_pieces(1)
        for step in range(2, shard_size - 1):
            lines[3].step(step)

        def attend(hp, lanes):
            for i in range(length // query):
                first, last = i * query, (i + 1) * query
                q2 = q_ref[first:last, lanes]
                out = None
                for head in (0, 1):
                    keep = head_lanes(head, q2.shape)
                    qm = jnp.where(keep, q2, jnp.zeros_like(q2))
                    s = dot_nt(qm, k_ref[:last, lanes])
                    r = lax.broadcasted_iota(jnp.int32, (query, query), 0)
                    c = lax.broadcasted_iota(jnp.int32, (query, query), 1)
                    tail = jnp.where(c <= r, s[:, first:], -1e30)
                    s = tail if i == 0 else jnp.concatenate([s[:, :first], tail], axis=1)
                    m = jnp.max(s, axis=1, keepdims=True)
                    p = jnp.exp(s - m)
                    total = jnp.sum(p, axis=1, keepdims=True)
                    low = (p * (1.0 / total)).astype(bf16)
                    o = dot_nn(low, v_ref[:last, lanes])
                    out = o if head == 0 else jnp.where(keep, o, out)
                    lse = jnp.transpose(jnp.broadcast_to(m + jnp.log(total), (query, 128)))
                    lse_ref[pl.ds(hp * 2 + head, 1), first:last] = lse[0:1, :]
                o_ref[first:last, lanes] = out.astype(bf16)

        if cols == 2 * pair:
            attend(0, slice(0, pair))
            for mask in near:
                cots_other.forward(mask)
            start_pieces(2)
            attend(1, slice(pair, cols))
        else:

            @pl.loop(0, cols // pair)
            def _(hp):
                attend(hp, rows_at(hp, pair))

            for mask in near:
                cots_other.forward(mask)
            start_pieces(2)
        for mask in far:
            cots_other.forward(mask)
        lines[3].step(shard_size - 1)
        start_pieces(3)
        outs.start(full_weights[3], weights_out[3])
        for held_heads, out in zip(heads_held, heads_out):
            outs.start(held_heads, out)
        scatter = SeqScatter(seq_size, terms, arrived, ss, sr)

        def compute(mask):
            tokens = o_ref[scatter.tokens(mask), :]
            for z in range(shard_size):
                scatter.put(mask, slice(z * part, (z + 1) * part), dot_nn(tokens, wo_all[z]))

        scatter.send_terms(compute, merge=True)
        for exchange in exchanges[:AHEAD]:
            exchange.settle()
        scatter.merge_inner()
        scatter.merge(hidden_ref)
        hidden = hidden_ref[...] + x_ref[...].astype(f32)
        hidden_ref[...] = hidden
        scaled = hidden * inverse_rms(hidden)
        for z in range(shard_size):
            lanes = slice(z * part, (z + 1) * part)
            normed_ref[:, lanes] = (scaled[:, lanes] * gains_all[z, 1:2, :]).astype(bf16)
        swap_tok = PairSwap(normed_ref, tok_other, swap_sem.at[1]).copy
        swap_tok.start()
        toks = SeqGather(seq_size, tok_all, rows, ms, mr, own=normed_ref)
        toks.start()
        own_tok = pltpu.make_async_copy(normed_ref, tok_all.at[mine_rows, :], local_sem.at[1])
        own_tok.start()
        for exchange in exchanges[AHEAD:]:
            exchange.start_outer()
        for mask in near:
            toks.forward(mask)
        for mask in far:
            toks.forward(mask)
        swap_cot.wait_send()
        gain.wait_send()
        scatter.finish()
        own_cot.wait()
        cots.finish()
        for line in lines:
            line.finish()
        swap_tok.wait()
        own_tok.wait()
        toks.finish()
        cots_other.finish()
        for exchange in exchanges[AHEAD:]:
            exchange.settle()
        for exchange in exchanges:
            exchange.wait()
        outs.wait()

    weight = array((shard_size, part, cols))
    out_weight = array((shard_size, cols, part))
    heads = array((length, cols))
    tokens = array((length, width))
    shapes = [piece_shape(kind, shard_size, part, block) for _, kind in pieces]
    count = len(pieces)
    outs = pl.pallas_call(
        kernel,
        name="forward_attention",
        out_shape=[
            tokens,
            array((length, table.shape[1]), f32),
            array((shard_size,) + gains.shape, f32),
            weight,
            weight,
            weight,
            out_weight,
            heads,
            heads,
            heads,
            heads,
            array((max(8, cols // HD), length), f32),
            array((rows, width), f32),
            tokens,
            tokens,
            tokens,
            array((rows, width)),
        ]
        + [array(s) for s in shapes],
        in_specs=in_vmem(8) + in_any(3),
        out_specs=in_any(1) + in_vmem(2) + in_any(8) + in_vmem(2) + in_any(4 + count),
        scratch_shapes=scatter_scratch(seq_size, rows, width)
        + [VMEM((rows, width), bf16), VMEM((length, width), bf16)]
        + held([weight] * 3 + [out_weight] + [heads] * 4)
        + [DMA((9,))]
        + [VMEM(s[1:], bf16) for s in shapes]
        + [DMA((count,))]
        + [DMA((seq_size,))] * 10
        + [DMA((shard_size,))] * 2
        + [DMA((4, 2, shard_size - 1))] * 2
        + [DMA((4,))]
        + [DMA((count, shard_size))] * 2
        + [DMA((2,)), DMA((2, 2))],
        compiler_params=kernel_params(1),
    )(x, gains, table, cot, *attn_weights, *mlp_weights)
    return outs[:17], list(outs[17:])


def mlp(tok, tok_other, cot, cot_other, pieces_in, mlp_weights, late, chunks, block, sums):
    seq_size, shard_size = lax.axis_size("seq"), lax.axis_size("shard")
    length, width = tok.shape
    rows = tok_other.shape[0]
    part = width // shard_size
    big = row_step(length, 512)
    steps = length // big
    pieces = weight_pieces(chunks)
    early = pieces[: len(pieces_in)]

    def kernel(*refs):
        take = Refs(refs)
        tok_swap, tok_hbm = take(2)
        cots = take(2)
        early_refs = take(len(early))
        mlp_refs = dict(zip(("gate", "up", "down"), take(3)))
        acts_out = take(3)
        grads_out = take(len(pieces))
        late_refs = take(len(late))
        sum_refs = take(sums)
        tok2, cot_rows, cot_cols, xt = take(4)
        weights = take(len(pieces))
        act_ref, dg_ref, du_ref = take(3)
        grads = take(len(pieces))
        tok_ref, tok_sem, out_sems = take(3)
        bounces, bounce_sems = take(len(late)), take(1)[0]
        tok_copy = pltpu.make_async_copy(tok_hbm, tok_ref, tok_sem)
        tok_copy.start()
        outs = Moves(out_sems)
        ts, tr, late_s, late_r, sum_s, sum_r, row_sem, col_sem, load_sem = take(9)

        me, mine = lax.axis_index("seq"), lax.axis_index("shard")
        entry_barrier(seq_neighbours(seq_size), shard_size)
        late_moves = [
            ShardExchange(
                shard_size, piece_source(kind, mlp_refs, c, block), out, late_s.at[i], late_r.at[i],
                bounces[i], bounce_sems.at[i],
            )
            for i, ((c, kind), out) in enumerate(zip(late, late_refs))
        ]
        for move in late_moves:
            move.start()
        other = SeqGather(seq_size, tok2, rows, ts, tr, own=tok_swap)
        other.start()
        tok2[rows_at(me, rows), :] = tok_swap[...]
        everything = dict(zip(early, early_refs)) | dict(zip(late, late_refs))
        loads = [
            pltpu.make_async_copy(everything[p], w, load_sem.at[i])
            for i, (p, w) in enumerate(zip(pieces, weights))
        ]
        for load in loads[: len(early)]:
            load.start()
        held = dict(zip(pieces, weights))

        def row_copy(plane, i, slot):
            return pltpu.make_async_copy(
                cots[plane].at[rows_at(i, big), :], cot_rows.at[slot], row_sem.at[slot]
            )

        def stage(plane, these, base):
            token_ref = (tok_ref, tok2)[plane]

            @pl.loop(0, steps)
            def _(i):
                slot = lax.rem(i + base, 2)

                @pl.when(i + 1 < steps)
                def _():
                    row_copy(plane, i + 1, 1 - slot).start()

                tokens = token_ref[rows_at(i, big), :]
                row_copy(plane, i, slot).wait()
                r = pl.ds(pl.multiple_of(plane * length + i * big, big), big)
                for c in these:
                    gate_w, up_w = held[c, "gate"], held[c, "up"]
                    gate = dot_nn(tokens, gate_w.reshape(width, block)[...])
                    up = dot_nn(tokens, up_w.reshape(width, block)[...])
                    d_act = dot_nt(cot_rows[slot, :, :part], held[c, "down"][0])
                    for z in range(1, shard_size):
                        lanes = slice(z * part, (z + 1) * part)
                        d_act += dot_nt(cot_rows[slot, :, lanes], held[c, "down"][z])
                    sig = jax.nn.sigmoid(gate)
                    silu = gate * sig
                    act_ref[c, r, :] = (silu * up).astype(bf16)
                    slope = sig * (1.0 + gate * (1.0 - sig))
                    dg_ref[c, r, :] = (d_act * up * slope).astype(bf16)
                    du_ref[c, r, :] = (d_act * silu).astype(bf16)

        def col_copy(z, slot):
            lanes = slice(z * part, (z + 1) * part)
            return [
                pltpu.make_async_copy(
                    cots[plane].at[:, lanes],
                    cot_cols.at[slot, pl.ds(plane * length, length), :],
                    col_sem.at[slot, plane],
                )
                for plane in (0, 1)
            ]

        def grad(c):
            for source, where in ((act_ref, 2), (dg_ref, 0), (du_ref, 1)):
                xt[where] = jnp.transpose(source[c])
            for copy in col_copy(0, 0):
                copy.start()
            for z in range(shard_size):
                lanes = slice(z * part, (z + 1) * part)
                if z + 1 < shard_size:
                    for copy in col_copy(z + 1, (z + 1) % 2):
                        copy.start()
                for which in (0, 1):
                    total = dot_nn(xt[which, :, :length], tok_ref[:, lanes])
                    total += dot_nn(xt[which, :, length:], tok2[:, lanes])
                    grads[3 * c + which][z] = total.astype(bf16)
                for copy in col_copy(z, z % 2):
                    copy.wait()
                grads[3 * c + 2][z] = dot_nn(xt[2], cot_cols[z % 2]).astype(bf16)

        def put_acts(these):
            for c in these:
                for ref, out in zip((act_ref, dg_ref, du_ref), acts_out):
                    outs.start(ref.at[c], out.at[c])

        def put_grads(c):
            for i in range(max(sums, 3 * c), 3 * c + 3):
                outs.start(grads[i], grads_out[i])

        sum_moves = [
            ShardExchange(shard_size, lambda j, g=g: g.at[j], out, sum_s.at[i], sum_r.at[i])
            for i, (g, out) in enumerate(zip(grads, sum_refs))
        ]

        row_copy(0, 0, 0).start()
        first_chunks = [c for c in range(chunks) if all((c, k) in early for k in ("gate", "up", "down"))]
        later_chunks = [c for c in range(chunks) if c not in first_chunks]
        for load in loads[: len(early)]:
            load.wait()
        tok_copy.wait()
        for move in late_moves:
            move.settle()
        stage(0, first_chunks, 0)
        row_copy(1, 0, 0).start()
        other.forwards()
        other.finish()
        stage(1, first_chunks, 0)
        put_acts(first_chunks)
        for c in first_chunks:
            grad(c)
            put_grads(c)
            for move in sum_moves[3 * c : 3 * c + 3]:
                move.start()
        if later_chunks:
            row_copy(0, 0, 0).start()
            for move in late_moves:
                move.wait_recv()
            for load in loads[len(early) :]:
                load.start()
            for load in loads[len(early) :]:
                load.wait()
            stage(0, later_chunks, 0)
            row_copy(1, 0, 0).start()
            stage(1, later_chunks, 0)
            put_acts(later_chunks)
            for c in later_chunks:
                grad(c)
                put_grads(c)
                for move in sum_moves[3 * c : 3 * c + 3]:
                    move.start()
        for move in late_moves:
            move.wait_send()
        for move in sum_moves:
            move.wait()
        outs.wait()

    piece = array((shard_size, block, part))
    act = array((chunks, 2 * length, block))
    late_shapes = [piece_shape(kind, shard_size, part, block) for _, kind in late]
    all_shapes = [piece_shape(kind, shard_size, part, block) for _, kind in pieces]
    outs = pl.pallas_call(
        kernel,
        name="mlp",
        out_shape=[act] * 3
        + [piece] * len(pieces)
        + [array(s) for s in late_shapes]
        + [piece] * sums,
        in_specs=in_vmem(1) + in_any(3 + len(early) + 3),
        out_specs=in_any(3 + len(pieces) + len(late) + sums),
        scratch_shapes=[
            VMEM((length, width), bf16),
            VMEM((2, big, width), bf16),
            VMEM((2, 2 * length, part), bf16),
            VMEM((3, block, 2 * length), bf16),
        ]
        + [VMEM(s, bf16) for s in all_shapes]
        + held([act] * 3 + [piece] * len(pieces))
        + [VMEM((length, width), bf16), DMA, DMA((3 * chunks + len(pieces),))]
        + [VMEM(s[1:], bf16) for s in late_shapes]
        + [DMA((max(1, len(late)),))]
        + [DMA((seq_size,))] * 2
        + [DMA((max(1, len(late)), shard_size))] * 2
        + [DMA((max(1, sums), shard_size))] * 2
        + [DMA((2,)), DMA((2, 2)), DMA((len(pieces),))],
        compiler_params=kernel_params(2),
    )(tok_other, tok, cot, cot_other, *pieces_in, *mlp_weights)
    outs = list(outs)
    first = 3 + len(pieces)
    second = first + len(late)
    return outs[:3], outs[3:first], outs[first:second], outs[second:]


def mlp_back(d_gate, d_up, gate, up, hidden, cot, gains_all, grads):
    seq_size, shard_size = lax.axis_size("seq"), lax.axis_size("shard")
    rows, width = hidden.shape
    chunks = len(gate)
    length = rows * seq_size
    part = width // shard_size
    count = len(grads)
    shared = length > 2048

    def kernel(*refs):
        take = Refs(refs)
        sources = take(2 + 2 * chunks)
        hidden_ref, cot_ref, gains_ref = take(3)
        grad_refs = take(count)
        d_hidden_ref, d_gain_ref, d_attn_all = take(3)
        sum_refs = take(count)
        terms = take(1 if shared else 2)
        arrived = take(2)
        scatter_sems = [take(2), take(2)]
        other_ref, swap_ref, d_attn_ref = take(3)
        ns, nr, swap_sem, own_sem, sum_s, sum_r = take(6)
        loaded, load_sems = take(2 + 2 * chunks), take(1)[0]
        bounces, bounce_sems = take(count), take(1)[0]
        dg_ref, du_ref = loaded[:2]
        gate_refs, up_refs = loaded[2 : 2 + chunks], loaded[2 + chunks :]
        loads = Moves(load_sems)
        for source, target in zip(sources, loaded):
            loads.start(source, target)

        me = lax.axis_index("seq")
        entry_barrier(seq_neighbours(seq_size), shard_size)
        moves = [
            ShardExchange(
                shard_size, lambda j, g=g: g.at[j], out, sum_s.at[i], sum_r.at[i], bounces[i],
                bounce_sems.at[i],
            )
            for i, (g, out) in enumerate(zip(grad_refs, sum_refs))
        ]
        for move in moves[:BEFORE]:
            move.start_outer()
        swap = PairSwap(other_ref, swap_ref, swap_sem).copy
        loads.wait()
        scatters = [
            SeqScatter(seq_size, terms[0 if shared else i], arrived[i], *scatter_sems[i])
            for i in range(2)
        ]

        def term(plane):
            scatter = scatters[plane]

            def compute(mask):
                tokens = scatter.tokens(mask, plane * length)
                for z in range(shard_size):
                    total = None
                    for c in range(chunks):
                        both = dot_nt(dg_ref[c, tokens, :], gate_refs[c][z])
                        both += dot_nt(du_ref[c, tokens, :], up_refs[c][z])
                        total = both if total is None else total + both
                    scatter.put(mask, slice(z * part, (z + 1) * part), total)

            return compute

        here, there = scatters
        there.send_terms(term(1), merge=True)
        if shared:
            there.merge_inner()
            there.merge(other_ref)
            swap.start()
            there.finish()
            here.send_terms(term(0), merge=True)
        else:
            here.send_terms(term(0))
            there.merge_inner()
            here.merge_leaves()
            there.merge(other_ref)
            swap.start()
        for move in moves:
            move.start_inner()
        for move in moves[BEFORE:]:
            move.start_outer()
        here.merge_inner()
        here.merge(d_hidden_ref)
        swap.wait()
        d_normed = d_hidden_ref[...] + swap_ref[...].astype(f32)
        values = hidden_ref[...]
        gain = jnp.concatenate([gains_ref[z, 1:2, :] for z in range(shard_size)], axis=1)
        d_values, d_gain = norm_back(values, inverse_rms(values), gain, d_normed)
        d_hidden = cot_ref[...].astype(f32) + d_values
        d_attn_ref[...] = d_hidden.astype(bf16)
        gather = SeqGather(seq_size, d_attn_all, rows, ns, nr, own=d_attn_ref)
        gather.start()
        for move in moves:
            move.settle()
        own = pltpu.make_async_copy(d_attn_ref, d_attn_all.at[rows_at(me, rows), :], own_sem)
        own.start()
        d_hidden_ref[...] = d_hidden
        d_gain_ref[...] = d_gain
        gather.forwards()
        own.wait()
        gather.finish()
        for scatter in scatters[: 1 if shared else 2]:
            scatter.finish()
        for move in moves:
            move.wait()

    scatter = scatter_scratch(seq_size, rows, width)
    inputs = [d_gate, d_up, *gate, *up]
    outs = pl.pallas_call(
        kernel,
        name="mlp_back",
        out_shape=[
            array((rows, width), f32),
            array((1, width), f32),
            array((length, width)),
        ]
        + [array(g.shape) for g in grads],
        in_specs=in_any(2 + 2 * chunks) + in_vmem(3) + in_any(count),
        out_specs=in_vmem(2) + in_any(1 + count),
        scratch_shapes=scatter[:1] * (1 if shared else 2)
        + scatter[1:2] * 2
        + [DMA((seq_size,))] * 4
        + [VMEM((rows, width), bf16)] * 3
        + [DMA((seq_size,))] * 2
        + [DMA((2,)), DMA]
        + [DMA((max(1, count), shard_size))] * 2
        + held(inputs)
        + [DMA((len(inputs),))]
        + [VMEM(g.shape[1:], bf16) for g in grads]
        + [DMA((max(1, count),))],
        compiler_params=kernel_params(3),
    )(*inputs, hidden, cot, gains_all, *grads)
    return outs[:3], list(outs[3:])


class OutputSum:
    def __init__(self, scatter, act, down_refs, base=0):
        self.scatter, self.act, self.down_refs, self.base = scatter, act, down_refs, base

    def compute(self, mask):
        tokens = self.scatter.tokens(mask, self.base)
        shards, _, part = self.down_refs[0].shape
        for z in range(shards):
            total = None
            for c, down in enumerate(self.down_refs):
                one = dot_nn(self.act[c, tokens, :], down[z])
                total = one if total is None else total + one
            self.scatter.put(mask, slice(z * part, (z + 1) * part), total)


def attend_back(d_attn, wo, mixed, q, k, v, lse, table, normed, grads, activ, down):
    seq_size, shard_size = lax.axis_size("seq"), lax.axis_size("shard")
    length, width = d_attn.shape
    rows = length // seq_size
    cols = q.shape[1]
    part = wo.shape[2]
    big = row_step(length, 512)
    block = row_step(length, 256)
    scale = 1.0 / math.sqrt(HD)
    pair = 2 * HD
    count = len(grads)
    chunks = len(down)

    def kernel(*refs):
        take = Refs(refs)
        sources = take(9 + chunks)
        grad_refs = take(count)
        act_all = take(1)[0] if chunks else None
        dq_ref, dk_ref, dv_ref, gq_ref, gk_ref, gv_ref = take(6)
        if chunks:
            swap_ref = take(1)[0]
        sum_refs = take(count + 1)
        do_ref, kt_ref, dk_acc, dv_acc, xt_ref, go_ref, sum_s, sum_r = take(8)
        loaded, load_sems = take(9 + chunks), take(1)[0]
        bounces, bounce_sems = take(count), take(1)[0]
        da_ref, wo_ref, mixed_ref, q_ref, k_ref, v_ref, lse_ref, t_ref, n_ref = loaded[:9]
        down_refs = loaded[9:]
        loads = Moves(load_sems)
        first = list(range(9, 9 + chunks)) + [0, 2]
        for i in first + [1, 3, 4, 5, 6, 7, 8]:
            loads.start(sources[i], loaded[i])

        if chunks:
            terms, arrived, ss, sr, act_ref, other_ref, act_sem, swap_sem = take(8)
            act_copy = pltpu.make_async_copy(
                act_all.at[:, pl.ds(length, length), :], act_ref, act_sem
            )
            act_copy.start()
        entry_barrier(seq_neighbours(seq_size) if chunks else [], shard_size)
        moves = [
            ShardExchange(
                shard_size, lambda j, g=g: g.at[j], out, sum_s.at[i], sum_r.at[i], bounce,
                bounce_sems.at[i],
            )
            for i, (g, out, bounce) in enumerate(
                zip(grad_refs + [go_ref], sum_refs, bounces + [None])
            )
        ]
        for move in moves[:-1]:
            move.start_outer()
        if chunks:
            swap = PairSwap(other_ref, swap_ref, swap_sem).copy
            act_copy.wait()
            loads.wait(chunks)
            out_sum = OutputSum(SeqScatter(seq_size, terms, arrived, ss, sr), act_ref, down_refs)
            out_sum.scatter.send_terms(out_sum.compute, merge=True)

        loads.wait(2)
        xt_ref[...] = jnp.transpose(mixed_ref[...])
        for z in range(shard_size):
            go_ref[z] = dot_nn(xt_ref[...], da_ref[:, z * part : (z + 1) * part]).astype(bf16)
        moves[-1].start_outer()
        loads.wait(6)

        @pl.loop(0, length // big)
        def _(i):
            r = rows_at(i, big)
            total = dot_nt(da_ref[r, :part], wo_ref[0])
            for z in range(1, shard_size):
                total += dot_nt(da_ref[r, z * part : (z + 1) * part], wo_ref[z])
            do_ref[r, :] = total.astype(bf16)

        kt_ref[...] = jnp.transpose(k_ref[...])
        for move in moves:
            move.settle()
        if chunks:
            out_sum.scatter.merge_inner()

        def heads(hp, lanes):
            dk_acc[...] = jnp.zeros_like(dk_acc)
            dv_acc[...] = jnp.zeros_like(dv_acc)
            for i in range(length // block):
                first, last = i * block, (i + 1) * block
                q2 = q_ref[first:last, lanes]
                do2 = do_ref[first:last, lanes]
                keys = k_ref[:last, lanes]
                values = v_ref[:last, lanes]
                dqt, dk_add, dv_add = None, None, None
                for head in (0, 1):
                    keep = head_lanes(head, q2.shape)
                    qm = jnp.where(keep, q2, jnp.zeros_like(q2))
                    dom = jnp.where(keep, do2, jnp.zeros_like(do2))
                    st = dot_nt(keys, qm)
                    row = lse_ref[pl.ds(hp * 2 + head, 1), first:last]
                    p = jnp.exp(st - row)
                    r = lax.broadcasted_iota(jnp.int32, (block, block), 0)
                    c = lax.broadcasted_iota(jnp.int32, (block, block), 1)
                    tail = jnp.where(r <= c, p[first:], 0.0)
                    p = tail if i == 0 else jnp.concatenate([p[:first], tail], axis=0)
                    dp = dot_nt(values, dom)
                    inner = jnp.sum(dp * p, axis=0, keepdims=True)
                    ds = (p * (dp - inner)).astype(bf16)
                    dv_one = dot_nn(p.astype(bf16), dom)
                    dk_one = dot_nn(ds, qm)
                    dv_add = dv_one if head == 0 else dv_add + dv_one
                    dk_add = dk_one if head == 0 else dk_add + dk_one
                    dqt_one = dot_nn(kt_ref[lanes, :last], ds)
                    if head == 0:
                        dqt = dqt_one
                    else:
                        sub = lax.broadcasted_iota(jnp.int32, dqt.shape, 0)
                        dqt = jnp.where(sub < HD, dqt, dqt_one)
                dk_acc[:last, :] += dk_add
                dv_acc[:last, :] += dv_add
                dq = (jnp.transpose(dqt) * scale).astype(bf16).astype(f32)
                dq_ref[first:last, lanes] = turn(dq, t_ref[first:last, :], True).astype(bf16)
            dv_ref[:, lanes] = dv_acc[...].astype(bf16)

            @pl.loop(0, length // big)
            def _(i):
                r = rows_at(i, big)
                dk = dk_acc[r, :].astype(bf16).astype(f32)
                dk_ref[r, lanes] = turn(dk, t_ref[r, :], True).astype(bf16)

        if chunks:
            for hp in range(cols // pair):
                heads(hp, slice(hp * pair, (hp + 1) * pair))
                if hp == 0:
                    out_sum.scatter.merge(other_ref)
                    swap.start()
                    for move in moves:
                        move.start_inner()
        else:
            for move in moves:
                move.start_inner()

            @pl.loop(0, cols // pair)
            def _(hp):
                heads(hp, rows_at(hp, pair))

        loads.wait()
        for source, out in ((dq_ref, gq_ref), (dk_ref, gk_ref), (dv_ref, gv_ref)):
            xt_ref[...] = jnp.transpose(source[...])
            for z in range(shard_size):
                out[z] = dot_nn(xt_ref[...], n_ref[:, z * part : (z + 1) * part]).astype(bf16)
        if chunks:
            swap.wait()
            out_sum.scatter.finish()
        for move in moves:
            move.wait()

    grad = array((shard_size, cols, part))
    scratch = [
        VMEM((length, cols), bf16),
        VMEM((cols, length), bf16),
        VMEM((length, pair), f32),
        VMEM((length, pair), f32),
        VMEM((cols, length), bf16),
        VMEM((shard_size, cols, part), bf16),
    ] + [DMA((count + 1, shard_size))] * 2
    inputs = [d_attn, wo, mixed, q, k, v, lse, table, normed, *down]
    scratch += held(inputs) + [DMA((len(inputs),))]
    scratch += [VMEM(g.shape[1:], bf16) for g in grads] + [DMA((count + 1,))]
    if chunks:
        scratch += scatter_scratch(seq_size, rows, width)
        scratch += [VMEM((chunks, length, activ.shape[2]), bf16), VMEM((rows, width), bf16)]
        scratch += [DMA, DMA((2,))]
    outs = pl.pallas_call(
        kernel,
        name="attend_back",
        out_shape=[array((length, cols))] * 3
        + [grad] * 3
        + [array((rows, width))] * (1 if chunks else 0)
        + [array(g.shape) for g in grads]
        + [grad],
        in_specs=in_any(9 + chunks + count + (1 if chunks else 0)),
        out_specs=in_vmem(7 if chunks else 6) + in_any(count + 1),
        scratch_shapes=scratch,
        compiler_params=kernel_params(4),
    )(*inputs, *grads, *([activ] if chunks else []))
    outs = list(outs)
    other = outs.pop(6) if chunks else None
    return outs[:3], outs[3:6], other, outs[6:]


def output_parts(activ, down, hidden):
    seq_size, shard_size = lax.axis_size("seq"), lax.axis_size("shard")
    rows, width = hidden.shape
    length = rows * seq_size
    chunks = len(down)

    def kernel(*refs):
        take = Refs(refs)
        act_ref, hidden_ref = take(2)
        down_refs = take(chunks)
        out_ref, terms, first, second = take(4)
        sems = [take(2), take(2)]
        total_ref, other_ref, swap_ref, swap_sem = take(4)
        entry_barrier(seq_neighbours(seq_size), shard_size)
        there, here = (
            OutputSum(SeqScatter(seq_size, terms, arrived, *sem), act_ref, down_refs, base)
            for arrived, sem, base in ((first, sems[0], length), (second, sems[1], 0))
        )
        there.scatter.run(there.compute, other_ref)
        swap = PairSwap(other_ref, swap_ref, swap_sem).copy
        swap.start()
        there.scatter.finish()
        here.scatter.run(here.compute, total_ref)
        swap.wait()
        out_ref[...] = (total_ref[...] + swap_ref[...].astype(f32) + hidden_ref[...]).astype(bf16)
        here.scatter.finish()

    scatter = scatter_scratch(seq_size, rows, width)
    return pl.pallas_call(
        kernel,
        name="output_parts",
        out_shape=array((rows, width)),
        in_specs=in_vmem(2 + chunks),
        out_specs=in_vmem(1)[0],
        scratch_shapes=scatter[:2]
        + scatter[1:2]
        + [DMA((seq_size,))] * 4
        + [VMEM((rows, width), f32), VMEM((rows, width), bf16), VMEM((rows, width), bf16)]
        + [DMA((2,))],
        compiler_params=kernel_params(6),
    )(activ, hidden, *down)


def finish(
    d_qkv, attn_weights, g_qkv, x, d_hidden, gains_all, d_gain_two, sums, g_output, block,
    output_of,
):
    seq_size, shard_size = lax.axis_size("seq"), lax.axis_size("shard")
    rows, width = x.shape
    part = width // shard_size
    cols = d_qkv[0].shape[1]
    length = rows * seq_size
    pieces = len(sums)
    half = pieces // 3 * block
    activ, down, hidden, other = output_of or (None, [], None, None)
    chunks = len(down)
    pairs = shard_size // 2

    def kernel(*refs):
        take = Refs(refs)
        x_ref, d_hidden_ref, gains_ref, gain2_ref = take(4)
        sources = take(9 + chunks)
        hidden_ref, other_ref = take(2) if chunks else (None, None)
        act_all = take(1)[0] if chunks else None
        sum_refs, go_ref = take(pieces), take(1)[0]
        d_inputs_ref, gain_ref = take(2)
        qkv_refs = take(3)
        output_ref = take(1)[0] if chunks else None
        wo_ref, wg_ref, wu_ref, wd_ref = take(4)
        total_ref, gain_mine, gain_shards, gain_line, gain_seq = take(5)
        gs, gr, hs, hr = take(4)
        in_terms, in_arrived, in_s, in_r = take(4)
        firsts, middles, seconds, reduce_sems = take(4)
        received, wide, tall, load_sem, store_sem = take(5)
        loaded, in_sems = take(9 + chunks), take(1)[0]
        d_refs, w_refs, g_refs = loaded[:3], loaded[3:6], loaded[6:9]
        down_refs = loaded[9:]
        ins = Moves(in_sems)
        for i in [6, 7, 8, 0, 1, 2, 3, 4, 5] + list(range(9, 9 + chunks)):
            ins.start(sources[i], loaded[i])
        if chunks:
            out_terms, out_arrived, out_s, out_r, act_ref, act_sem, out_total = take(7)
            act_copy = pltpu.make_async_copy(act_all.at[:, pl.ds(0, length), :], act_ref, act_sem)
            act_copy.start()

        me = lax.axis_index("seq")
        entry_barrier(range(1, seq_size), shard_size)
        reduces = [
            PairReduce(
                shard_size, g_refs[i], firsts.at[i], middles.at[i], seconds.at[i], reduce_sems.at[i]
            )
            for i in range(3)
        ]
        ins.wait(3)
        for reduce in reduces:
            reduce.start()
        ins.wait(6)
        in_sum = SeqScatter(seq_size, in_terms, in_arrived, in_s, in_r)

        def inputs_term(mask):
            tokens = in_sum.tokens(mask)
            for z in range(shard_size):
                total = None
                for d_ref, w_ref in zip(d_refs, w_refs):
                    term = dot_nt(d_ref[tokens, :], w_ref[z])
                    total = term if total is None else total + term
                in_sum.put(mask, slice(z * part, (z + 1) * part), total)

        in_sum.send_terms(inputs_term, merge=True)
        if chunks:
            act_copy.wait()
            ins.wait()
            out_sum = OutputSum(
                SeqScatter(seq_size, out_terms, out_arrived, out_s, out_r), act_ref, down_refs
            )
            out_sum.scatter.send_terms(out_sum.compute)

        loads = [
            pltpu.make_async_copy(source, received.at[i % 2], load_sem.at[i % 2])
            for i, source in enumerate(sum_refs)
        ]
        stores = []

        def store(staging, target, value):
            turn_of = sum(1 for s in stores if s[0] is staging)
            slot = turn_of % 2
            sem = store_sem.at[0 if staging is wide else 1, slot]
            if turn_of >= 2:
                [s for s in stores if s[0] is staging][-2][1].wait()
            staging[slot] = value.astype(bf16)
            copy = pltpu.make_async_copy(staging.at[slot], target, sem)
            copy.start()
            stores.append((staging, copy))

        def collect(i):
            if i + 1 < pieces:
                loads[i + 1].start()
            loads[i].wait()
            for parity in (0, 1):
                total = received[i % 2, parity].astype(f32)
                for p in range(1, pairs):
                    total = total + received[i % 2, 2 * p + parity].astype(f32)
                start = parity * half + i // 3 * block
                if i % 3 == 2:
                    store(wide, wd_ref.at[start : start + block, :], total)
                else:
                    target = (wg_ref, wu_ref)[i % 3]
                    store(tall, target.at[:, start : start + block], jnp.transpose(total))

        loads[0].start()
        third = (pieces + 2) // 3
        in_sum.merge_inner()
        reduces[0].middle()
        if chunks:
            out_sum.scatter.merge_leaves()
        for i in range(third):
            collect(i)
        reduces[1].middle()
        in_sum.merge(total_ref)
        values = x_ref[...].astype(f32)
        gain = jnp.concatenate([gains_ref[z, 0:1, :] for z in range(shard_size)], axis=1)
        d_values, d_gain = norm_back(values, inverse_rms(values), gain, total_ref[...])
        d_inputs_ref[...] = (d_hidden_ref[...] + d_values).astype(bf16)
        for z in range(shard_size):
            lanes = slice(z * part, (z + 1) * part)
            gain_mine[z, 0:1, :] = d_gain[:, lanes]
            gain_mine[z, 1:2, :] = gain2_ref[0:1, lanes]
            gain_mine[z, 2:, :] = jnp.zeros((6, part), f32)
        line = ShardExchange(shard_size, lambda j: gain_mine.at[j], gain_shards, gs, gr)
        line.start()
        for i in range(third, 2 * third):
            collect(i)
        reduces[2].middle()
        if chunks:
            out_sum.scatter.merge_inner()
        line.wait()
        gain_line[...] = sum(gain_shards[z] for z in range(shard_size))

        def to_seq(step):
            return pltpu.make_async_remote_copy(
                src_ref=gain_line,
                dst_ref=gain_seq.at[step],
                send_sem=hs.at[step],
                recv_sem=hr.at[step],
                device_id={"seq": jnp.bitwise_xor(me, step)},
                device_id_type=MESH,
            )

        for step in range(1, seq_size):
            to_seq(step).start()
        for i in range(2 * third, pieces):
            collect(i)
        wo_ref[...] = sum(go_ref[z].astype(f32) for z in range(shard_size)).astype(bf16)
        if chunks:
            out_sum.scatter.merge(out_total)
            output_ref[...] = (
                out_total[...] + other_ref[...].astype(f32) + hidden_ref[...]
            ).astype(bf16)
        for reduce, out in zip(reduces, qkv_refs):
            out[...] = jnp.transpose(reduce.total()).astype(bf16)
        for step in range(1, seq_size):
            to_seq(step).wait()
        gain_ref[...] = gain_line[...] + sum(gain_seq[step] for step in range(1, seq_size))
        for staging in (wide, tall):
            for _, copy in [s for s in stores if s[0] is staging][-2:]:
                copy.wait()
        for reduce in reduces:
            reduce.finish()
        in_sum.finish()
        if chunks:
            out_sum.scatter.finish()

    scratch = [
        VMEM((rows, width), f32),
        VMEM((shard_size, 8, part), f32),
        VMEM((shard_size, 8, part), f32),
        VMEM((8, part), f32),
        VMEM((seq_size, 8, part), f32),
    ]
    scratch += [DMA((shard_size,))] * 2 + [DMA((seq_size,))] * 2
    scratch += scatter_scratch(seq_size, rows, width)
    scratch += [VMEM((3, pairs, cols, part), bf16)] * 3 + [DMA((3, 4, pairs))]
    scratch += [
        VMEM((2, shard_size, block, part), bf16),
        VMEM((2, block, part), bf16),
        VMEM((2, part, block), bf16),
        DMA((2,)),
        DMA((2, 2)),
    ]
    inputs = [*d_qkv, *attn_weights, *g_qkv, *down]
    scratch += held(inputs) + [DMA((len(inputs),))]
    if chunks:
        scratch += scatter_scratch(seq_size, rows, width)
        scratch += [VMEM((chunks, length, block), bf16), DMA, VMEM((rows, width), f32)]
    extra = 1 if chunks else 0
    units = 2 * half
    outs = pl.pallas_call(
        kernel,
        name="finish",
        out_shape=[array((rows, width)), array((8, part), f32)]
        + [array((part, cols))] * 3
        + [array((rows, width))] * extra
        + [array((cols, part))]
        + [array((part, units))] * 2
        + [array((units, part))],
        in_specs=in_vmem(4)
        + in_any(9 + chunks)
        + in_vmem(2 * extra)
        + in_any(extra + pieces)
        + in_vmem(1),
        out_specs=in_vmem(6 + extra) + in_any(3),
        scratch_shapes=scratch,
        compiler_params=kernel_params(5),
    )(
        x, d_hidden, gains_all, d_gain_two, *inputs,
        *([hidden, other, activ] if chunks else []), *sums, g_output,
    )
    outs = list(outs)
    output = outs.pop(5) if chunks else None
    return outs, output


def widen(rows, grads, gains):
    part = gains.shape[1]

    def kernel(*refs):
        take = Refs(refs)
        grad_refs, row_refs, gain_ref = take(len(grads)), take(len(rows)), take(1)[0]
        row_outs, grad_outs, gain_outs = take(len(rows)), take(len(grads)), take(2)
        low, high, load_sems, store_sems = take(len(grads)), take(len(grads)), *take(2)
        loads, stores = Moves(load_sems), Moves(store_sems)
        for source, target in zip(grad_refs, low):
            loads.start(source, target)
        for source, target in zip(row_refs, row_outs):
            target[...] = source[...]
        for i, out in enumerate(gain_outs):
            out[...] = gain_ref[i : i + 1, :]
        for a, b, out in zip(low, high, grad_outs):
            loads.wait(1)
            b[...] = a[...].astype(f32)
            stores.start(b, out)
        stores.wait()

    wide = [array(g.shape, f32) for g in grads]
    return pl.pallas_call(
        kernel,
        name="widen",
        out_shape=[array(r.shape) for r in rows] + wide + [array((1, part), f32)] * 2,
        in_specs=in_any(len(grads)) + in_vmem(len(rows) + 1),
        out_specs=in_vmem(len(rows)) + in_any(len(grads)) + in_vmem(2),
        scratch_shapes=held(grads) + held(wide) + [DMA((len(grads),)), DMA((len(grads),))],
        compiler_params=kernel_params(),
    )(*grads, *rows, gains)


def rotation_table(position_ids):
    half = HD // 2
    freqs = theta_base ** (-(jnp.arange(half, dtype=f32) * 2.0) / HD)
    angles = position_ids.astype(f32)[:, None] * freqs[None, :]
    cosine, sine = jnp.cos(angles), jnp.sin(angles)
    return jnp.concatenate([cosine, cosine, -sine, sine], axis=1)


EARLY = 4
AHEAD = 4
BEFORE = 2
SUMS = (1, 4)
START = 2


def body(
    inputs,
    positions,
    attn_gain,
    w_query,
    w_key,
    w_value,
    w_output,
    mlp_gain,
    w_gate,
    w_up,
    w_down,
    cotangent,
):
    shard_size = lax.axis_size("shard")
    x, cot = inputs[0], cotangent[0]
    gains = jnp.pad(jnp.stack([attn_gain, mlp_gain]).astype(f32), ((0, 6), (0, 0)))
    table = rotation_table(positions[0])
    half = w_gate.shape[1] // 2
    block = row_step(half, 256)
    chunks = half // block
    pieces = weight_pieces(chunks)
    early, late = pieces[:EARLY], pieces[EARLY:]
    mlp_weights = (w_gate, w_up, w_down)
    held, early_weights = forward(
        x, gains, table, cot, (w_query, w_key, w_value, w_output), mlp_weights, early, block
    )
    normed, tables, gains_all, wq, wk, wv, wo, q, k, v, mixed, lse, hidden = held[:13]
    cot_all, cot_other, tok, tok_other = held[13:]
    acts, grads, late_weights, sums = mlp(
        tok, tok_other, cot_all, cot_other, early_weights, mlp_weights, late, chunks, block,
        min(SUMS[0], len(pieces)),
    )
    activ, d_gate, d_up = acts
    weights = dict(zip(pieces, early_weights + late_weights))

    def kind(name):
        return [weights[c, name] for c in range(chunks)]

    done = len(sums)
    more = min(SUMS[1], len(pieces) - done)
    (d_hidden, d_gain_two, d_attn), moved = mlp_back(
        d_gate, d_up, kind("gate"), kind("up"), hidden, cot, gains_all, grads[done : done + more]
    )
    sums += moved
    done += more
    down = kind("down")
    together = tok.shape[0] <= 2048
    d_qkv, g_qkv, other, moved = attend_back(
        d_attn, wo, mixed, q, k, v, lse, tables, normed, grads[done:], activ,
        down if together else [],
    )
    sums += moved[:-1]
    results, output = finish(
        d_qkv, (wq, wk, wv), g_qkv, x, d_hidden, gains_all, d_gain_two, sums, moved[-1], block,
        (activ, down, hidden, other) if together else None,
    )
    if not together:
        output = output_parts(activ, down, hidden)
    d_inputs, gain_sums, *grads = results
    output, d_inputs, *grads, gain_one, gain_two = widen([output, d_inputs], grads, gain_sums)
    return (
        output[None],
        d_inputs[None],
        gain_one.reshape(-1),
        *grads[:4],
        gain_two.reshape(-1),
        *grads[4:],
    )


def solution(mesh):
    in_specs = (
        P("shard", "seq", None),
        P("shard", "seq"),
        P("shard"),
        P("shard", "seq"),
        P("shard", "seq"),
        P("shard", "seq"),
        P("seq", "shard"),
        P("shard"),
        P("shard", "seq"),
        P("shard", "seq"),
        P("seq", "shard"),
        P("shard", "seq", None),
    )
    out_specs = (
        P("shard", "seq", None),
        P("shard", "seq", None),
        P("shard"),
        P("shard", "seq"),
        P("shard", "seq"),
        P("shard", "seq"),
        P("seq", "shard"),
        P("shard"),
        P("shard", "seq"),
        P("shard", "seq"),
        P("seq", "shard"),
    )
    return jax.shard_map(body, mesh=mesh, in_specs=in_specs, out_specs=out_specs, check_vma=False)
```

```python
import math

import jax
import jax.numpy as jnp
from jax import lax
from jax.experimental import pallas as pl
from jax.experimental.pallas import tpu as pltpu
from jax.sharding import PartitionSpec as P

HD = 64
epsilon = 1e-05
theta_base = 130000.0
bf16 = jnp.bfloat16
f32 = jnp.float32
VMEM = pltpu.VMEM
DMA = pltpu.SemaphoreType.DMA
MESH = pl.DeviceIdType.MESH


def dot_nn(a, b):
    return jnp.dot(a, b, preferred_element_type=f32)


def dot_nt(a, b):
    return lax.dot_general(a, b, (((1,), (1,)), ((), ())), preferred_element_type=f32)


def in_vmem(count):
    return [pl.BlockSpec(memory_space=VMEM)] * count


def in_any(count):
    return [pl.BlockSpec(memory_space=pl.ANY)] * count


def array(shape, dtype=bf16):
    return jax.ShapeDtypeStruct(shape, dtype)


def kernel_params(collective_id=None, limit=62):
    if collective_id is None:
        return pltpu.CompilerParams(vmem_limit_bytes=limit << 20)
    return pltpu.CompilerParams(
        collective_id=collective_id, has_side_effects=True, vmem_limit_bytes=limit << 20
    )


def popcount(mask):
    return bin(mask).count("1")


def chip_masks(size):
    return sorted(range(0, size, 2), key=lambda m: (popcount(m), m))


def chip_bits(size):
    return [1 << b for b in range(1, size.bit_length() - 1)]


def last_hop(mask, core):
    set_bits = [1 << b for b in range(1, mask.bit_length()) if mask >> b & 1]
    return set_bits[-1] if core == 0 else set_bits[0]


def further_masks(mask, core, size):
    return [
        mask | hop
        for hop in chip_bits(size)
        if not mask & hop and last_hop(mask | hop, core) == hop
    ]


def seq_neighbours(size):
    return [1] + chip_bits(size)


def entry_barrier(seq_masks, shard_size):
    barrier = pltpu.get_barrier_semaphore()
    me, mine = lax.axis_index("seq"), lax.axis_index("shard")
    for mask in seq_masks:
        pl.semaphore_signal(
            barrier, inc=1, device_id={"seq": jnp.bitwise_xor(me, mask)}, device_id_type=MESH
        )
    for step in range(1, shard_size):
        pl.semaphore_signal(
            barrier, inc=1, device_id={"shard": lax.rem(mine + step, shard_size)},
            device_id_type=MESH,
        )
    pl.semaphore_wait(barrier, len(seq_masks) + max(shard_size - 1, 0))


class SeqGather:
    def __init__(self, size, out, rows, send_sem, recv_sem, own=None):
        self.size, self.out, self.rows = size, out, rows
        self.send_sem, self.recv_sem = send_sem, recv_sem
        self.me = lax.axis_index("seq")
        self.core = lax.rem(self.me, 2)
        self.own = own

    def block(self, index):
        return self.out.at[pl.ds(pl.multiple_of(index * self.rows, self.rows), self.rows), :]

    def copy(self, arrives, hop):
        block = self.block(jnp.bitwise_xor(self.me, arrives ^ hop))
        src = self.own if arrives == hop and self.own is not None else block
        return pltpu.make_async_remote_copy(
            src_ref=src,
            dst_ref=block,
            send_sem=self.send_sem.at[arrives],
            recv_sem=self.recv_sem.at[arrives],
            device_id={"seq": jnp.bitwise_xor(self.me, hop)},
            device_id_type=MESH,
        )

    def wait_recv(self, mask):
        block = self.block(jnp.bitwise_xor(self.me, mask))
        pltpu.make_async_remote_copy(
            src_ref=block,
            dst_ref=block,
            send_sem=self.send_sem.at[mask],
            recv_sem=self.recv_sem.at[mask],
            device_id={"seq": jnp.bitwise_xor(self.me, 1)},
            device_id_type=MESH,
        ).wait_recv()

    def start(self):
        for hop in reversed(seq_neighbours(self.size)):
            self.copy(hop, hop).start()

    def forward(self, mask):
        self.wait_recv(mask)
        for core in (0, 1):
            for more in further_masks(mask, core, self.size):

                @pl.when(self.core == core)
                def _():
                    self.copy(more, more ^ mask).start()

        self.copy(mask | 1, 1).start()

    def forwards(self):
        for mask in chip_masks(self.size)[1:]:
            self.forward(mask)

    def finish(self):
        for mask in chip_masks(self.size):
            self.wait_recv(mask | 1)
        for mask in range(1, self.size):
            self.copy(mask, 1 if mask & 1 else mask & -mask).wait_send()


def height(mask, core, size):
    return max([0] + [1 + height(m, core, size) for m in further_masks(mask, core, size)])


class SeqScatter:
    def __init__(self, size, terms, arrived, send_sem, recv_sem):
        self.size, self.terms, self.arrived = size, terms, arrived
        self.send_sem, self.recv_sem = send_sem, recv_sem
        self.me = lax.axis_index("seq")
        self.core = lax.rem(self.me, 2)
        self.masks = chip_masks(size)[::-1]
        self.order = [
            sorted(self.masks, key=lambda m: (height(m, core, size), -popcount(m)))
            for core in (0, 1)
        ]
        self.leaves = size // 4
        self.merged = 0

    def copy(self, mask, hop):
        core = 1 - self.core if mask & 1 else self.core
        return pltpu.make_async_remote_copy(
            src_ref=self.terms.at[mask // 2, core],
            dst_ref=self.arrived.at[mask - 1],
            send_sem=self.send_sem.at[mask],
            recv_sem=self.recv_sem.at[mask],
            device_id={"seq": jnp.bitwise_xor(self.me, hop)},
            device_id_type=MESH,
        )

    def tokens(self, mask, base=0):
        pair = 2 * self.terms.shape[2]
        start = jnp.bitwise_xor(self.me, mask) // 2 * pair + base
        return pl.ds(pl.multiple_of(start, pair), pair)

    def put(self, mask, lanes, total):
        rows = self.terms.shape[2]
        self.terms[mask // 2, :, :, lanes] = total.astype(bf16).reshape(2, rows, -1)

    def add(self, mask, source, write):
        rows = self.terms.shape[2]
        step = 32 if rows % 32 == 0 else 16

        @pl.loop(0, rows // step)
        def _(i):
            part = pl.ds(pl.multiple_of(i * step, step), step)
            total = self.terms[mask // 2, self.core, part, :].astype(f32)
            for s in source:
                total = total + self.arrived[s - 1, part, :].astype(f32)
            write(part, total)

    def merge(self, result=None):
        for core in (0, 1):
            mask = self.order[core][self.merged]
            further = further_masks(mask, core, self.size)

            def keep(part, total, mask=mask):
                if mask:
                    self.terms[mask // 2, self.core, part, :] = total.astype(bf16)
                else:
                    result[part, :] = total.astype(result.dtype)

            @pl.when(self.core == core)
            def _(mask=mask, further=further, keep=keep, core=core):
                for m in [mask | 1] + further:
                    self.copy(m, 1).wait_recv()
                self.add(mask, [mask | 1] + further, keep)
                if mask:
                    self.copy(mask, last_hop(mask, core)).start()

        self.merged += 1

    def send_terms(self, compute, merge=False):
        done = set()
        for mask in self.masks:
            compute(mask)
            self.copy(mask | 1, 1).start()
            if merge and self.merged < self.leaves:
                if all(order[self.merged] in done for order in self.order):
                    self.merge()
            done.add(mask)
        if merge:
            self.merge_leaves()

    def merge_leaves(self):
        while self.merged < self.leaves:
            self.merge()

    def merge_inner(self):
        while self.merged < len(self.masks) - 1:
            self.merge()

    def run(self, compute, result):
        self.send_terms(compute, merge=True)
        self.merge_inner()
        self.merge(result)

    def finish(self):
        for mask in range(1, self.size):
            self.copy(mask, 1).wait_send()


def scatter_scratch(seq_size, rows, width):
    return [
        VMEM((seq_size // 2, 2, rows, width), bf16),
        VMEM((seq_size - 1, rows, width), bf16),
        DMA((seq_size,)),
        DMA((seq_size,)),
    ]


class LineGather:
    def __init__(self, size, own, out, send_sem, recv_sem, copy_sem):
        self.size, self.own, self.out = size, own, out
        self.send_sem, self.recv_sem, self.copy_sem = send_sem, recv_sem, copy_sem
        self.k = lax.axis_index("shard")

    def sent(self, way, step):
        block = self.k - step if way == 0 else self.k + step
        valid = (
            jnp.logical_and(self.k < self.size - 1, block >= 0)
            if way == 0
            else jnp.logical_and(self.k > 0, block <= self.size - 1)
        )
        safe = jnp.clip(block, 0, self.size - 1)
        target = jnp.clip(self.k + 1 if way == 0 else self.k - 1, 0, self.size - 1)
        return valid, pltpu.make_async_remote_copy(
            src_ref=self.own if step == 0 else self.out.at[safe],
            dst_ref=self.out.at[safe],
            send_sem=self.send_sem.at[way, step],
            recv_sem=self.recv_sem.at[way, step],
            device_id={"shard": target},
            device_id_type=MESH,
        )

    def received(self, way, step):
        block = self.k - 1 - step if way == 0 else self.k + 1 + step
        valid = block >= 0 if way == 0 else block <= self.size - 1
        safe = jnp.clip(block, 0, self.size - 1)
        return valid, pltpu.make_async_remote_copy(
            src_ref=self.own,
            dst_ref=self.out.at[safe],
            send_sem=self.send_sem.at[way, step],
            recv_sem=self.recv_sem.at[way, step],
            device_id={"shard": lax.rem(self.k + 1, self.size)},
            device_id_type=MESH,
        )

    def local(self):
        return pltpu.make_async_copy(self.own, self.out.at[self.k], self.copy_sem)

    def step(self, step):
        if step == 0:
            self.local().start()
        if step == self.size - 1:
            self.local().wait()
        for way in (0, 1):
            if step > 0:
                valid, copy = self.received(way, step - 1)

                @pl.when(valid)
                def _():
                    copy.wait_recv()

            if step < self.size - 1:
                valid, copy = self.sent(way, step)

                @pl.when(valid)
                def _():
                    copy.start()

    def finish(self):
        for step in range(self.size - 1):
            for way in (0, 1):
                valid, copy = self.sent(way, step)

                @pl.when(valid)
                def _():
                    copy.wait_send()


class ShardExchange:
    def __init__(self, size, source, out, send_sem, recv_sem, bounce=None, bounce_sem=None):
        self.size, self.source, self.out = size, source, out
        self.send_sem, self.recv_sem = send_sem, recv_sem
        self.bounce, self.bounce_sem = bounce, bounce_sem
        self.k = lax.axis_index("shard")

    def copy(self, step):
        target = lax.rem(self.k + step, self.size)
        return pltpu.make_async_remote_copy(
            src_ref=self.source(target),
            dst_ref=self.out.at[self.k],
            send_sem=self.send_sem.at[step],
            recv_sem=self.recv_sem.at[step],
            device_id={"shard": target},
            device_id_type=MESH,
        )

    def arrival(self, step):
        return pltpu.make_async_remote_copy(
            src_ref=self.out.at[self.k],
            dst_ref=self.out.at[lax.rem(self.k + self.size - step, self.size)],
            send_sem=self.send_sem.at[step],
            recv_sem=self.recv_sem.at[step],
            device_id={"shard": lax.rem(self.k + step, self.size)},
            device_id_type=MESH,
        )

    def local(self):
        source = self.source(self.k) if self.bounce is None else self.bounce
        return pltpu.make_async_copy(source, self.out.at[self.k], self.send_sem.at[0])

    def lift(self):
        return pltpu.make_async_copy(self.source(self.k), self.bounce, self.bounce_sem)

    def start_local(self):
        if self.bounce is None:
            self.local().start()
        else:
            self.lift().start()

    def settle(self):
        if self.bounce is not None:
            self.lift().wait()
            self.local().start()

    def inner(self, step):
        target = lax.rem(self.k + step, self.size)
        beside = jnp.abs(target - self.k) == 1
        return jnp.logical_and(beside, target // 2 != self.k // 2)

    def start_inner(self):
        for step in (1, self.size - 1):

            @pl.when(self.inner(step))
            def _():
                self.copy(step).start()

    def start_outer(self):
        self.start_local()
        for step in range(1, self.size):

            @pl.when(jnp.logical_not(self.inner(step)))
            def _():
                self.copy(step).start()

    def start(self):
        self.start_local()
        for step in range(1, self.size):
            self.copy(step).start()

    def wait_recv(self):
        self.local().wait()
        for step in range(1, self.size):
            self.arrival(step).wait_recv()

    def wait_send(self):
        for step in range(1, self.size):
            self.copy(step).wait_send()

    def wait(self):
        self.wait_recv()
        self.wait_send()


class PairReduce:
    def __init__(self, size, terms, first, middle_terms, second, sems):
        self.size, self.terms, self.first, self.second = size, terms, first, second
        self.middle_terms = middle_terms
        self.sems = sems
        self.k = lax.axis_index("shard")
        self.pairs = size // 2

    def swap(self, pair):
        target = 2 * pair + 1 - lax.rem(self.k, 2)
        return pltpu.make_async_remote_copy(
            src_ref=self.terms.at[target],
            dst_ref=self.first.at[pair],
            send_sem=self.sems.at[0, pair],
            recv_sem=self.sems.at[1, pair],
            device_id={"shard": jnp.bitwise_xor(self.k, 1)},
            device_id_type=MESH,
        )

    def cross(self, step):
        mine = self.k // 2
        pair = lax.rem(mine + step, self.pairs)
        target = 2 * pair + lax.rem(self.k, 2)
        return pair, target, pltpu.make_async_remote_copy(
            src_ref=self.middle_terms.at[step],
            dst_ref=self.second.at[step],
            send_sem=self.sems.at[2, step],
            recv_sem=self.sems.at[3, step],
            device_id={"shard": target},
            device_id_type=MESH,
        )

    def start(self):
        for pair in range(self.pairs):
            self.swap(pair).start()

    def middle(self):
        for pair in range(self.pairs):
            self.swap(pair).wait_recv()
        for step in range(1, self.pairs):
            pair, target, copy = self.cross(step)
            total = self.terms[target].astype(f32) + self.first[pair].astype(f32)
            self.middle_terms[step] = total.astype(bf16)
            copy.start()

    def total(self):
        for step in range(1, self.pairs):
            self.cross(step)[2].wait_recv()
        total = self.terms[self.k].astype(f32) + self.first[self.k // 2].astype(f32)
        for step in range(1, self.pairs):
            total = total + self.second[step].astype(f32)
        return total

    def finish(self):
        for pair in range(self.pairs):
            self.swap(pair).wait_send()
        for step in range(1, self.pairs):
            self.cross(step)[2].wait_send()


class PairSwap:
    def __init__(self, source, out, sems):
        mine = lax.axis_index("shard")
        self.copy = pltpu.make_async_remote_copy(
            src_ref=source,
            dst_ref=out,
            send_sem=sems.at[0],
            recv_sem=sems.at[1],
            device_id={"shard": jnp.bitwise_xor(mine, 1)},
            device_id_type=MESH,
        )


class Moves:
    def __init__(self, sems):
        self.sems, self.copies = sems, []

    def start(self, source, target):
        copy = pltpu.make_async_copy(source, target, self.sems.at[len(self.copies)])
        copy.start()
        self.copies.append(copy)
        return copy

    def wait(self, count=None):
        count = len(self.copies) if count is None else count
        for copy in [c for c in self.copies if c is not None][:count]:
            copy.wait()
        left = [i for i, c in enumerate(self.copies) if c is not None][:count]
        for i in left:
            self.copies[i] = None


def held(arrays):
    return [VMEM(a.shape, a.dtype) for a in arrays]


class Refs:
    def __init__(self, refs):
        self.refs = list(refs)

    def __call__(self, count):
        out, self.refs = self.refs[:count], self.refs[count:]
        return out


def inverse_rms(values):
    return lax.rsqrt(jnp.mean(values * values, axis=-1, keepdims=True) + epsilon)


def norm_back(values, inverse, gain, d_normed):
    scaled = d_normed * gain
    d_values = inverse * scaled - values * (inverse * inverse * inverse) * jnp.mean(
        scaled * values, axis=-1, keepdims=True
    )
    return d_values, jnp.sum(d_normed * values * inverse, axis=0, keepdims=True)


def head_lanes(head, shape):
    lane = lax.broadcasted_iota(jnp.int32, shape, 1)
    return lane < HD if head == 0 else lane >= HD


def turn(values, table, back):
    width = values.shape[1]
    cosine = jnp.concatenate([table[:, :HD]] * (width // HD), axis=1)
    sine = jnp.concatenate([table[:, HD:]] * (width // HD), axis=1)
    lane = lax.broadcasted_iota(jnp.int32, values.shape, 1)
    half = HD // 2
    partner = jnp.where(
        lane % HD < half,
        pltpu.roll(values, width - half, 1),
        pltpu.roll(values, half, 1),
    )
    if back:
        return values * cosine - partner * sine
    return values * cosine + partner * sine


def row_step(length, most):
    return most if length % most == 0 else length


def rows_at(index, step):
    return pl.ds(pl.multiple_of(index * step, step), step)


def weight_pieces(chunks):
    return [(c, kind) for c in range(chunks) for kind in ("gate", "up", "down")]


def piece_shape(kind, shards, part, block):
    return (shards, block, part) if kind == "down" else (shards, part, block)


def piece_source(kind, refs, chunk, block):
    ref = refs[kind]
    half = (ref.shape[0] if kind == "down" else ref.shape[1]) // 2

    def source(j):
        start = pl.multiple_of(lax.rem(j, 2) * half + chunk * block, block)
        if kind == "down":
            return ref.at[pl.ds(start, block), :]
        return ref.at[:, pl.ds(start, block)]

    return source


def split_masks(size):
    masks = chip_masks(size)[1:]
    return [m for m in masks if popcount(m) == 1], [m for m in masks if popcount(m) > 1]


def forward(x, gain_one, gain_two, table, cot, attn_weights, mlp_weights, pieces, block):
    seq_size, shard_size = lax.axis_size("seq"), lax.axis_size("shard")
    rows, width = x.shape
    part, cols = attn_weights[0].shape
    length = rows * seq_size
    big = row_step(length, 512)
    query = row_step(length, 256 if length <= 2048 else 128)
    pair = 2 * HD
    scale = 1.0 / math.sqrt(HD)

    def kernel(*refs):
        take = Refs(refs)
        x_ref, gain_one_ref, gain_two_ref, table_ref, cot_ref = take(5)
        own_weights = take(4)
        mlp_refs = dict(zip(("gate", "up", "down"), take(3)))
        normed_out, table_all, gains_all = take(3)
        weights_out = take(4)
        heads_out = take(4)
        lse_ref, hidden_ref = take(2)
        cot_all, cot_other, tok_all, tok_other = take(4)
        piece_refs = take(len(pieces))
        terms, arrived, ss, sr = take(4)
        normed_ref, normed_all = take(2)
        full_weights, heads_held = take(4), take(4)
        q_ref, k_ref, v_ref, o_ref = heads_held
        out_sems = take(1)[0]
        bounces, bounce_sems, gains_ref = take(len(pieces)), *take(2)
        ns, nr, ts, tr, cs, cr, ds, dr, ms, mr = take(10)
        gs, gr, line_s, line_r, line_c, piece_s, piece_r, local_sem, swap_sem = take(9)

        me, mine = lax.axis_index("seq"), lax.axis_index("shard")
        gains_ref[...] = jnp.zeros_like(gains_ref)
        gains_ref[0:1, :] = gain_one_ref[...].astype(f32).reshape(1, part)
        gains_ref[1:2, :] = gain_two_ref[...].astype(f32).reshape(1, part)
        entry_barrier(seq_neighbours(seq_size), shard_size)
        gain = ShardExchange(shard_size, lambda j: gains_ref, gains_all, gs, gr)
        gain.start()
        lines = [
            LineGather(shard_size, own, out, line_s.at[i], line_r.at[i], line_c.at[i])
            for i, (own, out) in enumerate(zip(own_weights, full_weights))
        ]
        wq_all, wk_all, wv_all, wo_all = full_weights
        exchanges = [
            ShardExchange(
                shard_size, piece_source(kind, mlp_refs, c, block), out, piece_s.at[i],
                piece_r.at[i], bounces[i], bounce_sems.at[i],
            )
            for i, ((c, kind), out) in enumerate(zip(pieces, piece_refs))
        ]
        mine_rows = rows_at(me, rows)
        own_cot = pltpu.make_async_copy(cot_ref, cot_all.at[mine_rows, :], local_sem.at[0])
        tables = SeqGather(seq_size, table_all, rows, ts, tr)
        normed = SeqGather(seq_size, normed_all, rows, ns, nr)
        cots = SeqGather(seq_size, cot_all, rows, cs, cr, own=cot_ref)
        cots_other = SeqGather(seq_size, cot_other, rows, ds, dr)
        swap_cot = PairSwap(cot_ref, cot_other.at[mine_rows, :], swap_sem.at[0]).copy
        for line in lines[:3]:
            line.step(0)
        swap_cot.start()
        own_cot.start()
        table_all[mine_rows, :] = table_ref[...]
        tables.start()
        gain.wait_recv()
        values = x_ref[...].astype(f32)
        scaled = values * inverse_rms(values)
        for z in range(shard_size):
            lanes = slice(z * part, (z + 1) * part)
            normed_all[mine_rows, lanes] = (scaled[:, lanes] * gains_all[z, 0:1, :]).astype(bf16)
        normed.start()
        tables.forwards()
        for line in lines[:3]:
            line.step(1)
        for exchange in exchanges:
            exchange.start_inner()
        near, far = split_masks(seq_size)
        for mask in near:
            normed.forward(mask)
        cots.start()
        for step in range(2, shard_size):
            for line in lines[:3]:
                line.step(step)
            if step == 2:
                lines[3].step(0)
                for mask in far:
                    normed.forward(mask)
                swap_cot.wait_recv()
                cots_other.start()
        tables.finish()
        normed.finish()
        outs = Moves(out_sems)
        outs.start(normed_all, normed_out)
        for held_weight, out in list(zip(full_weights, weights_out))[:3]:
            outs.start(held_weight, out)
        for mask in near:
            cots.forward(mask)
        lines[3].step(1)

        def start_pieces(point):
            if point == START:
                for exchange in exchanges[:AHEAD]:
                    exchange.start_outer()

        start_pieces(0)

        wq, wk, wv = (w.reshape(width, cols) for w in (wq_all, wk_all, wv_all))

        @pl.loop(0, length // big)
        def _(i):
            r = rows_at(i, big)
            tokens = normed_all[r, :]
            tab = table_all[r, :]
            q = turn(dot_nn(tokens, wq[...]), tab, False).astype(bf16)
            q_ref[r, :] = q * jnp.asarray(scale, bf16)
            k_ref[r, :] = turn(dot_nn(tokens, wk[...]), tab, False).astype(bf16)
            v_ref[r, :] = dot_nn(tokens, wv[...]).astype(bf16)

        for mask in far:
            cots.forward(mask)
        start_pieces(1)
        for step in range(2, shard_size - 1):
            lines[3].step(step)

        def attend(hp, lanes):
            for i in range(length // query):
                first, last = i * query, (i + 1) * query
                q2 = q_ref[first:last, lanes]
                out = None
                for head in (0, 1):
                    keep = head_lanes(head, q2.shape)
                    qm = jnp.where(keep, q2, jnp.zeros_like(q2))
                    s = dot_nt(qm, k_ref[:last, lanes])
                    r = lax.broadcasted_iota(jnp.int32, (query, query), 0)
                    c = lax.broadcasted_iota(jnp.int32, (query, query), 1)
                    tail = jnp.where(c <= r, s[:, first:], -1e30)
                    s = tail if i == 0 else jnp.concatenate([s[:, :first], tail], axis=1)
                    m = jnp.max(s, axis=1, keepdims=True)
                    p = jnp.exp(s - m)
                    total = jnp.sum(p, axis=1, keepdims=True)
                    low = (p * (1.0 / total)).astype(bf16)
                    o = dot_nn(low, v_ref[:last, lanes])
                    out = o if head == 0 else jnp.where(keep, o, out)
                    lse = jnp.transpose(jnp.broadcast_to(m + jnp.log(total), (query, 128)))
                    lse_ref[pl.ds(hp * 2 + head, 1), first:last] = lse[0:1, :]
                o_ref[first:last, lanes] = out.astype(bf16)

        if cols == 2 * pair:
            attend(0, slice(0, pair))
            for mask in near:
                cots_other.forward(mask)
            start_pieces(2)
            attend(1, slice(pair, cols))
        else:

            @pl.loop(0, cols // pair)
            def _(hp):
                attend(hp, rows_at(hp, pair))

            for mask in near:
                cots_other.forward(mask)
            start_pieces(2)
        for mask in far:
            cots_other.forward(mask)
        lines[3].step(shard_size - 1)
        start_pieces(3)
        outs.start(full_weights[3], weights_out[3])
        for held_heads, out in zip(heads_held, heads_out):
            outs.start(held_heads, out)
        scatter = SeqScatter(seq_size, terms, arrived, ss, sr)

        def compute(mask):
            tokens = o_ref[scatter.tokens(mask), :]
            for z in range(shard_size):
                scatter.put(mask, slice(z * part, (z + 1) * part), dot_nn(tokens, wo_all[z]))

        scatter.send_terms(compute, merge=True)
        for exchange in exchanges[:AHEAD]:
            exchange.settle()
        scatter.merge_inner()
        scatter.merge(hidden_ref)
        hidden = hidden_ref[...] + x_ref[...].astype(f32)
        hidden_ref[...] = hidden
        scaled = hidden * inverse_rms(hidden)
        for z in range(shard_size):
            lanes = slice(z * part, (z + 1) * part)
            normed_ref[:, lanes] = (scaled[:, lanes] * gains_all[z, 1:2, :]).astype(bf16)
        swap_tok = PairSwap(normed_ref, tok_other, swap_sem.at[1]).copy
        swap_tok.start()
        toks = SeqGather(seq_size, tok_all, rows, ms, mr, own=normed_ref)
        toks.start()
        own_tok = pltpu.make_async_copy(normed_ref, tok_all.at[mine_rows, :], local_sem.at[1])
        own_tok.start()
        for exchange in exchanges[AHEAD:]:
            exchange.start_outer()
        for mask in near:
            toks.forward(mask)
        for mask in far:
            toks.forward(mask)
        swap_cot.wait_send()
        gain.wait_send()
        scatter.finish()
        own_cot.wait()
        cots.finish()
        for line in lines:
            line.finish()
        swap_tok.wait()
        own_tok.wait()
        toks.finish()
        cots_other.finish()
        for exchange in exchanges[AHEAD:]:
            exchange.settle()
        for exchange in exchanges:
            exchange.wait()
        outs.wait()

    weight = array((shard_size, part, cols))
    out_weight = array((shard_size, cols, part))
    heads = array((length, cols))
    tokens = array((length, width))
    shapes = [piece_shape(kind, shard_size, part, block) for _, kind in pieces]
    count = len(pieces)
    outs = pl.pallas_call(
        kernel,
        name="forward_attention",
        out_shape=[
            tokens,
            array((length, table.shape[1]), f32),
            array((shard_size, 8, part), f32),
            weight,
            weight,
            weight,
            out_weight,
            heads,
            heads,
            heads,
            heads,
            array((max(8, cols // HD), length), f32),
            array((rows, width), f32),
            tokens,
            tokens,
            tokens,
            array((rows, width)),
        ]
        + [array(s) for s in shapes],
        in_specs=in_vmem(9) + in_any(3),
        out_specs=in_any(1) + in_vmem(2) + in_any(8) + in_vmem(2) + in_any(4 + count),
        scratch_shapes=scatter_scratch(seq_size, rows, width)
        + [VMEM((rows, width), bf16), VMEM((length, width), bf16)]
        + held([weight] * 3 + [out_weight] + [heads] * 4)
        + [DMA((9,))]
        + [VMEM(s[1:], bf16) for s in shapes]
        + [DMA((count,)), VMEM((8, part), f32)]
        + [DMA((seq_size,))] * 10
        + [DMA((shard_size,))] * 2
        + [DMA((4, 2, shard_size - 1))] * 2
        + [DMA((4,))]
        + [DMA((count, shard_size))] * 2
        + [DMA((2,)), DMA((2, 2))],
        compiler_params=kernel_params(1),
    )(x, gain_one, gain_two, table, cot, *attn_weights, *mlp_weights)
    return outs[:17], list(outs[17:])


def mlp(tok, tok_other, cot, cot_other, pieces_in, mlp_weights, late, chunks, block, sums):
    seq_size, shard_size = lax.axis_size("seq"), lax.axis_size("shard")
    length, width = tok.shape
    rows = tok_other.shape[0]
    part = width // shard_size
    big = row_step(length, 512)
    steps = length // big
    pieces = weight_pieces(chunks)
    early = pieces[: len(pieces_in)]

    def kernel(*refs):
        take = Refs(refs)
        tok_swap, tok_hbm = take(2)
        cots = take(2)
        early_refs = take(len(early))
        mlp_refs = dict(zip(("gate", "up", "down"), take(3)))
        acts_out = take(3)
        grads_out = take(len(pieces))
        late_refs = take(len(late))
        sum_refs = take(sums)
        tok2, cot_rows, cot_cols, xt = take(4)
        weights = take(len(pieces))
        act_ref, dg_ref, du_ref = take(3)
        grads = take(len(pieces))
        tok_ref, tok_sem, out_sems = take(3)
        bounces, bounce_sems = take(len(late)), take(1)[0]
        tok_copy = pltpu.make_async_copy(tok_hbm, tok_ref, tok_sem)
        tok_copy.start()
        outs = Moves(out_sems)
        ts, tr, late_s, late_r, sum_s, sum_r, row_sem, col_sem, load_sem = take(9)

        me, mine = lax.axis_index("seq"), lax.axis_index("shard")
        entry_barrier(seq_neighbours(seq_size), shard_size)
        late_moves = [
            ShardExchange(
                shard_size, piece_source(kind, mlp_refs, c, block), out, late_s.at[i], late_r.at[i],
                bounces[i], bounce_sems.at[i],
            )
            for i, ((c, kind), out) in enumerate(zip(late, late_refs))
        ]
        for move in late_moves:
            move.start()
        other = SeqGather(seq_size, tok2, rows, ts, tr, own=tok_swap)
        other.start()
        tok2[rows_at(me, rows), :] = tok_swap[...]
        everything = dict(zip(early, early_refs)) | dict(zip(late, late_refs))
        loads = [
            pltpu.make_async_copy(everything[p], w, load_sem.at[i])
            for i, (p, w) in enumerate(zip(pieces, weights))
        ]
        for load in loads[: len(early)]:
            load.start()
        held = dict(zip(pieces, weights))

        def row_copy(plane, i, slot):
            return pltpu.make_async_copy(
                cots[plane].at[rows_at(i, big), :], cot_rows.at[slot], row_sem.at[slot]
            )

        def stage(plane, these, base):
            token_ref = (tok_ref, tok2)[plane]

            @pl.loop(0, steps)
            def _(i):
                slot = lax.rem(i + base, 2)

                @pl.when(i + 1 < steps)
                def _():
                    row_copy(plane, i + 1, 1 - slot).start()

                tokens = token_ref[rows_at(i, big), :]
                row_copy(plane, i, slot).wait()
                r = pl.ds(pl.multiple_of(plane * length + i * big, big), big)
                for c in these:
                    gate_w, up_w = held[c, "gate"], held[c, "up"]
                    gate = dot_nn(tokens, gate_w.reshape(width, block)[...])
                    up = dot_nn(tokens, up_w.reshape(width, block)[...])
                    d_act = dot_nt(cot_rows[slot, :, :part], held[c, "down"][0])
                    for z in range(1, shard_size):
                        lanes = slice(z * part, (z + 1) * part)
                        d_act += dot_nt(cot_rows[slot, :, lanes], held[c, "down"][z])
                    sig = jax.nn.sigmoid(gate)
                    silu = gate * sig
                    act_ref[c, r, :] = (silu * up).astype(bf16)
                    slope = sig * (1.0 + gate * (1.0 - sig))
                    dg_ref[c, r, :] = (d_act * up * slope).astype(bf16)
                    du_ref[c, r, :] = (d_act * silu).astype(bf16)

        def col_copy(z, slot):
            lanes = slice(z * part, (z + 1) * part)
            return [
                pltpu.make_async_copy(
                    cots[plane].at[:, lanes],
                    cot_cols.at[slot, pl.ds(plane * length, length), :],
                    col_sem.at[slot, plane],
                )
                for plane in (0, 1)
            ]

        def grad(c):
            for source, where in ((act_ref, 2), (dg_ref, 0), (du_ref, 1)):
                xt[where] = jnp.transpose(source[c])
            for copy in col_copy(0, 0):
                copy.start()
            for z in range(shard_size):
                lanes = slice(z * part, (z + 1) * part)
                if z + 1 < shard_size:
                    for copy in col_copy(z + 1, (z + 1) % 2):
                        copy.start()
                for which in (0, 1):
                    total = dot_nn(xt[which, :, :length], tok_ref[:, lanes])
                    total += dot_nn(xt[which, :, length:], tok2[:, lanes])
                    grads[3 * c + which][z] = total.astype(bf16)
                for copy in col_copy(z, z % 2):
                    copy.wait()
                grads[3 * c + 2][z] = dot_nn(xt[2], cot_cols[z % 2]).astype(bf16)

        def put_acts(these):
            for c in these:
                for ref, out in zip((act_ref, dg_ref, du_ref), acts_out):
                    outs.start(ref.at[c], out.at[c])

        def put_grads(c):
            for i in range(max(sums, 3 * c), 3 * c + 3):
                outs.start(grads[i], grads_out[i])

        sum_moves = [
            ShardExchange(shard_size, lambda j, g=g: g.at[j], out, sum_s.at[i], sum_r.at[i])
            for i, (g, out) in enumerate(zip(grads, sum_refs))
        ]

        row_copy(0, 0, 0).start()
        first_chunks = [c for c in range(chunks) if all((c, k) in early for k in ("gate", "up", "down"))]
        later_chunks = [c for c in range(chunks) if c not in first_chunks]
        for load in loads[: len(early)]:
            load.wait()
        tok_copy.wait()
        for move in late_moves:
            move.settle()
        stage(0, first_chunks, 0)
        row_copy(1, 0, 0).start()
        other.forwards()
        other.finish()
        stage(1, first_chunks, 0)
        put_acts(first_chunks)
        for c in first_chunks:
            grad(c)
            put_grads(c)
            for move in sum_moves[3 * c : 3 * c + 3]:
                move.start()
        if later_chunks:
            row_copy(0, 0, 0).start()
            for move in late_moves:
                move.wait_recv()
            for load in loads[len(early) :]:
                load.start()
            for load in loads[len(early) :]:
                load.wait()
            stage(0, later_chunks, 0)
            row_copy(1, 0, 0).start()
            stage(1, later_chunks, 0)
            put_acts(later_chunks)
            for c in later_chunks:
                grad(c)
                put_grads(c)
                for move in sum_moves[3 * c : 3 * c + 3]:
                    move.start()
        for move in late_moves:
            move.wait_send()
        for move in sum_moves:
            move.wait()
        outs.wait()

    piece = array((shard_size, block, part))
    act = array((chunks, 2 * length, block))
    late_shapes = [piece_shape(kind, shard_size, part, block) for _, kind in late]
    all_shapes = [piece_shape(kind, shard_size, part, block) for _, kind in pieces]
    outs = pl.pallas_call(
        kernel,
        name="mlp",
        out_shape=[act] * 3
        + [piece] * len(pieces)
        + [array(s) for s in late_shapes]
        + [piece] * sums,
        in_specs=in_vmem(1) + in_any(3 + len(early) + 3),
        out_specs=in_any(3 + len(pieces) + len(late) + sums),
        scratch_shapes=[
            VMEM((length, width), bf16),
            VMEM((2, big, width), bf16),
            VMEM((2, 2 * length, part), bf16),
            VMEM((3, block, 2 * length), bf16),
        ]
        + [VMEM(s, bf16) for s in all_shapes]
        + held([act] * 3 + [piece] * len(pieces))
        + [VMEM((length, width), bf16), DMA, DMA((3 * chunks + len(pieces),))]
        + [VMEM(s[1:], bf16) for s in late_shapes]
        + [DMA((max(1, len(late)),))]
        + [DMA((seq_size,))] * 2
        + [DMA((max(1, len(late)), shard_size))] * 2
        + [DMA((max(1, sums), shard_size))] * 2
        + [DMA((2,)), DMA((2, 2)), DMA((len(pieces),))],
        compiler_params=kernel_params(2),
    )(tok_other, tok, cot, cot_other, *pieces_in, *mlp_weights)
    outs = list(outs)
    first = 3 + len(pieces)
    second = first + len(late)
    return outs[:3], outs[3:first], outs[first:second], outs[second:]


def mlp_back(d_gate, d_up, gate, up, hidden, cot, gains_all, grads):
    seq_size, shard_size = lax.axis_size("seq"), lax.axis_size("shard")
    rows, width = hidden.shape
    chunks = len(gate)
    length = rows * seq_size
    part = width // shard_size
    count = len(grads)
    shared = length > 2048

    def kernel(*refs):
        take = Refs(refs)
        sources = take(2 + 2 * chunks)
        hidden_ref, cot_ref, gains_ref = take(3)
        grad_refs = take(count)
        d_hidden_ref, d_gain_ref, d_attn_all = take(3)
        sum_refs = take(count)
        terms = take(1 if shared else 2)
        arrived = take(2)
        scatter_sems = [take(2), take(2)]
        other_ref, swap_ref, d_attn_ref = take(3)
        ns, nr, swap_sem, own_sem, sum_s, sum_r = take(6)
        loaded, load_sems = take(2 + 2 * chunks), take(1)[0]
        bounces, bounce_sems = take(count), take(1)[0]
        dg_ref, du_ref = loaded[:2]
        gate_refs, up_refs = loaded[2 : 2 + chunks], loaded[2 + chunks :]
        loads = Moves(load_sems)
        for source, target in zip(sources, loaded):
            loads.start(source, target)

        me = lax.axis_index("seq")
        entry_barrier(seq_neighbours(seq_size), shard_size)
        moves = [
            ShardExchange(
                shard_size, lambda j, g=g: g.at[j], out, sum_s.at[i], sum_r.at[i], bounces[i],
                bounce_sems.at[i],
            )
            for i, (g, out) in enumerate(zip(grad_refs, sum_refs))
        ]
        for move in moves[:BEFORE]:
            move.start_outer()
        swap = PairSwap(other_ref, swap_ref, swap_sem).copy
        loads.wait()
        scatters = [
            SeqScatter(seq_size, terms[0 if shared else i], arrived[i], *scatter_sems[i])
            for i in range(2)
        ]

        def term(plane):
            scatter = scatters[plane]

            def compute(mask):
                tokens = scatter.tokens(mask, plane * length)
                for z in range(shard_size):
                    total = None
                    for c in range(chunks):
                        both = dot_nt(dg_ref[c, tokens, :], gate_refs[c][z])
                        both += dot_nt(du_ref[c, tokens, :], up_refs[c][z])
                        total = both if total is None else total + both
                    scatter.put(mask, slice(z * part, (z + 1) * part), total)

            return compute

        here, there = scatters
        there.send_terms(term(1), merge=True)
        if shared:
            there.merge_inner()
            there.merge(other_ref)
            swap.start()
            there.finish()
            here.send_terms(term(0), merge=True)
        else:
            here.send_terms(term(0))
            there.merge_inner()
            here.merge_leaves()
            there.merge(other_ref)
            swap.start()
        for move in moves:
            move.start_inner()
        for move in moves[BEFORE:]:
            move.start_outer()
        here.merge_inner()
        here.merge(d_hidden_ref)
        swap.wait()
        d_normed = d_hidden_ref[...] + swap_ref[...].astype(f32)
        values = hidden_ref[...]
        gain = jnp.concatenate([gains_ref[z, 1:2, :] for z in range(shard_size)], axis=1)
        d_values, d_gain = norm_back(values, inverse_rms(values), gain, d_normed)
        d_hidden = cot_ref[...].astype(f32) + d_values
        d_attn_ref[...] = d_hidden.astype(bf16)
        gather = SeqGather(seq_size, d_attn_all, rows, ns, nr, own=d_attn_ref)
        gather.start()
        for move in moves:
            move.settle()
        own = pltpu.make_async_copy(d_attn_ref, d_attn_all.at[rows_at(me, rows), :], own_sem)
        own.start()
        d_hidden_ref[...] = d_hidden
        d_gain_ref[...] = d_gain
        gather.forwards()
        own.wait()
        gather.finish()
        for scatter in scatters[: 1 if shared else 2]:
            scatter.finish()
        for move in moves:
            move.wait()

    scatter = scatter_scratch(seq_size, rows, width)
    inputs = [d_gate, d_up, *gate, *up]
    outs = pl.pallas_call(
        kernel,
        name="mlp_back",
        out_shape=[
            array((rows, width), f32),
            array((1, width), f32),
            array((length, width)),
        ]
        + [array(g.shape) for g in grads],
        in_specs=in_any(2 + 2 * chunks) + in_vmem(3) + in_any(count),
        out_specs=in_vmem(2) + in_any(1 + count),
        scratch_shapes=scatter[:1] * (1 if shared else 2)
        + scatter[1:2] * 2
        + [DMA((seq_size,))] * 4
        + [VMEM((rows, width), bf16)] * 3
        + [DMA((seq_size,))] * 2
        + [DMA((2,)), DMA]
        + [DMA((max(1, count), shard_size))] * 2
        + held(inputs)
        + [DMA((len(inputs),))]
        + [VMEM(g.shape[1:], bf16) for g in grads]
        + [DMA((max(1, count),))],
        compiler_params=kernel_params(3),
    )(*inputs, hidden, cot, gains_all, *grads)
    return outs[:3], list(outs[3:])


class OutputSum:
    def __init__(self, scatter, act, down_refs, base=0):
        self.scatter, self.act, self.down_refs, self.base = scatter, act, down_refs, base

    def compute(self, mask):
        tokens = self.scatter.tokens(mask, self.base)
        shards, _, part = self.down_refs[0].shape
        for z in range(shards):
            total = None
            for c, down in enumerate(self.down_refs):
                one = dot_nn(self.act[c, tokens, :], down[z])
                total = one if total is None else total + one
            self.scatter.put(mask, slice(z * part, (z + 1) * part), total)


def attend_back(d_attn, wo, mixed, q, k, v, lse, table, normed, grads, activ, down):
    seq_size, shard_size = lax.axis_size("seq"), lax.axis_size("shard")
    length, width = d_attn.shape
    rows = length // seq_size
    cols = q.shape[1]
    part = wo.shape[2]
    big = row_step(length, 512)
    block = row_step(length, 256)
    scale = 1.0 / math.sqrt(HD)
    pair = 2 * HD
    count = len(grads)
    chunks = len(down)

    def kernel(*refs):
        take = Refs(refs)
        sources = take(9 + chunks)
        grad_refs = take(count)
        act_all = take(1)[0] if chunks else None
        dq_ref, dk_ref, dv_ref, gq_ref, gk_ref, gv_ref = take(6)
        if chunks:
            swap_ref = take(1)[0]
        sum_refs = take(count + 1)
        do_ref, kt_ref, dk_acc, dv_acc, xt_ref, go_ref, sum_s, sum_r = take(8)
        loaded, load_sems = take(9 + chunks), take(1)[0]
        bounces, bounce_sems = take(count), take(1)[0]
        da_ref, wo_ref, mixed_ref, q_ref, k_ref, v_ref, lse_ref, t_ref, n_ref = loaded[:9]
        down_refs = loaded[9:]
        loads = Moves(load_sems)
        first = list(range(9, 9 + chunks)) + [0, 2]
        for i in first + [1, 3, 4, 5, 6, 7, 8]:
            loads.start(sources[i], loaded[i])

        if chunks:
            terms, arrived, ss, sr, act_ref, other_ref, act_sem, swap_sem = take(8)
            act_copy = pltpu.make_async_copy(
                act_all.at[:, pl.ds(length, length), :], act_ref, act_sem
            )
            act_copy.start()
        entry_barrier(seq_neighbours(seq_size) if chunks else [], shard_size)
        moves = [
            ShardExchange(
                shard_size, lambda j, g=g: g.at[j], out, sum_s.at[i], sum_r.at[i], bounce,
                bounce_sems.at[i],
            )
            for i, (g, out, bounce) in enumerate(
                zip(grad_refs + [go_ref], sum_refs, bounces + [None])
            )
        ]
        for move in moves[:-1]:
            move.start_outer()
        if chunks:
            swap = PairSwap(other_ref, swap_ref, swap_sem).copy
            act_copy.wait()
            loads.wait(chunks)
            out_sum = OutputSum(SeqScatter(seq_size, terms, arrived, ss, sr), act_ref, down_refs)
            out_sum.scatter.send_terms(out_sum.compute, merge=True)

        loads.wait(2)
        xt_ref[...] = jnp.transpose(mixed_ref[...])
        for z in range(shard_size):
            go_ref[z] = dot_nn(xt_ref[...], da_ref[:, z * part : (z + 1) * part]).astype(bf16)
        moves[-1].start_outer()
        loads.wait(6)

        @pl.loop(0, length // big)
        def _(i):
            r = rows_at(i, big)
            total = dot_nt(da_ref[r, :part], wo_ref[0])
            for z in range(1, shard_size):
                total += dot_nt(da_ref[r, z * part : (z + 1) * part], wo_ref[z])
            do_ref[r, :] = total.astype(bf16)

        kt_ref[...] = jnp.transpose(k_ref[...])
        for move in moves:
            move.settle()
        if chunks:
            out_sum.scatter.merge_inner()

        def heads(hp, lanes):
            dk_acc[...] = jnp.zeros_like(dk_acc)
            dv_acc[...] = jnp.zeros_like(dv_acc)
            for i in range(length // block):
                first, last = i * block, (i + 1) * block
                q2 = q_ref[first:last, lanes]
                do2 = do_ref[first:last, lanes]
                keys = k_ref[:last, lanes]
                values = v_ref[:last, lanes]
                dqt, dk_add, dv_add = None, None, None
                for head in (0, 1):
                    keep = head_lanes(head, q2.shape)
                    qm = jnp.where(keep, q2, jnp.zeros_like(q2))
                    dom = jnp.where(keep, do2, jnp.zeros_like(do2))
                    st = dot_nt(keys, qm)
                    row = lse_ref[pl.ds(hp * 2 + head, 1), first:last]
                    p = jnp.exp(st - row)
                    r = lax.broadcasted_iota(jnp.int32, (block, block), 0)
                    c = lax.broadcasted_iota(jnp.int32, (block, block), 1)
                    tail = jnp.where(r <= c, p[first:], 0.0)
                    p = tail if i == 0 else jnp.concatenate([p[:first], tail], axis=0)
                    dp = dot_nt(values, dom)
                    inner = jnp.sum(dp * p, axis=0, keepdims=True)
                    ds = (p * (dp - inner)).astype(bf16)
                    dv_one = dot_nn(p.astype(bf16), dom)
                    dk_one = dot_nn(ds, qm)
                    dv_add = dv_one if head == 0 else dv_add + dv_one
                    dk_add = dk_one if head == 0 else dk_add + dk_one
                    dqt_one = dot_nn(kt_ref[lanes, :last], ds)
                    if head == 0:
                        dqt = dqt_one
                    else:
                        sub = lax.broadcasted_iota(jnp.int32, dqt.shape, 0)
                        dqt = jnp.where(sub < HD, dqt, dqt_one)
                dk_acc[:last, :] += dk_add
                dv_acc[:last, :] += dv_add
                dq = (jnp.transpose(dqt) * scale).astype(bf16).astype(f32)
                dq_ref[first:last, lanes] = turn(dq, t_ref[first:last, :], True).astype(bf16)
            dv_ref[:, lanes] = dv_acc[...].astype(bf16)

            @pl.loop(0, length // big)
            def _(i):
                r = rows_at(i, big)
                dk = dk_acc[r, :].astype(bf16).astype(f32)
                dk_ref[r, lanes] = turn(dk, t_ref[r, :], True).astype(bf16)

        if chunks:
            for hp in range(cols // pair):
                heads(hp, slice(hp * pair, (hp + 1) * pair))
                if hp == 0:
                    out_sum.scatter.merge(other_ref)
                    swap.start()
                    for move in moves:
                        move.start_inner()
        else:
            for move in moves:
                move.start_inner()

            @pl.loop(0, cols // pair)
            def _(hp):
                heads(hp, rows_at(hp, pair))

        loads.wait()
        for source, out in ((dq_ref, gq_ref), (dk_ref, gk_ref), (dv_ref, gv_ref)):
            xt_ref[...] = jnp.transpose(source[...])
            for z in range(shard_size):
                out[z] = dot_nn(xt_ref[...], n_ref[:, z * part : (z + 1) * part]).astype(bf16)
        if chunks:
            swap.wait()
            out_sum.scatter.finish()
        for move in moves:
            move.wait()

    grad = array((shard_size, cols, part))
    scratch = [
        VMEM((length, cols), bf16),
        VMEM((cols, length), bf16),
        VMEM((length, pair), f32),
        VMEM((length, pair), f32),
        VMEM((cols, length), bf16),
        VMEM((shard_size, cols, part), bf16),
    ] + [DMA((count + 1, shard_size))] * 2
    inputs = [d_attn, wo, mixed, q, k, v, lse, table, normed, *down]
    scratch += held(inputs) + [DMA((len(inputs),))]
    scratch += [VMEM(g.shape[1:], bf16) for g in grads] + [DMA((count + 1,))]
    if chunks:
        scratch += scatter_scratch(seq_size, rows, width)
        scratch += [VMEM((chunks, length, activ.shape[2]), bf16), VMEM((rows, width), bf16)]
        scratch += [DMA, DMA((2,))]
    outs = pl.pallas_call(
        kernel,
        name="attend_back",
        out_shape=[array((length, cols))] * 3
        + [grad] * 3
        + [array((rows, width))] * (1 if chunks else 0)
        + [array(g.shape) for g in grads]
        + [grad],
        in_specs=in_any(9 + chunks + count + (1 if chunks else 0)),
        out_specs=in_vmem(7 if chunks else 6) + in_any(count + 1),
        scratch_shapes=scratch,
        compiler_params=kernel_params(4),
    )(*inputs, *grads, *([activ] if chunks else []))
    outs = list(outs)
    other = outs.pop(6) if chunks else None
    return outs[:3], outs[3:6], other, outs[6:]


def output_parts(activ, down, hidden):
    seq_size, shard_size = lax.axis_size("seq"), lax.axis_size("shard")
    rows, width = hidden.shape
    length = rows * seq_size
    chunks = len(down)

    def kernel(*refs):
        take = Refs(refs)
        act_ref, hidden_ref = take(2)
        down_refs = take(chunks)
        out_ref, terms, first, second = take(4)
        sems = [take(2), take(2)]
        total_ref, other_ref, swap_ref, swap_sem = take(4)
        entry_barrier(seq_neighbours(seq_size), shard_size)
        there, here = (
            OutputSum(SeqScatter(seq_size, terms, arrived, *sem), act_ref, down_refs, base)
            for arrived, sem, base in ((first, sems[0], length), (second, sems[1], 0))
        )
        there.scatter.run(there.compute, other_ref)
        swap = PairSwap(other_ref, swap_ref, swap_sem).copy
        swap.start()
        there.scatter.finish()
        here.scatter.run(here.compute, total_ref)
        swap.wait()
        out_ref[...] = (total_ref[...] + swap_ref[...].astype(f32) + hidden_ref[...]).astype(bf16)
        here.scatter.finish()

    scatter = scatter_scratch(seq_size, rows, width)
    return pl.pallas_call(
        kernel,
        name="output_parts",
        out_shape=array((rows, width)),
        in_specs=in_vmem(2 + chunks),
        out_specs=in_vmem(1)[0],
        scratch_shapes=scatter[:2]
        + scatter[1:2]
        + [DMA((seq_size,))] * 4
        + [VMEM((rows, width), f32), VMEM((rows, width), bf16), VMEM((rows, width), bf16)]
        + [DMA((2,))],
        compiler_params=kernel_params(6),
    )(activ, hidden, *down)


def finish(
    d_qkv, attn_weights, g_qkv, x, d_hidden, gains_all, d_gain_two, sums, g_output, block,
    output_of,
):
    seq_size, shard_size = lax.axis_size("seq"), lax.axis_size("shard")
    rows, width = x.shape
    part = width // shard_size
    cols = d_qkv[0].shape[1]
    length = rows * seq_size
    pieces = len(sums)
    half = pieces // 3 * block
    activ, down, hidden, other = output_of or (None, [], None, None)
    chunks = len(down)
    pairs = shard_size // 2

    def kernel(*refs):
        take = Refs(refs)
        x_ref, d_hidden_ref, gains_ref, gain2_ref = take(4)
        sources = take(9 + chunks)
        hidden_ref, other_ref = take(2) if chunks else (None, None)
        act_all = take(1)[0] if chunks else None
        sum_refs, go_ref = take(pieces), take(1)[0]
        d_inputs_ref, gain_ref = take(2)
        qkv_refs = take(3)
        output_ref = take(1)[0] if chunks else None
        wo_ref, wg_ref, wu_ref, wd_ref = take(4)
        total_ref, gain_mine, gain_shards, gain_line, gain_seq = take(5)
        gs, gr, hs, hr = take(4)
        in_terms, in_arrived, in_s, in_r = take(4)
        firsts, middles, seconds, reduce_sems = take(4)
        received, wide, tall, load_sem, store_sem = take(5)
        loaded, in_sems = take(9 + chunks), take(1)[0]
        d_refs, w_refs, g_refs = loaded[:3], loaded[3:6], loaded[6:9]
        down_refs = loaded[9:]
        ins = Moves(in_sems)
        for i in [6, 7, 8, 0, 1, 2, 3, 4, 5] + list(range(9, 9 + chunks)):
            ins.start(sources[i], loaded[i])
        if chunks:
            out_terms, out_arrived, out_s, out_r, act_ref, act_sem, out_total = take(7)
            act_copy = pltpu.make_async_copy(act_all.at[:, pl.ds(0, length), :], act_ref, act_sem)
            act_copy.start()

        me = lax.axis_index("seq")
        entry_barrier(range(1, seq_size), shard_size)
        reduces = [
            PairReduce(
                shard_size, g_refs[i], firsts.at[i], middles.at[i], seconds.at[i], reduce_sems.at[i]
            )
            for i in range(3)
        ]
        ins.wait(3)
        for reduce in reduces:
            reduce.start()
        ins.wait(6)
        in_sum = SeqScatter(seq_size, in_terms, in_arrived, in_s, in_r)

        def inputs_term(mask):
            tokens = in_sum.tokens(mask)
            for z in range(shard_size):
                total = None
                for d_ref, w_ref in zip(d_refs, w_refs):
                    term = dot_nt(d_ref[tokens, :], w_ref[z])
                    total = term if total is None else total + term
                in_sum.put(mask, slice(z * part, (z + 1) * part), total)

        in_sum.send_terms(inputs_term, merge=True)
        if chunks:
            act_copy.wait()
            ins.wait()
            out_sum = OutputSum(
                SeqScatter(seq_size, out_terms, out_arrived, out_s, out_r), act_ref, down_refs
            )
            out_sum.scatter.send_terms(out_sum.compute)

        loads = [
            pltpu.make_async_copy(source, received.at[i % 2], load_sem.at[i % 2])
            for i, source in enumerate(sum_refs)
        ]
        stores = []

        def store(staging, target, value):
            turn_of = sum(1 for s in stores if s[0] is staging)
            slot = turn_of % 2
            sem = store_sem.at[0 if staging is wide else 1, slot]
            if turn_of >= 2:
                [s for s in stores if s[0] is staging][-2][1].wait()
            staging[slot] = value.astype(bf16)
            copy = pltpu.make_async_copy(staging.at[slot], target, sem)
            copy.start()
            stores.append((staging, copy))

        def collect(i):
            if i + 1 < pieces:
                loads[i + 1].start()
            loads[i].wait()
            for parity in (0, 1):
                total = received[i % 2, parity].astype(f32)
                for p in range(1, pairs):
                    total = total + received[i % 2, 2 * p + parity].astype(f32)
                start = parity * half + i // 3 * block
                if i % 3 == 2:
                    store(wide, wd_ref.at[start : start + block, :], total)
                else:
                    target = (wg_ref, wu_ref)[i % 3]
                    store(tall, target.at[:, start : start + block], jnp.transpose(total))

        loads[0].start()
        third = (pieces + 2) // 3
        in_sum.merge_inner()
        reduces[0].middle()
        if chunks:
            out_sum.scatter.merge_leaves()
        for i in range(third):
            collect(i)
        reduces[1].middle()
        in_sum.merge(total_ref)
        values = x_ref[...].astype(f32)
        gain = jnp.concatenate([gains_ref[z, 0:1, :] for z in range(shard_size)], axis=1)
        d_values, d_gain = norm_back(values, inverse_rms(values), gain, total_ref[...])
        d_inputs_ref[...] = (d_hidden_ref[...] + d_values).astype(bf16)
        for z in range(shard_size):
            lanes = slice(z * part, (z + 1) * part)
            gain_mine[z, 0:1, :] = d_gain[:, lanes]
            gain_mine[z, 1:2, :] = gain2_ref[0:1, lanes]
            gain_mine[z, 2:, :] = jnp.zeros((6, part), f32)
        line = ShardExchange(shard_size, lambda j: gain_mine.at[j], gain_shards, gs, gr)
        line.start()
        for i in range(third, 2 * third):
            collect(i)
        reduces[2].middle()
        if chunks:
            out_sum.scatter.merge_inner()
        line.wait()
        gain_line[...] = sum(gain_shards[z] for z in range(shard_size))

        def to_seq(step):
            return pltpu.make_async_remote_copy(
                src_ref=gain_line,
                dst_ref=gain_seq.at[step],
                send_sem=hs.at[step],
                recv_sem=hr.at[step],
                device_id={"seq": jnp.bitwise_xor(me, step)},
                device_id_type=MESH,
            )

        for step in range(1, seq_size):
            to_seq(step).start()
        for i in range(2 * third, pieces):
            collect(i)
        wo_ref[...] = sum(go_ref[z].astype(f32) for z in range(shard_size)).astype(bf16)
        if chunks:
            out_sum.scatter.merge(out_total)
            output_ref[...] = (
                out_total[...] + other_ref[...].astype(f32) + hidden_ref[...]
            ).astype(bf16)
        for reduce, out in zip(reduces, qkv_refs):
            out[...] = jnp.transpose(reduce.total()).astype(bf16)
        for step in range(1, seq_size):
            to_seq(step).wait()
        gain_ref[...] = gain_line[...] + sum(gain_seq[step] for step in range(1, seq_size))
        for staging in (wide, tall):
            for _, copy in [s for s in stores if s[0] is staging][-2:]:
                copy.wait()
        for reduce in reduces:
            reduce.finish()
        in_sum.finish()
        if chunks:
            out_sum.scatter.finish()

    scratch = [
        VMEM((rows, width), f32),
        VMEM((shard_size, 8, part), f32),
        VMEM((shard_size, 8, part), f32),
        VMEM((8, part), f32),
        VMEM((seq_size, 8, part), f32),
    ]
    scratch += [DMA((shard_size,))] * 2 + [DMA((seq_size,))] * 2
    scratch += scatter_scratch(seq_size, rows, width)
    scratch += [VMEM((3, pairs, cols, part), bf16)] * 3 + [DMA((3, 4, pairs))]
    scratch += [
        VMEM((2, shard_size, block, part), bf16),
        VMEM((2, block, part), bf16),
        VMEM((2, part, block), bf16),
        DMA((2,)),
        DMA((2, 2)),
    ]
    inputs = [*d_qkv, *attn_weights, *g_qkv, *down]
    scratch += held(inputs) + [DMA((len(inputs),))]
    if chunks:
        scratch += scatter_scratch(seq_size, rows, width)
        scratch += [VMEM((chunks, length, block), bf16), DMA, VMEM((rows, width), f32)]
    extra = 1 if chunks else 0
    units = 2 * half
    outs = pl.pallas_call(
        kernel,
        name="finish",
        out_shape=[array((rows, width)), array((8, part), f32)]
        + [array((part, cols))] * 3
        + [array((rows, width))] * extra
        + [array((cols, part))]
        + [array((part, units))] * 2
        + [array((units, part))],
        in_specs=in_vmem(4)
        + in_any(9 + chunks)
        + in_vmem(2 * extra)
        + in_any(extra + pieces)
        + in_vmem(1),
        out_specs=in_vmem(6 + extra) + in_any(3),
        scratch_shapes=scratch,
        compiler_params=kernel_params(5),
    )(
        x, d_hidden, gains_all, d_gain_two, *inputs,
        *([hidden, other, activ] if chunks else []), *sums, g_output,
    )
    outs = list(outs)
    output = outs.pop(5) if chunks else None
    return outs, output


def widen(rows, grads, gains):
    part = gains.shape[1]

    def kernel(*refs):
        take = Refs(refs)
        grad_refs, row_refs, gain_ref = take(len(grads)), take(len(rows)), take(1)[0]
        row_outs, grad_outs, gain_outs = take(len(rows)), take(len(grads)), take(2)
        low, high, load_sems, store_sems = take(len(grads)), take(len(grads)), *take(2)
        loads, stores = Moves(load_sems), Moves(store_sems)
        for source, target in zip(grad_refs, low):
            loads.start(source, target)
        for source, target in zip(row_refs, row_outs):
            target[...] = source[...]
        for i, out in enumerate(gain_outs):
            out[...] = gain_ref[i : i + 1, :]
        for a, b, out in zip(low, high, grad_outs):
            loads.wait(1)
            b[...] = a[...].astype(f32)
            stores.start(b, out)
        stores.wait()

    wide = [array(g.shape, f32) for g in grads]
    return pl.pallas_call(
        kernel,
        name="widen",
        out_shape=[array(r.shape) for r in rows] + wide + [array((1, part), f32)] * 2,
        in_specs=in_any(len(grads)) + in_vmem(len(rows) + 1),
        out_specs=in_vmem(len(rows)) + in_any(len(grads)) + in_vmem(2),
        scratch_shapes=held(grads) + held(wide) + [DMA((len(grads),)), DMA((len(grads),))],
        compiler_params=kernel_params(),
    )(*grads, *rows, gains)


def rotation_table(position_ids):
    half = HD // 2
    freqs = theta_base ** (-(jnp.arange(half, dtype=f32) * 2.0) / HD)
    angles = position_ids.astype(f32)[:, None] * freqs[None, :]
    cosine, sine = jnp.cos(angles), jnp.sin(angles)
    return jnp.concatenate([cosine, cosine, -sine, sine], axis=1)


EARLY = 4
AHEAD = 4
BEFORE = 2
SUMS = (1, 4)
START = 2


def body(
    inputs,
    positions,
    attn_gain,
    w_query,
    w_key,
    w_value,
    w_output,
    mlp_gain,
    w_gate,
    w_up,
    w_down,
    cotangent,
):
    shard_size = lax.axis_size("shard")
    x, cot = inputs[0], cotangent[0]
    table = rotation_table(positions[0])
    half = w_gate.shape[1] // 2
    block = row_step(half, 256)
    chunks = half // block
    pieces = weight_pieces(chunks)
    early, late = pieces[:EARLY], pieces[EARLY:]
    mlp_weights = (w_gate, w_up, w_down)
    held, early_weights = forward(
        x, attn_gain, mlp_gain, table, cot, (w_query, w_key, w_value, w_output), mlp_weights, early, block
    )
    normed, tables, gains_all, wq, wk, wv, wo, q, k, v, mixed, lse, hidden = held[:13]
    cot_all, cot_other, tok, tok_other = held[13:]
    acts, grads, late_weights, sums = mlp(
        tok, tok_other, cot_all, cot_other, early_weights, mlp_weights, late, chunks, block,
        min(SUMS[0], len(pieces)),
    )
    activ, d_gate, d_up = acts
    weights = dict(zip(pieces, early_weights + late_weights))

    def kind(name):
        return [weights[c, name] for c in range(chunks)]

    done = len(sums)
    more = min(SUMS[1], len(pieces) - done)
    (d_hidden, d_gain_two, d_attn), moved = mlp_back(
        d_gate, d_up, kind("gate"), kind("up"), hidden, cot, gains_all, grads[done : done + more]
    )
    sums += moved
    done += more
    down = kind("down")
    together = tok.shape[0] <= 2048
    d_qkv, g_qkv, other, moved = attend_back(
        d_attn, wo, mixed, q, k, v, lse, tables, normed, grads[done:], activ,
        down if together else [],
    )
    sums += moved[:-1]
    results, output = finish(
        d_qkv, (wq, wk, wv), g_qkv, x, d_hidden, gains_all, d_gain_two, sums, moved[-1], block,
        (activ, down, hidden, other) if together else None,
    )
    if not together:
        output = output_parts(activ, down, hidden)
    d_inputs, gain_sums, *grads = results
    output, d_inputs, *grads, gain_one, gain_two = widen([output, d_inputs], grads, gain_sums)
    return (
        output[None],
        d_inputs[None],
        gain_one.reshape(-1),
        *grads[:4],
        gain_two.reshape(-1),
        *grads[4:],
    )


def solution(mesh):
    in_specs = (
        P("shard", "seq", None),
        P("shard", "seq"),
        P("shard"),
        P("shard", "seq"),
        P("shard", "seq"),
        P("shard", "seq"),
        P("seq", "shard"),
        P("shard"),
        P("shard", "seq"),
        P("shard", "seq"),
        P("seq", "shard"),
        P("shard", "seq", None),
    )
    out_specs = (
        P("shard", "seq", None),
        P("shard", "seq", None),
        P("shard"),
        P("shard", "seq"),
        P("shard", "seq"),
        P("shard", "seq"),
        P("seq", "shard"),
        P("shard"),
        P("shard", "seq"),
        P("shard", "seq"),
        P("seq", "shard"),
    )
    return jax.shard_map(body, mesh=mesh, in_specs=in_specs, out_specs=out_specs, check_vma=False)
```
